256 devices in a mesh: gx: 16 (over z, x_lo), gy: 16 (over x_hi, y, core).
Axes of the slice: x: 4 (x_hi: 2, x_lo: 2; x = x_hi * 2 + x_lo), y: 4, z: 8, core: 2. Of those that a mesh axis runs over, the one named last changes fastest.
Arguments:
- populations: float32 [27, 8, 128, 4096], P(None, None, 'gx', 'gy'), may hold values from 0 to 1, as said below
- bottom_in: float32 [9, 128, 4096], P(None, 'gx', 'gy'), may hold values from 0.01 to 0.06
- top_in: float32 [9, 128, 4096], P(None, 'gx', 'gy'), may hold values from 0.01 to 0.06
- turbine_mask: int32 [8, 128, 4096], P(None, 'gx', 'gy'), may hold values from 0 to 1, as said below
- rotor_index: int32 [8, 128, 4096], P(None, 'gx', 'gy'), may hold values from 0 to 63, as said below
Outputs:
- final_populations: float32 [27, 8, 128, 4096], P(None, None, 'gx', 'gy')
The draws below stay inside these ranges and needn't reach their ends.
Inputs may be any that keep to these rules, and one draw needn't show every extreme that they name: `populations`: every population is positive, near a jet-shaped equilibrium. Cells with turbine_mask 1 form actuator disks: the cells of one disk lie in two streamwise-neighbouring cells and within 2 cells of the disk's hub, spanwise and vertically. All cells of one disk carry one rotor_index and different disks carry different ones; some rotors have no cell with turbine_mask 1. Where turbine_mask is 0, rotor_index is arbitrary.
All inputs are finite; a program needn't handle non-finite values.
Results may differ from the reference program's by a relative error of at most 0.0001.
Values sent between devices are 32-bit elements; how exact they have to be, the bound alone decides.
No kernel may reach another device: no remote copies, remote signals or barrier semaphores. Data moves between devices by JAX's collectives and lax.ppermute only.
A program may use at most 64 MiB of HBM per device.

```python
import math
import jax
import jax.numpy as jnp
import numpy as np
from jax import lax

CX = 8
CY = 256
NZ = 8
ROTORS = 64
STEPS = 2
NX = 128
NY = 4096


def disk_cells(key):
    key = jax.random.fold_in(key, 101)
    table_key, name_key, offset_key, hub_key = jax.random.split(key, 4)
    radius = NZ // 4
    stripes_x = NX // CX
    stripes_y = NY // CY
    corners = stripes_x * stripes_y
    placed = min(ROTORS - max(1, ROTORS // 8), corners)
    corner_rank = jax.random.permutation(table_key, corners).astype(jnp.int32)
    rotor_names = jax.random.permutation(name_key, ROTORS).astype(jnp.int32)
    owner_table = rotor_names[jnp.minimum(corner_rank, ROTORS - 1)]
    offset_table = jax.random.randint(offset_key, (corners,), 1 - radius, radius, jnp.int32)
    hub_table = jax.random.randint(hub_key, (corners,), radius, NZ - radius, jnp.int32)
    level_index = jnp.arange(NZ, dtype=jnp.int32)[:, None, None]
    stream_index = jnp.arange(NX, dtype=jnp.int32)[None, :, None]
    span_index = jnp.arange(NY, dtype=jnp.int32)[None, None, :]
    edge_row = jnp.logical_or(stream_index % CX == CX - 1, stream_index % CX == 0)
    stripe_x = (stream_index + 1) // CX % stripes_x
    raw_y = (span_index + CY // 2) // CY
    corner = stripe_x * stripes_y + raw_y % stripes_y
    centre = raw_y * CY + offset_table[corner]
    apart_y = span_index - centre
    apart_z = level_index - hub_table[corner]
    within = apart_y * apart_y + apart_z * apart_z <= radius * radius
    inside = jnp.logical_and(jnp.logical_and(edge_row, corner_rank[corner] < placed), within)
    owner = jnp.broadcast_to(owner_table[corner], (NZ, NX, NY))
    return (inside, owner)


def draw_turbine_mask(key, part):
    inside, owner = disk_cells(key)
    return inside.astype(jnp.int32)


def draw_rotor_index(key, part):
    inside, owner = disk_cells(key)
    key = jax.random.fold_in(key, 13)
    filler = jax.random.randint(key, (NZ, NX, NY), 0, ROTORS, jnp.int32)
    return jnp.where(inside, owner, filler).astype(jnp.int32)


def draw_populations(key, part):
    key = jax.random.fold_in(key, 11)
    noise_key, rough_key, phase_key = jax.random.split(key, 3)
    single = jnp.array([1.0 / 6.0, 2.0 / 3.0, 1.0 / 6.0], jnp.float32)
    weights = (single[:, None, None] * single[None, :, None] * single[None, None, :]).reshape(27)
    height = (jnp.arange(NZ, dtype=jnp.float32) + 0.5) / NZ
    jet = 0.08 * jnp.sin(math.pi * height)
    signs = (jnp.arange(27) // 9 - 1).astype(jnp.float32)
    phases = jax.random.uniform(phase_key, (2,), jnp.float32, 0.0, 2.0 * math.pi)
    along = jnp.arange(NX, dtype=jnp.float32) / NX
    across = jnp.arange(NY, dtype=jnp.float32) / NY
    broad = 0.015 * jnp.sin(2.0 * math.pi * along + phases[0])[:, None] + 0.015 * jnp.sin(4.0 * math.pi * across + phases[1])[None, :]
    rough = jax.random.uniform(rough_key, (NX, NY), jnp.float32, -0.04, 0.04)
    noise = jax.random.uniform(noise_key, (27, NZ, NX, NY), jnp.float32, 0.75, 1.25)
    speed = jet[:, None, None] + (broad + rough)[None]
    base = weights[:, None, None, None] * (1.0 + 3.0 * signs[:, None, None, None] * speed[None])
    return (base * noise).astype(jnp.float32)


def block_scale(rng, dims, shards, low, high):
    def one(position, blocks):
        draws = jax.random.uniform(jax.random.fold_in(jax.random.fold_in(rng, 6), position), (blocks,), jnp.float32, low / len(shards), high / len(shards))
        return jnp.repeat(jnp.exp(draws), dims[position] // blocks).reshape((-1,) + (1,) * (len(dims) - position - 1))

    factor_of = one(*shards[0])
    for cut in shards[1:]:
        factor_of = factor_of * one(*cut)
    return factor_of


def setup_inputs(seed: int = 0) -> dict:
    seeds = jax.random.split(jax.random.key(seed), 6)
    return {
        "populations": draw_populations(jax.random.fold_in(seeds[5], 71), 0),
        "bottom_in": jnp.clip(0.01 + 0.04999999888241291 * jax.random.uniform(seeds[1], (9, NX, NY), jnp.float32) ** block_scale(seeds[1], (9, NX, NY), ((1, 16), (2, 16)), -0.2, 0.2), 0.01, 0.06),
        "top_in": jnp.clip(0.01 + 0.04999999888241291 * jax.random.uniform(seeds[2], (9, NX, NY), jnp.float32) ** block_scale(seeds[2], (9, NX, NY), ((1, 16), (2, 16)), -0.2, 0.2), 0.01, 0.06),
        "turbine_mask": draw_turbine_mask(jax.random.fold_in(seeds[5], 71), 0),
        "rotor_index": draw_rotor_index(jax.random.fold_in(seeds[5], 71), 0),
    }


SOUND = 1.0 / 3.0
TAU_BASE = 0.52
SMAG_GAIN = 5.0
HIGH_RATE = 1.0
CORIOLIS = 0.05
GEO_U = 0.08
GEO_V = 0.0
THRUST_GAIN = 4.0
EXACT = lax.Precision.HIGHEST

def moment_tables():
    vander = np.array([[1.0, 1.0, 1.0], [-1.0, 0.0, 1.0], [1.0, 0.0, 1.0]])
    inverse = np.array([[0.0, -0.5, 0.5], [1.0, 0.0, -1.0], [0.0, 0.5, 0.5]])
    forward = np.kron(np.kron(vander, vander), vander)
    backward = np.kron(np.kron(inverse, inverse), inverse)
    orders = [first + second + third for first in range(3) for second in range(3) for third in range(3)]
    return (jnp.asarray(forward, jnp.float32), jnp.asarray(backward, jnp.float32), orders)

def factors(speed):
    return jnp.stack([jnp.ones_like(speed), speed, speed * speed + SOUND])

def equilibrium(density, x_speed, y_speed, z_speed):
    along_x = factors(x_speed)
    along_y = factors(y_speed)
    along_z = factors(z_speed)
    product = density[None, None, None] * along_x[:, None, None] * along_y[None, :, None] * along_z[None, None, :]
    return product.reshape((27,) + density.shape)

def collide(flat, thrust):
    forward, backward, orders = moment_tables()
    moments = jnp.dot(forward, flat, precision=EXACT)
    density = moments[0]
    x_speed = moments[9] / density
    y_speed = moments[3] / density
    z_speed = moments[1] / density
    settled = equilibrium(density, x_speed, y_speed, z_speed)
    excess = moments - settled
    strain = excess[18] * excess[18] + excess[6] * excess[6] + excess[2] * excess[2]
    strain = strain + 2.0 * (excess[12] * excess[12] + excess[10] * excess[10] + excess[4] * excess[4])
    omega = 1.0 / (TAU_BASE + SMAG_GAIN * jnp.sqrt(strain))
    second_mask = jnp.asarray([1.0 if order == 2 else 0.0 for order in orders], jnp.float32)[:, None]
    high_mask = jnp.asarray([1.0 if order >= 3 else 0.0 for order in orders], jnp.float32)[:, None]
    rate = second_mask * omega[None, :] + high_mask * HIGH_RATE
    x_push = CORIOLIS * (y_speed - GEO_V) - thrust
    y_push = -CORIOLIS * (x_speed - GEO_U)
    forced = equilibrium(density, x_speed + x_push, y_speed + y_push, z_speed)
    relaxed = moments - rate * excess + (forced - settled)
    return jnp.dot(backward, relaxed, precision=EXACT)

def streamwise(populations):
    signs = jnp.asarray(np.repeat(np.array([-1.0, 0.0, 1.0]), 9), jnp.float32)
    x_flux = lax.optimization_barrier(jnp.sum(signs[:, None, None, None] * populations, 0))
    return x_flux / lax.optimization_barrier(jnp.sum(populations, 0))

def vertical(shifted, slot, bottom_in, top_in):
    upward = slot % 3
    column = slot // 3
    if upward == 2:
        return jnp.concatenate([bottom_in[column][None], shifted[:-1]], 0)
    if upward == 0:
        return jnp.concatenate([shifted[1:], top_in[column][None]], 0)
    return shifted

def stream(post, bottom_in, top_in):
    layers = []
    for slot in range(27):
        across = slot // 9
        span = slot // 3 % 3
        shifted = jnp.roll(post[slot], (across - 1, span - 1), axis=(1, 2))
        layers.append(vertical(shifted, slot, bottom_in, top_in))
    return jnp.stack(layers)

def one_row(pair):
    block, push = pair
    return collide(block.reshape(27, -1), push.reshape(-1)).reshape(block.shape)

def reference(populations, bottom_in, top_in, turbine_mask, rotor_index):
    covered = turbine_mask.astype(jnp.float32)
    owners = rotor_index.reshape(-1)
    counts = jax.ops.segment_sum(covered.reshape(-1), owners, num_segments=ROTORS)
    state = populations
    for _ in range(STEPS):
        x_speed = streamwise(state)
        totals = jax.ops.segment_sum((x_speed * covered).reshape(-1), owners, num_segments=ROTORS)
        disk = totals / jnp.maximum(counts, 1.0)
        thrust = covered * THRUST_GAIN * (disk * jnp.abs(disk))[rotor_index]
        by_rows = jnp.moveaxis(state, 2, 0)
        thrust_rows = jnp.moveaxis(thrust, 1, 0)
        post = jnp.moveaxis(lax.map(one_row, (by_rows, thrust_rows)), 0, 2)
        state = stream(post, bottom_in, top_in)
    return state
```

```python
import functools

import jax
import jax.numpy as jnp
from jax import lax
from jax.experimental import pallas as pl
from jax.experimental.pallas import tpu as pltpu
from jax.sharding import PartitionSpec as P

ROTORS = 64
SOUND = 1.0 / 3.0
TAU_BASE = 0.52
SMAG_GAIN = 5.0
CORIOLIS = 0.05
GEO_U = 0.08
THRUST_GAIN = 4.0
EMPTY = 127
LEVELS = 8
VMEM_LIMIT = 48 * 1024 * 1024

RHO, VX, VY, VZ, DXX, DYY, DZZ, DXY, DXZ, DYZ = range(10)
X_FIELDS = (RHO, VX, VY, VZ, DXX, DXY, DXZ)
Y_FIELDS = (RHO, VX, VY, VZ, DYY, DXY, DYZ)


def iota(axis):
    return lax.broadcasted_iota(jnp.int32, (8, 128), axis)


def roll(block, shift, axis):
    size = block.shape[axis]
    return pltpu.roll(block, shift % size, axis) if shift % size else block


def low_moments(f):
    along_z = {}
    for a in range(3):
        for b in range(3):
            low, mid, high = f(a, b, 0), f(a, b, 1), f(a, b, 2)
            ends = low + high
            along_z[a, b] = (ends + mid, high - low, ends)
    slabs = []
    for a in range(3):
        (l0, l1, l2), (m0, m1, m2), (h0, h1, h2) = (along_z[a, b] for b in range(3))
        ends = l0 + h0
        slabs.append((ends + m0, h0 - l0, ends, l1 + m1 + h1, h1 - l1, l2 + m2 + h2))
    low, mid, high = slabs
    ends = low[0] + high[0]
    return {
        "0": ends + mid[0],
        "x": high[0] - low[0],
        "xx": ends,
        "y": low[1] + mid[1] + high[1],
        "xy": high[1] - low[1],
        "yy": low[2] + mid[2] + high[2],
        "z": low[3] + mid[3] + high[3],
        "xz": high[3] - low[3],
        "yz": low[4] + mid[4] + high[4],
        "zz": low[5] + mid[5] + high[5],
    }


def relax(m):
    rho = m["0"]
    inverse = 1.0 / rho
    ux, uy, uz = m["x"] * inverse, m["y"] * inverse, m["z"] * inverse
    third = rho * SOUND
    qxx = m["xx"] - (m["x"] * ux + third)
    qyy = m["yy"] - (m["y"] * uy + third)
    qzz = m["zz"] - (m["z"] * uz + third)
    qxy = m["xy"] - m["x"] * uy
    qxz = m["xz"] - m["x"] * uz
    qyz = m["yz"] - m["y"] * uz
    strain = qxx * qxx + qyy * qyy + qzz * qzz + 2.0 * (qxy * qxy + qxz * qxz + qyz * qyz)
    keep = 1.0 - 1.0 / (TAU_BASE + SMAG_GAIN * jnp.sqrt(strain))
    vx = ux + CORIOLIS * uy
    vy = uy - CORIOLIS * (ux - GEO_U)
    fields = [rho, vx, vy, uz] + [keep * q for q in (qxx, qyy, qzz, qxy, qxz, qyz)]
    return ux, fields


def shapes(speed):
    square = speed * speed + SOUND
    return (0.5 * (square - speed), 1.0 - square, 0.5 * (square + speed))


def spread(values):
    lanes = iota(1)
    stride = 1
    while len(values) > 1:
        first = (lanes & stride) == 0
        values = [
            jnp.where(first, a, b) + roll(jnp.where(first, b, a), stride, 1)
            for a, b in zip(values[0::2], values[1::2])
        ]
        stride *= 2
    total = values[0]
    while stride < 128:
        total = total + roll(total, stride, 1)
        stride *= 2
    for shift in (4, 2, 1):
        total = total + roll(total, shift, 0)
    return total


def rotor_sums(labels, speeds, with_counts):
    sums, counts = [], []
    for rotor in range(ROTORS):
        total = jnp.zeros((8, 128), jnp.float32)
        count = jnp.zeros((8, 128), jnp.float32)
        for label, speed in zip(labels, speeds):
            hit = label == rotor
            total = total + jnp.where(hit, speed, 0.0)
            if with_counts:
                count = count + jnp.where(hit, 1.0, 0.0)
        sums.append(total)
        counts.append(count)
    if with_counts:
        return spread(sums + counts)
    return jnp.where(iota(1) < ROTORS, spread(sums), 0.0)


def collide(f, label, state, to_right, to_left, edges, with_labels):
    lanes = iota(1)
    rows = iota(0)
    labels, speeds = [], []
    right_edge = jnp.zeros((8, 128), jnp.float32)
    left_edge = jnp.zeros((8, 128), jnp.float32)
    for z in range(LEVELS):
        halves = []
        for j in range(2):
            ux, fields = relax(low_moments(functools.partial(f, z, j)))
            for index, value in enumerate(fields):
                state[index, j, 8 * z : 8 * z + 8, :] = value
            mark = label(z, j)
            labels.append(mark)
            speeds.append(ux)
            halves.append([fields[index] for index in Y_FIELDS] + [mark.astype(jnp.float32)])
        for index in range(8):
            both = jnp.where(lanes == 0, halves[0][index], halves[1][index])
            place = 16 * index + 2 * z
            moved = roll(both, place + 1, 1)
            right_edge = jnp.where(lanes == place, moved, right_edge)
            left_edge = jnp.where(lanes == place + 1, moved, left_edge)
    edges[0] = right_edge
    edges[1] = left_edge
    for target, row in ((to_right, 7), (to_left, 0)):
        slot = 0
        for index in X_FIELDS:
            for j in range(2):
                target[slot] = state[index, j, pl.ds(row, 8, stride=8), :]
                slot += 1
    sums = rotor_sums(labels, speeds, with_labels)
    for target, row in ((to_right, 7), (to_left, 0)):
        last = target.shape[0] - 1
        upper = jnp.broadcast_to(right_edge[row : row + 1], (8, 128))
        lower = jnp.broadcast_to(left_edge[row : row + 1], (8, 128))
        target[last] = jnp.where(rows == 0, upper, jnp.where(rows == 1, lower, sums))
    edges[2] = sums


def first_kernel(f_ref, mask_ref, rotor_ref, state, labels, to_right, to_left, edges):
    def f(z, j, a, b, c):
        return f_ref[9 * a + 3 * b + c, z, :, 128 * j : 128 * j + 128]

    def label(z, j):
        here = (z, slice(None), slice(128 * j, 128 * j + 128))
        mark = jnp.where(mask_ref[here] != 0, rotor_ref[here], EMPTY)
        labels[j, 8 * z : 8 * z + 8, :] = mark
        return mark

    collide(f, label, state, to_right, to_left, edges, True)
    for target, row in ((to_right, 7), (to_left, 0)):
        for j in range(2):
            target[2 * len(X_FIELDS) + j] = labels[j, pl.ds(row, 8, stride=8), :].astype(jnp.float32)


def relay_kernel(edges, left, right, to_up, to_down):
    rows = iota(0)
    last = left.shape[0] - 1
    a, b = left[last], right[last]
    sums = edges[2] + a[2:3] + b[2:3]
    to_up[0] = edges[0]
    to_up[1] = jnp.where(rows == 0, a[0:1], jnp.where(rows == 7, b[0:1], sums))
    to_down[0] = edges[1]
    to_down[1] = jnp.where(rows == 0, a[1:2], jnp.where(rows == 7, b[1:2], sums))


def look_up(table, label):
    return jnp.take_along_axis(table, label, axis=1, mode="promise_in_bounds")


def stream(table, state, labels, left, right, left_marks, right_marks, below, above, bottom, top, out, ghost):
    lanes = iota(1)
    rows = iota(0)
    for side, (source, marks) in enumerate(((left, left_marks), (right, right_marks))):
        a = 2 - 2 * side
        sign = 1.0 - 2.0 * side
        for j in range(2):
            rho, vx, vy, vz, dxx, dxy, dxz = (source[2 * n + j] for n in range(7))
            vx = vx - look_up(table, marks(j))
            part = rho * shapes(vx)[a]
            along_y, along_z = shapes(vy), shapes(vz)
            for b in range(3):
                column = part * along_y[b]
                for c in range(3):
                    value = column * along_z[c]
                    if b == 1 and c == 1:
                        value = value + 0.5 * dxx
                    elif c == 1:
                        value = value + (0.25 * sign * (b - 1)) * dxy
                    elif b == 1:
                        value = value + (0.25 * sign * (c - 1)) * dxz
                    ghost[side, 3 * b + c, j] = value

    even = (lanes & 1) == 0
    sign = jnp.where(even, 0.25, -0.25)

    def column_slots(block, wanted):
        rho, vx, vy, vz, dyy, dxy, dyz, mark = (roll(block, -16 * n, 1) for n in range(8))
        vx = vx - look_up(table, jnp.clip(mark, 0.0, float(EMPTY)).astype(jnp.int32))
        along_x, along_y, along_z = shapes(vx), shapes(vy), shapes(vz)
        part = rho * jnp.where(even, along_y[2], along_y[0])
        slots = {}
        for a in wanted:
            piece = part * along_x[a]
            for c in range(3):
                value = piece * along_z[c]
                if a == 1 and c == 1:
                    value = value + 0.5 * dyy
                elif c == 1:
                    value = value + ((a - 1) * sign) * dxy
                elif a == 1:
                    value = value + ((c - 1) * sign) * dyz
                slots[a, c] = value
        return slots

    def merged(n):
        return jnp.where(even, below[n], roll(above[n], -2, 1))

    columns = column_slots(merged(0), (0, 1, 2))
    corners = column_slots(merged(1), (0, 2))
    for c in range(3):
        columns[2, c] = jnp.where(rows == 0, corners[2, c], roll(columns[2, c], 1, 0))
        columns[0, c] = jnp.where(rows == 7, corners[0, c], roll(columns[0, c], -1, 0))

    for z in range(LEVELS):
        tiles = []
        for j in range(2):
            fields = [state[index, j, 8 * z : 8 * z + 8, :] for index in range(10)]
            thrust = look_up(table, labels[j, 8 * z : 8 * z + 8, :])
            parts = [fields[RHO] * h for h in shapes(fields[VX] - thrust)]
            tiles.append((fields, parts, shapes(fields[VY]), shapes(fields[VZ])))
        for c in range(3):
            level = z + c - 1
            if level < 0 or level >= LEVELS:
                continue
            for a in range(3):
                inflow = roll(columns[a, c], -2 * z, 1)
                for b in range(3):
                    values = []
                    for j, (d, parts, along_y, along_z) in enumerate(tiles):
                        value = parts[a] * along_y[b] * along_z[c]
                        ones = (a == 1) + (b == 1) + (c == 1)
                        if ones == 3:
                            value = value - (d[DXX] + d[DYY] + d[DZZ])
                        elif ones == 2:
                            value = value + 0.5 * (d[DXX] if a != 1 else d[DYY] if b != 1 else d[DZZ])
                        elif ones == 1 and c == 1:
                            value = value + (0.25 * (a - 1) * (b - 1)) * d[DXY]
                        elif ones == 1 and b == 1:
                            value = value + (0.25 * (a - 1) * (c - 1)) * d[DXZ]
                        elif ones == 1:
                            value = value + (0.25 * (b - 1) * (c - 1)) * d[DYZ]
                        if a == 2:
                            value = jnp.where(rows == 0, ghost[0, 3 * b + c, j, z : z + 1, :], roll(value, 1, 0))
                        elif a == 0:
                            value = jnp.where(rows == 7, ghost[1, 3 * b + c, j, z : z + 1, :], roll(value, -1, 0))
                        values.append(value)
                    first, second = values
                    if b == 2:
                        first, second = roll(first, 1, 1), roll(second, 1, 1)
                        second = jnp.where(lanes == 0, first, second)
                        first = jnp.where(lanes == 0, inflow, first)
                    elif b == 0:
                        first, second = roll(first, -1, 1), roll(second, -1, 1)
                        first = jnp.where(lanes == 127, second, first)
                        second = jnp.where(lanes == 127, inflow, second)
                    out[9 * a + 3 * b + c, level, :, 0:128] = first
                    out[9 * a + 3 * b + c, level, :, 128:256] = second
    for a in range(3):
        for b in range(3):
            out[9 * a + 3 * b + 2, 0] = bottom[3 * a + b]
            out[9 * a + 3 * b, LEVELS - 1] = top[3 * a + b]


def disk_table(sums, counts):
    disk = sums / jnp.maximum(counts, 1.0)
    return jnp.where(iota(1) < ROTORS, THRUST_GAIN * disk * jnp.abs(disk), 0.0)


def all_sums(edges, left, right, below, above):
    last = left.shape[0] - 1
    return edges[2] + left[last][2:3] + right[last][2:3] + below[1][2:3] + above[1][2:3]


def marks_of(message):
    return lambda j: message[2 * len(X_FIELDS) + j].astype(jnp.int32)


def middle_kernel(
    state, labels, edges, left, right, below, above, bottom, top,
    new_state, to_right, to_left, new_edges, counts, f_ref, ghost,
):
    totals = all_sums(edges, left, right, below, above)
    seen = roll(totals, 64, 1)
    counts[...] = seen
    table = disk_table(totals, seen)
    stream(table, state, labels, left, right, marks_of(left), marks_of(right), below, above, bottom, top, f_ref, ghost)

    def f(z, j, a, b, c):
        return f_ref[9 * a + 3 * b + c, z, :, 128 * j : 128 * j + 128]

    def label(z, j):
        return labels[j, 8 * z : 8 * z + 8, :]

    collide(f, label, new_state, to_right, to_left, new_edges, False)


def last_kernel(
    state, labels, edges, left, right, old_left, old_right, below, above, bottom, top, counts, out, ghost
):
    totals = all_sums(edges, left, right, below, above)
    table = disk_table(totals, counts[...])
    stream(table, state, labels, left, right, marks_of(old_left), marks_of(old_right), below, above, bottom, top, out, ghost)


def call(kernel, inputs, outputs, scratch=()):
    whole = pl.BlockSpec(memory_space=pltpu.VMEM)
    return pl.pallas_call(
        kernel,
        out_shape=[jax.ShapeDtypeStruct(shape, dtype) for shape, dtype in outputs],
        in_specs=[whole] * len(inputs),
        out_specs=[whole] * len(outputs),
        scratch_shapes=[pltpu.VMEM(shape, jnp.float32) for shape in scratch],
        compiler_params=pltpu.CompilerParams(vmem_limit_bytes=VMEM_LIMIT),
    )(*inputs)


def both_ways(upward, downward, axis):
    count = lax.axis_size(axis)
    return (
        lax.ppermute(upward, axis, [(i, (i + 1) % count) for i in range(count)]),
        lax.ppermute(downward, axis, [((i + 1) % count, i) for i in range(count)]),
    )


def body(populations, bottom_in, top_in, turbine_mask, rotor_index):
    f32 = jnp.float32
    state_shape = ((10, 2, 64, 128), f32)
    edge_shape = ((3, 8, 128), f32)
    y_shape = ((2, 8, 128), f32)
    ghost = (2, 9, 2, 8, 128)
    n = 2 * len(X_FIELDS)
    x_first, x_later = ((n + 3, 8, 128), f32), ((n + 1, 8, 128), f32)

    state, labels, to_right, to_left, edges = call(
        first_kernel,
        (populations, turbine_mask, rotor_index),
        (state_shape, ((2, 64, 128), jnp.int32), x_first, x_first, edge_shape),
    )
    left, right = both_ways(to_right, to_left, "gx")
    to_up, to_down = call(relay_kernel, (edges, left, right), (y_shape, y_shape))
    below, above = both_ways(to_up, to_down, "gy")

    state, to_right, to_left, edges, counts = call(
        middle_kernel,
        (state, labels, edges, left, right, below, above, bottom_in, top_in),
        (state_shape, x_later, x_later, edge_shape, ((8, 128), f32)),
        (populations.shape, ghost),
    )
    old_left, old_right = left, right
    left, right = both_ways(to_right, to_left, "gx")
    to_up, to_down = call(relay_kernel, (edges, left, right), (y_shape, y_shape))
    below, above = both_ways(to_up, to_down, "gy")

    (out,) = call(
        last_kernel,
        (state, labels, edges, left, right, old_left, old_right, below, above, bottom_in, top_in, counts),
        ((populations.shape, f32),),
        (ghost,),
    )
    return out


def solution(mesh):
    placed = (
        P(None, None, "gx", "gy"),
        P(None, "gx", "gy"),
        P(None, "gx", "gy"),
        P(None, "gx", "gy"),
        P(None, "gx", "gy"),
    )
    return jax.shard_map(
        body, mesh=mesh, in_specs=placed, out_specs=P(None, None, "gx", "gy"), check_vma=False
    )
```

```python
import functools

import jax
import jax.numpy as jnp
from jax import lax
from jax.experimental import pallas as pl
from jax.experimental.pallas import tpu as pltpu
from jax.sharding import PartitionSpec as P

ROTORS = 64
SOUND = 1.0 / 3.0
TAU_BASE = 0.52
SMAG_GAIN = 5.0
CORIOLIS = 0.05
GEO_U = 0.08
THRUST_GAIN = 4.0
EMPTY = 127
LEVELS = 8
VMEM_LIMIT = 48 * 1024 * 1024

RHO, VX, VY, VZ, DXX, DYY, DZZ, DXY, DXZ, DYZ = range(10)
X_FIELDS = (RHO, VX, VY, VZ, DXX, DXY, DXZ)
Y_FIELDS = (RHO, VX, VY, VZ, DYY, DXY, DYZ)


def iota(axis):
    return lax.broadcasted_iota(jnp.int32, (8, 128), axis)


def roll(block, shift, axis):
    size = block.shape[axis]
    return pltpu.roll(block, shift % size, axis) if shift % size else block


def low_moments(f):
    along_z = {}
    for a in range(3):
        for b in range(3):
            low, mid, high = f(a, b, 0), f(a, b, 1), f(a, b, 2)
            ends = low + high
            along_z[a, b] = (ends + mid, high - low, ends)
    slabs = []
    for a in range(3):
        (l0, l1, l2), (m0, m1, m2), (h0, h1, h2) = (along_z[a, b] for b in range(3))
        ends = l0 + h0
        slabs.append((ends + m0, h0 - l0, ends, l1 + m1 + h1, h1 - l1, l2 + m2 + h2))
    low, mid, high = slabs
    ends = low[0] + high[0]
    return {
        "0": ends + mid[0],
        "x": high[0] - low[0],
        "xx": ends,
        "y": low[1] + mid[1] + high[1],
        "xy": high[1] - low[1],
        "yy": low[2] + mid[2] + high[2],
        "z": low[3] + mid[3] + high[3],
        "xz": high[3] - low[3],
        "yz": low[4] + mid[4] + high[4],
        "zz": low[5] + mid[5] + high[5],
    }


def relax(m):
    rho = m["0"]
    inverse = 1.0 / rho
    ux, uy, uz = m["x"] * inverse, m["y"] * inverse, m["z"] * inverse
    third = rho * SOUND
    qxx = m["xx"] - (m["x"] * ux + third)
    qyy = m["yy"] - (m["y"] * uy + third)
    qzz = m["zz"] - (m["z"] * uz + third)
    qxy = m["xy"] - m["x"] * uy
    qxz = m["xz"] - m["x"] * uz
    qyz = m["yz"] - m["y"] * uz
    strain = qxx * qxx + qyy * qyy + qzz * qzz + 2.0 * (qxy * qxy + qxz * qxz + qyz * qyz)
    keep = 1.0 - 1.0 / (TAU_BASE + SMAG_GAIN * jnp.sqrt(strain))
    vx = ux + CORIOLIS * uy
    vy = uy - CORIOLIS * (ux - GEO_U)
    fields = [rho, vx, vy, uz] + [keep * q for q in (qxx, qyy, qzz, qxy, qxz, qyz)]
    return ux, fields


def shapes(speed):
    square = speed * speed + SOUND
    return (0.5 * (square - speed), 1.0 - square, 0.5 * (square + speed))


def spread(values):
    lanes = iota(1)
    stride = 1
    while len(values) > 1:
        first = (lanes & stride) == 0
        values = [
            jnp.where(first, a, b) + roll(jnp.where(first, b, a), stride, 1)
            for a, b in zip(values[0::2], values[1::2])
        ]
        stride *= 2
    total = values[0]
    while stride < 128:
        total = total + roll(total, stride, 1)
        stride *= 2
    for shift in (4, 2, 1):
        total = total + roll(total, shift, 0)
    return total


def rotor_sums(labels, speeds, with_counts):
    sums, counts = [], []
    for rotor in range(ROTORS):
        total = jnp.zeros((8, 128), jnp.float32)
        count = jnp.zeros((8, 128), jnp.float32)
        for label, speed in zip(labels, speeds):
            hit = label == rotor
            total = total + jnp.where(hit, speed, 0.0)
            if with_counts:
                count = count + jnp.where(hit, 1.0, 0.0)
        sums.append(total)
        counts.append(count)
    if with_counts:
        return spread(sums + counts)
    return jnp.where(iota(1) < ROTORS, spread(sums), 0.0)


def collide(f, label, state, marks=(), speeds=(), first=False):
    marks, speeds = list(marks), list(speeds)
    for z in range(LEVELS):
        for j in range(2):
            ux, fields = relax(low_moments(functools.partial(f, z, j)))
            for index, value in enumerate(fields):
                state[index, j, 8 * z : 8 * z + 8, :] = value
            marks.append(label(z, j))
            speeds.append(ux)
    return rotor_sums(marks, speeds, first)


def first_kernel(f_ref, mask_ref, rotor_ref, bottom, top, state, labels, edges, to_up, to_down):
    lanes = iota(1)

    def f(z, j, a, b, c):
        return f_ref[9 * a + 3 * b + c, z, :, 128 * j : 128 * j + 128]

    def label(z, j):
        here = (z, slice(None), slice(128 * j, 128 * j + 128))
        mark = jnp.where(mask_ref[here] != 0, rotor_ref[here], EMPTY)
        labels[j, 8 * z : 8 * z + 8, :] = mark
        return mark

    sums = collide(f, label, state, first=True)

    def edge(read):
        block = jnp.zeros((8, 128), jnp.float32)
        for z in range(LEVELS):
            both = jnp.where(lanes < 64, read(z, 0), read(z, 1))
            block = jnp.where(lanes // 16 == z, roll(both, 16 * z + 8, 1), block)
        return block

    blocks = [edge(lambda z, j, n=n: state[n, j, 8 * z : 8 * z + 8, :]) for n in range(10)]
    blocks.append(edge(lambda z, j: labels[j, 8 * z : 8 * z + 8, :].astype(jnp.float32)))
    for n, block in enumerate(blocks):
        edges[n] = block
    edges[11] = sums
    low = (lanes & 8) == 0
    for n in range(6):
        one = blocks[2 * n]
        other = blocks[2 * n + 1] if n < 5 else one
        to_up[n] = jnp.where(low, one, roll(other, 8, 1))
        to_down[n] = jnp.where(low, roll(other, -8, 1), one)
    to_up[6] = sums
    to_down[6] = sums
    for place, source in ((7, bottom), (8, top)):
        upward = jnp.zeros((8, 128), jnp.float32)
        downward = upward
        for n in range(9):
            both = jnp.where(lanes < 64, source[n, :, 0:128], source[n, :, 128:256])
            moved = roll(both, 8 * n + 8, 1)
            upward = jnp.where(lanes // 8 == n, moved, upward)
            downward = jnp.where(lanes // 8 == n + 1, moved, downward)
        to_up[place] = upward
        to_down[place] = downward


def rows_of(blocks, row):
    rows = iota(0)
    out = jnp.broadcast_to(blocks[0][row : row + 1], (8, 128))
    for n in range(1, len(blocks)):
        out = jnp.where(rows == n, jnp.broadcast_to(blocks[n][row : row + 1], (8, 128)), out)
    return out


def edge_rows(state, target, row):
    slot = 0
    for index in X_FIELDS:
        for j in range(2):
            target[slot] = state[index, j, pl.ds(row, 8, stride=8), :]
            slot += 1
    return slot


def relay_kernel(state, labels, edges, below, above, domains, to_right, to_left, column_sums):
    low = (iota(1) & 8) == 0
    sums = edges[11] + below[6] + above[6]
    column_sums[...] = sums
    for n in range(11):
        under, over = below[n // 2], above[n // 2]
        if n % 2:
            under, over = roll(under, -8, 1), roll(over, 8, 1)
        domains[0, n] = jnp.where(low, under, edges[n])
        domains[1, n] = jnp.where(low, edges[n], over)
    for target, row in ((to_right, 7), (to_left, 0)):
        slot = edge_rows(state, target, row)
        for j in range(2):
            target[slot + j] = labels[j, pl.ds(row, 8, stride=8), :].astype(jnp.float32)
        for side in range(2):
            target[slot + 2 + side] = rows_of([domains[side, n] for n in X_FIELDS + (10,)], row)
        target[slot + 4] = sums


def look_up(table, label):
    return jnp.take_along_axis(table, label, axis=1, mode="promise_in_bounds")


def index_of(mark):
    return jnp.clip(mark, 0.0, float(EMPTY)).astype(jnp.int32)


def slot_value(d, parts, along_y, along_z, a, b, c):
    value = parts[a] * along_y[b] * along_z[c]
    ones = (a == 1) + (b == 1) + (c == 1)
    if ones == 3:
        return value - (d[DXX] + d[DYY] + d[DZZ])
    if ones == 2:
        return value + 0.5 * (d[DXX] if a != 1 else d[DYY] if b != 1 else d[DZZ])
    if ones == 1 and c == 1:
        return value + (0.25 * (a - 1) * (b - 1)) * d[DXY]
    if ones == 1 and b == 1:
        return value + (0.25 * (a - 1) * (c - 1)) * d[DXZ]
    if ones == 1:
        return value + (0.25 * (b - 1) * (c - 1)) * d[DYZ]
    return value


def entering(table, fields, mark, a):
    rho, vx, vy, vz, dxx, dxy, dxz = fields
    part = rho * shapes(vx - look_up(table, mark))[a]
    d = {DXX: dxx, DXY: dxy, DXZ: dxz}
    along_y, along_z = shapes(vy), shapes(vz)
    return {(b, c): slot_value(d, {a: part}, along_y, along_z, a, b, c) for b in range(3) for c in range(3)}


def shift_rows(value, a, before, after):
    if a == 2:
        return jnp.where(iota(0) == 0, before, roll(value, 1, 0))
    if a == 0:
        return jnp.where(iota(0) == 7, after, roll(value, -1, 0))
    return value


def row_blocks(block, count):
    return [jnp.broadcast_to(block[n : n + 1], (8, 128)) for n in range(count)]


def step_domain(table, side, domains, left, right, below, above):
    lanes = iota(1)
    d = [domains[side, n] for n in range(10)]
    thrust = look_up(table, index_of(domains[side, 10]))
    parts = [d[RHO] * h for h in shapes(d[VX] - thrust)]
    along_y, along_z = shapes(d[VY]), shapes(d[VZ])
    n = 2 * len(X_FIELDS) + 2 + side
    beside = {}
    for a, message in ((2, left), (0, right)):
        fields = row_blocks(message[n], 8)
        beside[a] = entering(table, fields[:7], index_of(fields[7]), a)
    into, new = {}, {}
    for a in range(3):
        for b in range(3):
            for c in range(3):
                value = slot_value(d, parts, along_y, along_z, a, b, c)
                value = shift_rows(value, a, beside[2][b, c], beside[0][b, c])
                value = roll(value, b - 1, 1)
                if b == 2 - 2 * side:
                    into[a, c] = value
                slot = 3 * a + b
                message = above if side else below
                if c == 2:
                    value = jnp.where(lanes < 16, roll(message[7], -8 * slot, 1), roll(value, 16, 1))
                elif c == 0:
                    value = jnp.where(lanes >= 112, roll(message[8], 112 - 8 * slot, 1), roll(value, -16, 1))
                new[a, b, c] = value
    return into, new


def last_columns(table, strip, left, right):
    even = (iota(1) & 1) == 0
    sign = jnp.where(even, 0.25, -0.25)

    def slots_of(fields, wanted):
        rho, vx, vy, vz, dyy, dxy, dyz, mark = fields
        along_x, along_y, along_z = shapes(vx - look_up(table, index_of(mark))), shapes(vy), shapes(vz)
        part = rho * jnp.where(even, along_y[2], along_y[0])
        slots = {}
        for a in wanted:
            piece = part * along_x[a]
            for c in range(3):
                value = piece * along_z[c]
                if a == 1 and c == 1:
                    value = value + 0.5 * dyy
                elif c == 1:
                    value = value + ((a - 1) * sign) * dxy
                elif a == 1:
                    value = value + ((c - 1) * sign) * dyz
                slots[a, c] = value
        return slots

    n = 2 * len(X_FIELDS)
    columns = slots_of([strip[k] for k in range(8)], (0, 1, 2))
    before = slots_of(row_blocks(left[n], 8), (2,))
    after = slots_of(row_blocks(right[n], 8), (0,))
    for c in range(3):
        columns[2, c] = shift_rows(columns[2, c], 2, before[2, c], None)
        columns[0, c] = shift_rows(columns[0, c], 0, None, after[0, c])
    return columns


def stream(table, state, labels, columns, left, right, left_marks, right_marks, bottom, top, out, ghost):
    lanes = iota(1)
    for side, (source, marks) in enumerate(((left, left_marks), (right, right_marks))):
        a = 2 - 2 * side
        for j in range(2):
            fields = [source[2 * n + j] for n in range(len(X_FIELDS))]
            for (b, c), value in entering(table, fields, marks(j), a).items():
                ghost[side, 3 * b + c, j] = value

    for z in range(LEVELS):
        tiles = []
        for j in range(2):
            fields = [state[index, j, 8 * z : 8 * z + 8, :] for index in range(10)]
            thrust = look_up(table, labels[j, 8 * z : 8 * z + 8, :])
            parts = [fields[RHO] * h for h in shapes(fields[VX] - thrust)]
            tiles.append((fields, parts, shapes(fields[VY]), shapes(fields[VZ])))
        for c in range(3):
            level = z + c - 1
            if level < 0 or level >= LEVELS:
                continue
            for a in range(3):
                inflow = roll(columns[a, c], -16 * z - 8, 1)
                for b in range(3):
                    first, second = (
                        shift_rows(
                            slot_value(*tile, a, b, c),
                            a,
                            ghost[0, 3 * b + c, j, z : z + 1, :],
                            ghost[1, 3 * b + c, j, z : z + 1, :],
                        )
                        for j, tile in enumerate(tiles)
                    )
                    if b == 2:
                        first, second = roll(first, 1, 1), roll(second, 1, 1)
                        second = jnp.where(lanes == 0, first, second)
                        first = jnp.where(lanes == 0, inflow, first)
                    elif b == 0:
                        first, second = roll(first, -1, 1), roll(second, -1, 1)
                        first = jnp.where(lanes == 127, second, first)
                        second = jnp.where(lanes == 127, inflow, second)
                    out[9 * a + 3 * b + c, level, :, 0:128] = first
                    out[9 * a + 3 * b + c, level, :, 128:256] = second
    for a in range(3):
        for b in range(3):
            out[9 * a + 3 * b + 2, 0] = bottom[3 * a + b]
            out[9 * a + 3 * b, LEVELS - 1] = top[3 * a + b]


def disk_table(sums, counts):
    disk = sums / jnp.maximum(counts, 1.0)
    return jnp.where(iota(1) < ROTORS, THRUST_GAIN * disk * jnp.abs(disk), 0.0)


def marks_of(message):
    return lambda j: message[2 * len(X_FIELDS) + j].astype(jnp.int32)


def middle_kernel(
    state, labels, domains, column_sums, left, right, below, above, bottom, top,
    new_state, to_right, to_left, strip, counts, sums_out, f_ref, ghost,
):
    lanes = iota(1)
    even = (lanes & 1) == 0
    last = 2 * len(X_FIELDS) + 4
    totals = column_sums[...] + left[last] + right[last]
    seen = roll(totals, 64, 1)
    counts[...] = seen
    table = disk_table(totals, seen)

    marks, speeds, kept, columns = [], [], [], [{}, {}]
    for side in range(2):
        columns[side], new = step_domain(table, side, domains, left, right, below, above)
        ux, fields = relax(low_moments(lambda a, b, c: new[a, b, c]))
        column = lanes & 15
        near = jnp.logical_and(column >= 8, column < 13) if side else jnp.logical_and(column >= 3, column < 8)
        mark = domains[side, 10]
        marks.append(jnp.where(near, index_of(mark), EMPTY))
        speeds.append(ux)
        kept.append([fields[n] for n in Y_FIELDS] + [mark])
    strips = [jnp.where(even, roll(one, 1, 1), roll(other, -1, 1)) for one, other in zip(*kept)]
    for n, block in enumerate(strips):
        strip[n] = block
    merged = {key: jnp.where(even, columns[0][key], columns[1][key]) for key in columns[0]}
    stream(table, state, labels, merged, left, right, marks_of(left), marks_of(right), bottom, top, f_ref, ghost)

    def f(z, j, a, b, c):
        return f_ref[9 * a + 3 * b + c, z, :, 128 * j : 128 * j + 128]

    def label(z, j):
        return labels[j, 8 * z : 8 * z + 8, :]

    sums = collide(f, label, new_state, marks, speeds)
    sums_out[...] = sums
    for target, row in ((to_right, 7), (to_left, 0)):
        slot = edge_rows(new_state, target, row)
        target[slot] = rows_of(strips, row)
        target[slot + 1] = sums


def last_kernel(
    state, labels, strip, sums, counts, left, right, old_left, old_right, bottom, top, out, ghost
):
    last = 2 * len(X_FIELDS) + 1
    totals = sums[...] + left[last] + right[last]
    table = disk_table(totals, counts[...])
    columns = last_columns(table, strip, left, right)
    stream(table, state, labels, columns, left, right, marks_of(old_left), marks_of(old_right), bottom, top, out, ghost)


def call(kernel, inputs, outputs, scratch=()):
    whole = pl.BlockSpec(memory_space=pltpu.VMEM)
    return pl.pallas_call(
        kernel,
        out_shape=[jax.ShapeDtypeStruct(shape, dtype) for shape, dtype in outputs],
        in_specs=[whole] * len(inputs),
        out_specs=[whole] * len(outputs),
        scratch_shapes=[pltpu.VMEM(shape, jnp.float32) for shape in scratch],
        compiler_params=pltpu.CompilerParams(vmem_limit_bytes=VMEM_LIMIT),
    )(*inputs)


def both_ways(upward, downward, axis):
    count = lax.axis_size(axis)
    return (
        lax.ppermute(upward, axis, [(i, (i + 1) % count) for i in range(count)]),
        lax.ppermute(downward, axis, [((i + 1) % count, i) for i in range(count)]),
    )


def body(populations, bottom_in, top_in, turbine_mask, rotor_index):
    f32 = jnp.float32
    state_shape = ((10, 2, 64, 128), f32)
    one = ((8, 128), f32)
    ghost = (2, 9, 2, 8, 128)
    n = 2 * len(X_FIELDS)

    def blocks(*count):
        return (count + (8, 128), f32)

    state, labels, edges, to_up, to_down = call(
        first_kernel,
        (populations, turbine_mask, rotor_index, bottom_in, top_in),
        (state_shape, ((2, 64, 128), jnp.int32), blocks(12), blocks(9), blocks(9)),
    )
    below, above = both_ways(to_up, to_down, "gy")
    domains, to_right, to_left, column_sums = call(
        relay_kernel,
        (state, labels, edges, below, above),
        (blocks(2, 11), blocks(n + 5), blocks(n + 5), one),
    )
    old_left, old_right = both_ways(to_right, to_left, "gx")
    state, to_right, to_left, strip, counts, sums = call(
        middle_kernel,
        (state, labels, domains, column_sums, old_left, old_right, below, above, bottom_in, top_in),
        (state_shape, blocks(n + 2), blocks(n + 2), blocks(8), one, one),
        (populations.shape, ghost),
    )
    left, right = both_ways(to_right, to_left, "gx")
    (out,) = call(
        last_kernel,
        (state, labels, strip, sums, counts, left, right, old_left, old_right, bottom_in, top_in),
        ((populations.shape, f32),),
        (ghost,),
    )
    return out


def solution(mesh):
    placed = (
        P(None, None, "gx", "gy"),
        P(None, "gx", "gy"),
        P(None, "gx", "gy"),
        P(None, "gx", "gy"),
        P(None, "gx", "gy"),
    )
    return jax.shard_map(
        body, mesh=mesh, in_specs=placed, out_specs=P(None, None, "gx", "gy"), check_vma=False
    )
```

```python
import functools

import jax
import jax.numpy as jnp
from jax import lax
from jax.experimental import pallas as pl
from jax.experimental.pallas import tpu as pltpu
from jax.sharding import PartitionSpec as P

ROTORS = 64
SOUND = 1.0 / 3.0
TAU_BASE = 0.52
SMAG_GAIN = 5.0
CORIOLIS = 0.05
GEO_U = 0.08
THRUST_GAIN = 4.0
EMPTY = 127
LEVELS = 8
VMEM_LIMIT = 48 * 1024 * 1024

RHO, VX, VY, VZ, DXX, DYY, DZZ, DXY, DXZ, DYZ = range(10)
X_FIELDS = (RHO, VX, VY, VZ, DXX, DXY, DXZ)
Y_FIELDS = (RHO, VX, VY, VZ, DYY, DXY, DYZ)


def iota(axis):
    return lax.broadcasted_iota(jnp.int32, (8, 128), axis)


def roll(block, shift, axis):
    size = block.shape[axis]
    return pltpu.roll(block, shift % size, axis) if shift % size else block


def low_moments(f):
    along_z = {}
    for a in range(3):
        for b in range(3):
            low, mid, high = f(a, b, 0), f(a, b, 1), f(a, b, 2)
            ends = low + high
            along_z[a, b] = (ends + mid, high - low, ends)
    slabs = []
    for a in range(3):
        (l0, l1, l2), (m0, m1, m2), (h0, h1, h2) = (along_z[a, b] for b in range(3))
        ends = l0 + h0
        slabs.append((ends + m0, h0 - l0, ends, l1 + m1 + h1, h1 - l1, l2 + m2 + h2))
    low, mid, high = slabs
    ends = low[0] + high[0]
    return {
        "0": ends + mid[0],
        "x": high[0] - low[0],
        "xx": ends,
        "y": low[1] + mid[1] + high[1],
        "xy": high[1] - low[1],
        "yy": low[2] + mid[2] + high[2],
        "z": low[3] + mid[3] + high[3],
        "xz": high[3] - low[3],
        "yz": low[4] + mid[4] + high[4],
        "zz": low[5] + mid[5] + high[5],
    }


def relax(m):
    rho = m["0"]
    inverse = 1.0 / rho
    ux, uy, uz = m["x"] * inverse, m["y"] * inverse, m["z"] * inverse
    third = rho * SOUND
    qxx = m["xx"] - (m["x"] * ux + third)
    qyy = m["yy"] - (m["y"] * uy + third)
    qzz = m["zz"] - (m["z"] * uz + third)
    qxy = m["xy"] - m["x"] * uy
    qxz = m["xz"] - m["x"] * uz
    qyz = m["yz"] - m["y"] * uz
    strain = qxx * qxx + qyy * qyy + qzz * qzz + 2.0 * (qxy * qxy + qxz * qxz + qyz * qyz)
    keep = 1.0 - 1.0 / (TAU_BASE + SMAG_GAIN * jnp.sqrt(strain))
    vx = ux + CORIOLIS * uy
    vy = uy - CORIOLIS * (ux - GEO_U)
    fields = [rho, vx, vy, uz] + [keep * q for q in (qxx, qyy, qzz, qxy, qxz, qyz)]
    return ux, fields


def shapes(speed):
    square = speed * speed + SOUND
    return (0.5 * (square - speed), 1.0 - square, 0.5 * (square + speed))


def spread(values):
    lanes = iota(1)
    stride = 1
    while len(values) > 1:
        first = (lanes & stride) == 0
        values = [
            jnp.where(first, a, b) + roll(jnp.where(first, b, a), stride, 1)
            for a, b in zip(values[0::2], values[1::2])
        ]
        stride *= 2
    total = values[0]
    while stride < 128:
        total = total + roll(total, stride, 1)
        stride *= 2
    for shift in (4, 2, 1):
        total = total + roll(total, shift, 0)
    return total


def rotor_sums(labels, speeds, with_counts):
    sums, counts = [], []
    for rotor in range(ROTORS):
        total = jnp.zeros((8, 128), jnp.float32)
        count = jnp.zeros((8, 128), jnp.float32)
        for label, speed in zip(labels, speeds):
            hit = label == rotor
            total = total + jnp.where(hit, speed, 0.0)
            if with_counts:
                count = count + jnp.where(hit, 1.0, 0.0)
        sums.append(total)
        counts.append(count)
    if with_counts:
        return spread(sums + counts)
    return jnp.where(iota(1) < ROTORS, spread(sums), 0.0)


def collide(f, label, state, marks=(), speeds=(), first=False):
    marks, speeds = list(marks), list(speeds)
    for z in range(LEVELS):
        for j in range(2):
            ux, fields = relax(low_moments(functools.partial(f, z, j)))
            for index, value in enumerate(fields):
                state[index, j, 8 * z : 8 * z + 8, :] = value
            marks.append(label(z, j))
            speeds.append(ux)
    return rotor_sums(marks, speeds, first)


def first_kernel(
    f_hbm, mask_hbm, rotor_hbm, bottom_hbm, top_hbm, state, labels, edges, to_even, to_odd,
    f_ref, mask_ref, rotor_ref, bottom, top, arrived,
):
    lanes = iota(1)
    levels = [pltpu.make_async_copy(f_hbm.at[:, z], f_ref.at[:, z], arrived.at[z]) for z in range(LEVELS)]
    others = [
        pltpu.make_async_copy(source, target, arrived.at[LEVELS + n])
        for n, (source, target) in enumerate(
            ((mask_hbm, mask_ref), (rotor_hbm, rotor_ref), (bottom_hbm, bottom), (top_hbm, top))
        )
    ]
    for copy in [levels[0]] + others[:2] + levels[1:] + others[2:]:
        copy.start()
    others[0].wait()
    others[1].wait()
    waiting = list(levels)

    def f(z, j, a, b, c):
        if len(waiting) == LEVELS - z:
            waiting.pop(0).wait()
        return f_ref[9 * a + 3 * b + c, z, :, 128 * j : 128 * j + 128]

    def label(z, j):
        here = (z, slice(None), slice(128 * j, 128 * j + 128))
        mark = jnp.where(mask_ref[here] != 0, rotor_ref[here], EMPTY)
        labels[j, 8 * z : 8 * z + 8, :] = mark
        return mark

    sums = collide(f, label, state, first=True)

    def edge(read):
        block = jnp.zeros((8, 128), jnp.float32)
        for z in range(LEVELS):
            both = jnp.where(lanes < 64, read(z, 0), read(z, 1))
            block = jnp.where(lanes // 16 == z, roll(both, 16 * z + 8, 1), block)
        return block

    blocks = [edge(lambda z, j, n=n: state[n, j, 8 * z : 8 * z + 8, :]) for n in range(10)]
    blocks.append(edge(lambda z, j: labels[j, 8 * z : 8 * z + 8, :].astype(jnp.float32)))
    for n, block in enumerate(blocks):
        edges[n] = block
    edges[11] = sums
    upward_first = lax.rem(lax.axis_index("gy"), 2) == 0
    low = (lanes & 8) == 0

    def send(n, upward, downward):
        to_even[n] = jnp.where(upward_first, upward, downward)
        to_odd[n] = jnp.where(upward_first, downward, upward)

    for n in range(6):
        one = blocks[2 * n]
        other = blocks[2 * n + 1] if n < 5 else one
        send(n, jnp.where(low, one, roll(other, 8, 1)), jnp.where(low, roll(other, -8, 1), one))
    send(6, sums, sums)
    others[2].wait()
    others[3].wait()
    for place, source in ((7, bottom), (8, top)):
        upward = jnp.zeros((8, 128), jnp.float32)
        downward = upward
        for n in range(9):
            both = jnp.where(lanes < 64, source[n, :, 0:128], source[n, :, 128:256])
            moved = roll(both, 8 * n + 8, 1)
            upward = jnp.where(lanes // 8 == n, moved, upward)
            downward = jnp.where(lanes // 8 == n + 1, moved, downward)
        send(place, upward, downward)


def rows_of(blocks, row):
    rows = iota(0)
    out = jnp.broadcast_to(blocks[0][row : row + 1], (8, 128))
    for n in range(1, len(blocks)):
        out = jnp.where(rows == n, jnp.broadcast_to(blocks[n][row : row + 1], (8, 128)), out)
    return out


def edge_rows(state, target, row):
    slot = 0
    for index in X_FIELDS:
        for j in range(2):
            target[slot] = state[index, j, pl.ds(row, 8, stride=8), :]
            slot += 1
    return slot


def relay_kernel(state, labels, edges, even, odd, domains, to_right, to_left, column_sums, beside):
    upward_first = lax.rem(lax.axis_index("gy"), 2) == 0
    below = [jnp.where(upward_first, odd[n], even[n]) for n in range(9)]
    above = [jnp.where(upward_first, even[n], odd[n]) for n in range(9)]
    for side, message in enumerate((below, above)):
        for n in range(2):
            beside[side, n] = message[7 + n]
    low = (iota(1) & 8) == 0
    sums = edges[11] + below[6] + above[6]
    column_sums[...] = sums
    for n in range(11):
        under, over = below[n // 2], above[n // 2]
        if n % 2:
            under, over = roll(under, -8, 1), roll(over, 8, 1)
        domains[0, n] = jnp.where(low, under, edges[n])
        domains[1, n] = jnp.where(low, edges[n], over)
    for target, row in ((to_right, 7), (to_left, 0)):
        slot = edge_rows(state, target, row)
        for j in range(2):
            target[slot + j] = labels[j, pl.ds(row, 8, stride=8), :].astype(jnp.float32)
        for side in range(2):
            target[slot + 2 + side] = rows_of([domains[side, n] for n in X_FIELDS + (10,)], row)
        target[slot + 4] = sums


def look_up(table, label):
    return jnp.take_along_axis(table, label, axis=1, mode="promise_in_bounds")


def index_of(mark):
    return jnp.clip(mark, 0.0, float(EMPTY)).astype(jnp.int32)


def slot_value(d, parts, along_y, along_z, a, b, c):
    value = parts[a] * along_y[b] * along_z[c]
    ones = (a == 1) + (b == 1) + (c == 1)
    if ones == 3:
        return value - (d[DXX] + d[DYY] + d[DZZ])
    if ones == 2:
        return value + 0.5 * (d[DXX] if a != 1 else d[DYY] if b != 1 else d[DZZ])
    if ones == 1 and c == 1:
        return value + (0.25 * (a - 1) * (b - 1)) * d[DXY]
    if ones == 1 and b == 1:
        return value + (0.25 * (a - 1) * (c - 1)) * d[DXZ]
    if ones == 1:
        return value + (0.25 * (b - 1) * (c - 1)) * d[DYZ]
    return value


def entering(table, fields, mark, a):
    rho, vx, vy, vz, dxx, dxy, dxz = fields
    part = rho * shapes(vx - look_up(table, mark))[a]
    d = {DXX: dxx, DXY: dxy, DXZ: dxz}
    along_y, along_z = shapes(vy), shapes(vz)
    return {(b, c): slot_value(d, {a: part}, along_y, along_z, a, b, c) for b in range(3) for c in range(3)}


def shift_rows(value, a, before, after):
    if a == 2:
        return jnp.where(iota(0) == 0, before, roll(value, 1, 0))
    if a == 0:
        return jnp.where(iota(0) == 7, after, roll(value, -1, 0))
    return value


def row_blocks(block, count):
    return [jnp.broadcast_to(block[n : n + 1], (8, 128)) for n in range(count)]


def step_domain(table, side, domains, left, right, beside):
    lanes = iota(1)
    d = [domains[side, n] for n in range(10)]
    thrust = look_up(table, index_of(domains[side, 10]))
    parts = [d[RHO] * h for h in shapes(d[VX] - thrust)]
    along_y, along_z = shapes(d[VY]), shapes(d[VZ])
    n = 2 * len(X_FIELDS) + 2 + side
    outer = {}
    for a, message in ((2, left), (0, right)):
        fields = row_blocks(message[n], 8)
        outer[a] = entering(table, fields[:7], index_of(fields[7]), a)
    into, new = {}, {}
    for a in range(3):
        for b in range(3):
            for c in range(3):
                value = slot_value(d, parts, along_y, along_z, a, b, c)
                value = shift_rows(value, a, outer[2][b, c], outer[0][b, c])
                value = roll(value, b - 1, 1)
                if b == 2 - 2 * side:
                    into[a, c] = value
                slot = 3 * a + b
                if c == 2:
                    value = jnp.where(lanes < 16, roll(beside[side, 0], -8 * slot, 1), roll(value, 16, 1))
                elif c == 0:
                    value = jnp.where(lanes >= 112, roll(beside[side, 1], 112 - 8 * slot, 1), roll(value, -16, 1))
                new[a, b, c] = value
    return into, new


def last_columns(table, strip, left, right):
    even = (iota(1) & 1) == 0
    sign = jnp.where(even, 0.25, -0.25)

    def slots_of(fields, wanted):
        rho, vx, vy, vz, dyy, dxy, dyz, mark = fields
        along_x, along_y, along_z = shapes(vx - look_up(table, index_of(mark))), shapes(vy), shapes(vz)
        part = rho * jnp.where(even, along_y[2], along_y[0])
        slots = {}
        for a in wanted:
            piece = part * along_x[a]
            for c in range(3):
                value = piece * along_z[c]
                if a == 1 and c == 1:
                    value = value + 0.5 * dyy
                elif c == 1:
                    value = value + ((a - 1) * sign) * dxy
                elif a == 1:
                    value = value + ((c - 1) * sign) * dyz
                slots[a, c] = value
        return slots

    n = 2 * len(X_FIELDS)
    columns = slots_of([strip[k] for k in range(8)], (0, 1, 2))
    before = slots_of(row_blocks(left[n], 8), (2,))
    after = slots_of(row_blocks(right[n], 8), (0,))
    for c in range(3):
        columns[2, c] = shift_rows(columns[2, c], 2, before[2, c], None)
        columns[0, c] = shift_rows(columns[0, c], 0, None, after[0, c])
    return columns


def stream(table, state, labels, columns, left, right, left_marks, right_marks, bottom, top, out, ghost, whole=None):
    lanes = iota(1)
    for side, (source, marks) in enumerate(((left, left_marks), (right, right_marks))):
        a = 2 - 2 * side
        for j in range(2):
            fields = [source[2 * n + j] for n in range(len(X_FIELDS))]
            for (b, c), value in entering(table, fields, marks(j), a).items():
                ghost[side, 3 * b + c, j] = value

    for a in range(3):
        for b in range(3):
            out[9 * a + 3 * b + 2, 0] = bottom[3 * a + b]
            out[9 * a + 3 * b, LEVELS - 1] = top[3 * a + b]

    for z in range(LEVELS):
        tiles = []
        for j in range(2):
            fields = [state[index, j, 8 * z : 8 * z + 8, :] for index in range(10)]
            thrust = look_up(table, labels[j, 8 * z : 8 * z + 8, :])
            parts = [fields[RHO] * h for h in shapes(fields[VX] - thrust)]
            tiles.append((fields, parts, shapes(fields[VY]), shapes(fields[VZ])))
        for c in range(3):
            level = z + c - 1
            if level < 0 or level >= LEVELS:
                continue
            for a in range(3):
                inflow = roll(columns[a, c], -16 * z - 8, 1)
                for b in range(3):
                    first, second = (
                        shift_rows(
                            slot_value(*tile, a, b, c),
                            a,
                            ghost[0, 3 * b + c, j, z : z + 1, :],
                            ghost[1, 3 * b + c, j, z : z + 1, :],
                        )
                        for j, tile in enumerate(tiles)
                    )
                    if b == 2:
                        first, second = roll(first, 1, 1), roll(second, 1, 1)
                        second = jnp.where(lanes == 0, first, second)
                        first = jnp.where(lanes == 0, inflow, first)
                    elif b == 0:
                        first, second = roll(first, -1, 1), roll(second, -1, 1)
                        first = jnp.where(lanes == 127, second, first)
                        second = jnp.where(lanes == 127, inflow, second)
                    out[9 * a + 3 * b + c, level, :, 0:128] = first
                    out[9 * a + 3 * b + c, level, :, 128:256] = second
        if whole and z:
            whole(z - 1)
    if whole:
        whole(LEVELS - 1)


def disk_table(sums, counts):
    disk = sums / jnp.maximum(counts, 1.0)
    return jnp.where(iota(1) < ROTORS, THRUST_GAIN * disk * jnp.abs(disk), 0.0)


def marks_of(message):
    return lambda j: message[2 * len(X_FIELDS) + j].astype(jnp.int32)


def middle_kernel(
    state, labels, domains, column_sums, beside, left, right, bottom, top,
    new_state, to_right, to_left, strip, counts, sums_out, f_ref, ghost,
):
    lanes = iota(1)
    even = (lanes & 1) == 0
    last = 2 * len(X_FIELDS) + 4
    totals = column_sums[...] + left[last] + right[last]
    seen = roll(totals, 64, 1)
    counts[...] = seen
    table = disk_table(totals, seen)

    marks, speeds, kept, columns = [], [], [], [{}, {}]
    for side in range(2):
        columns[side], new = step_domain(table, side, domains, left, right, beside)
        ux, fields = relax(low_moments(lambda a, b, c: new[a, b, c]))
        column = lanes & 15
        near = jnp.logical_and(column >= 8, column < 13) if side else jnp.logical_and(column >= 3, column < 8)
        mark = domains[side, 10]
        marks.append(jnp.where(near, index_of(mark), EMPTY))
        speeds.append(ux)
        kept.append([fields[n] for n in Y_FIELDS] + [mark])
    strips = [jnp.where(even, roll(one, 1, 1), roll(other, -1, 1)) for one, other in zip(*kept)]
    for n, block in enumerate(strips):
        strip[n] = block
    merged = {key: jnp.where(even, columns[0][key], columns[1][key]) for key in columns[0]}
    stream(table, state, labels, merged, left, right, marks_of(left), marks_of(right), bottom, top, f_ref, ghost)

    def f(z, j, a, b, c):
        return f_ref[9 * a + 3 * b + c, z, :, 128 * j : 128 * j + 128]

    def label(z, j):
        return labels[j, 8 * z : 8 * z + 8, :]

    sums = collide(f, label, new_state, marks, speeds)
    sums_out[...] = sums
    for target, row in ((to_right, 7), (to_left, 0)):
        slot = edge_rows(new_state, target, row)
        target[slot] = rows_of(strips, row)
        target[slot + 1] = sums


def last_kernel(
    state, labels, strip, sums, counts, left, right, old_left, old_right, bottom, top, out_hbm, out, ghost, gone
):
    last = 2 * len(X_FIELDS) + 1
    totals = sums[...] + left[last] + right[last]
    table = disk_table(totals, counts[...])
    columns = last_columns(table, strip, left, right)
    copies = [pltpu.make_async_copy(out.at[:, z], out_hbm.at[:, z], gone.at[z]) for z in range(LEVELS)]
    stream(
        table, state, labels, columns, left, right, marks_of(old_left), marks_of(old_right), bottom, top, out, ghost,
        whole=lambda z: copies[z].start(),
    )
    for copy in copies:
        copy.wait()


def call(kernel, inputs, outputs, scratch=(), in_hbm=0, out_hbm=0, copies=0):
    inputs = [pltpu.with_memory_space_constraint(x, pltpu.HBM) if n < in_hbm else x for n, x in enumerate(inputs)]

    def specs(count, outside):
        return [pl.BlockSpec(memory_space=pltpu.HBM if n < outside else pltpu.VMEM) for n in range(count)]

    return pl.pallas_call(
        kernel,
        out_shape=[jax.ShapeDtypeStruct(shape, dtype) for shape, dtype in outputs],
        in_specs=specs(len(inputs), in_hbm),
        out_specs=specs(len(outputs), out_hbm),
        scratch_shapes=[pltpu.VMEM(shape, dtype) for shape, dtype in scratch]
        + ([pltpu.SemaphoreType.DMA((copies,))] if copies else []),
        compiler_params=pltpu.CompilerParams(vmem_limit_bytes=VMEM_LIMIT),
    )(*inputs)


def both_ways(upward, downward, axis):
    count = lax.axis_size(axis)
    return (
        lax.ppermute(upward, axis, [(i, (i + 1) % count) for i in range(count)]),
        lax.ppermute(downward, axis, [((i + 1) % count, i) for i in range(count)]),
    )


def swapped(even, odd, axis):
    count = lax.axis_size(axis)

    def pairs(start):
        there = [(i, (i + 1) % count) for i in range(start, count, 2)]
        return there + [(j, i) for i, j in there]

    return lax.ppermute(even, axis, pairs(0)), lax.ppermute(odd, axis, pairs(1))


def body(populations, bottom_in, top_in, turbine_mask, rotor_index):
    f32 = jnp.float32
    state_shape = ((10, 2, 64, 128), f32)
    one = ((8, 128), f32)
    ghost = ((2, 9, 2, 8, 128), f32)
    inflow = (bottom_in.shape, f32)
    cells = (turbine_mask.shape, jnp.int32)
    whole = (populations.shape, f32)
    n = 2 * len(X_FIELDS)

    def blocks(*count):
        return (count + (8, 128), f32)

    state, labels, edges, to_even, to_odd = call(
        first_kernel,
        (populations, turbine_mask, rotor_index, bottom_in, top_in),
        (state_shape, ((2, 64, 128), jnp.int32), blocks(12), blocks(9), blocks(9)),
        (whole, cells, cells, inflow, inflow),
        in_hbm=5,
        copies=LEVELS + 4,
    )
    even, odd = swapped(to_even, to_odd, "gy")
    domains, to_right, to_left, column_sums, beside = call(
        relay_kernel,
        (state, labels, edges, even, odd),
        (blocks(2, 11), blocks(n + 5), blocks(n + 5), one, blocks(2, 2)),
    )
    old_left, old_right = both_ways(to_right, to_left, "gx")
    state, to_right, to_left, strip, counts, sums = call(
        middle_kernel,
        (state, labels, domains, column_sums, beside, old_left, old_right, bottom_in, top_in),
        (state_shape, blocks(n + 2), blocks(n + 2), blocks(8), one, one),
        (whole, ghost),
    )
    left, right = both_ways(to_right, to_left, "gx")
    (out,) = call(
        last_kernel,
        (state, labels, strip, sums, counts, left, right, old_left, old_right, bottom_in, top_in),
        (whole,),
        (whole, ghost),
        out_hbm=1,
        copies=LEVELS,
    )
    return out


def solution(mesh):
    placed = (
        P(None, None, "gx", "gy"),
        P(None, "gx", "gy"),
        P(None, "gx", "gy"),
        P(None, "gx", "gy"),
        P(None, "gx", "gy"),
    )
    return jax.shard_map(
        body, mesh=mesh, in_specs=placed, out_specs=P(None, None, "gx", "gy"), check_vma=False
    )
```

```python
import functools

import jax
import jax.numpy as jnp
from jax import lax
from jax.experimental import pallas as pl
from jax.experimental.pallas import tpu as pltpu
from jax.sharding import PartitionSpec as P

ROTORS = 64
SOUND = 1.0 / 3.0
TAU_BASE = 0.52
SMAG_GAIN = 5.0
CORIOLIS = 0.05
GEO_U = 0.08
THRUST_GAIN = 4.0
EMPTY = 127
LEVELS = 8
VMEM_LIMIT = 48 * 1024 * 1024

RHO, VX, VY, VZ, DXX, DYY, DZZ, DXY, DXZ, DYZ = range(10)
SPEED = 10
LABEL = 10
SPAN = 5
X_FIELDS = (RHO, VX, VY, VZ, DXX, DXY, DXZ)
Y_FIELDS = (RHO, VX, VY, VZ, DYY, DXY, DYZ)


def iota(axis):
    return lax.broadcasted_iota(jnp.int32, (8, 128), axis)


def roll(block, shift, axis):
    size = block.shape[axis]
    return pltpu.roll(block, shift % size, axis) if shift % size else block


def low_moments(f):
    along_z = {}
    for a in range(3):
        for b in range(3):
            low, mid, high = f(a, b, 0), f(a, b, 1), f(a, b, 2)
            ends = low + high
            along_z[a, b] = (ends + mid, high - low, ends)
    slabs = []
    for a in range(3):
        (l0, l1, l2), (m0, m1, m2), (h0, h1, h2) = (along_z[a, b] for b in range(3))
        ends = l0 + h0
        slabs.append((ends + m0, h0 - l0, ends, l1 + m1 + h1, h1 - l1, l2 + m2 + h2))
    low, mid, high = slabs
    ends = low[0] + high[0]
    return {
        "0": ends + mid[0],
        "x": high[0] - low[0],
        "xx": ends,
        "y": low[1] + mid[1] + high[1],
        "xy": high[1] - low[1],
        "yy": low[2] + mid[2] + high[2],
        "z": low[3] + mid[3] + high[3],
        "xz": high[3] - low[3],
        "yz": low[4] + mid[4] + high[4],
        "zz": low[5] + mid[5] + high[5],
    }


def relax(m):
    rho = m["0"]
    inverse = 1.0 / rho
    ux, uy, uz = m["x"] * inverse, m["y"] * inverse, m["z"] * inverse
    third = rho * SOUND
    qxx = m["xx"] - (m["x"] * ux + third)
    qyy = m["yy"] - (m["y"] * uy + third)
    qzz = m["zz"] - (m["z"] * uz + third)
    qxy = m["xy"] - m["x"] * uy
    qxz = m["xz"] - m["x"] * uz
    qyz = m["yz"] - m["y"] * uz
    strain = qxx * qxx + qyy * qyy + qzz * qzz + 2.0 * (qxy * qxy + qxz * qxz + qyz * qyz)
    keep = 1.0 - 1.0 / (TAU_BASE + SMAG_GAIN * jnp.sqrt(strain))
    vx = ux + CORIOLIS * uy
    vy = uy - CORIOLIS * (ux - GEO_U)
    fields = [rho, vx, vy, uz] + [keep * q for q in (qxx, qyy, qzz, qxy, qxz, qyz)]
    return ux, fields


def shapes(speed):
    square = speed * speed + SOUND
    return (0.5 * (square - speed), 1.0 - square, 0.5 * (square + speed))


def over_rows(block, join=jnp.add):
    for shift in (4, 2, 1):
        block = join(block, roll(block, shift, 0))
    return block


def spread(leaf, join=jnp.add):
    lanes = iota(1)

    def node(stride, index):
        if stride == 1:
            return leaf(index)
        half = stride // 2
        a, b = node(half, index), node(half, index + half)
        first = (lanes & half) == 0
        return join(jnp.where(first, a, b), roll(jnp.where(first, b, a), half, 1))

    return over_rows(node(128, 0), join)


def rotor_sums(labels, speeds):
    def leaf(index):
        rotor, counting = index % ROTORS, index >= ROTORS
        total = jnp.zeros((8, 128), jnp.float32)
        for label, speed in zip(labels, speeds):
            total = total + jnp.where(label == rotor, 1.0 if counting else speed, 0.0)
        return total

    return spread(leaf)


def take(block, index):
    return jnp.take_along_axis(block, index, axis=1, mode="promise_in_bounds")


def sums_kernel(state, labels, own_sums):
    places = [(j, z) for j in range(2) for z in range(LEVELS)]
    own_sums[...] = rotor_sums(
        [labels[j, 8 * z : 8 * z + 8, :] for j, z in places],
        [state[SPEED, j, 8 * z : 8 * z + 8, :] for j, z in places],
    )


def beside_tile(domains, n):
    return jnp.where((iota(1) & 8) == 0, domains[0, n], domains[1, n])


def places_kernel(labels, domains, starts, found, found_beside):
    lanes = iota(1)
    far = 1024.0
    column = lanes & 15
    near = jnp.logical_and(column >= 3, column < 13)
    outside = jnp.where(near, index_of(beside_tile(domains, LABEL)), EMPTY)
    inside = {(j, z): labels[j, 8 * z : 8 * z + 8, :] for j in range(2) for z in range(LEVELS)}

    def leaf(index):
        rotor = index % ROTORS
        if index >= ROTORS:
            return jnp.where(outside == rotor, column.astype(jnp.float32), far)
        first = jnp.full((8, 128), far, jnp.float32)
        for j in range(2):
            hit = inside[j, 0] == rotor
            for z in range(1, LEVELS):
                hit = jnp.logical_or(hit, inside[j, z] == rotor)
            first = jnp.minimum(first, jnp.where(hit, (lanes + 128 * j).astype(jnp.float32), far))
        return first

    both = spread(leaf, jnp.minimum)
    begin = (jnp.where(both < far, both, 0.0)).astype(jnp.int32)
    begin_beside = roll(begin.astype(jnp.float32), 64, 1).astype(jnp.int32)
    starts[0] = begin
    starts[1] = begin_beside
    own = jnp.where(lanes < ROTORS, lanes, -1)
    for k in range(SPAN):
        index = (begin + k) & 127
        for z in range(LEVELS):
            for j in range(2):
                found[k, j, z] = jnp.where(take(inside[j, z], index) == own, 1.0, 0.0)
            index_beside = (begin_beside + (k + 16 * z)) & 127
            found_beside[k, z] = jnp.where(take(outside, index_beside) == own, 1.0, 0.0)


def found_sums(speed, speed_beside, starts, found, found_beside):
    total = jnp.zeros((8, 128), jnp.float32)
    for k in range(SPAN):
        index = (starts[0] + k) & 127
        for z in range(LEVELS):
            for j in range(2):
                total = total + jnp.where(found[k, j, z] > 0.0, take(speed(z, j), index), 0.0)
            index_beside = (starts[1] + (k + 16 * z)) & 127
            total = total + jnp.where(found_beside[k, z] > 0.0, take(speed_beside, index_beside), 0.0)
    return over_rows(total)


def collide(f, state, keep_speed):
    for z in range(LEVELS):
        for j in range(2):
            ux, fields = relax(low_moments(functools.partial(f, z, j)))
            for index, value in enumerate(fields):
                state[index, j, 8 * z : 8 * z + 8, :] = value
            keep_speed(z, j, ux)


def first_kernel(
    f_hbm, mask_hbm, rotor_hbm, bottom_hbm, top_hbm, state, labels, edges, to_even, to_odd,
    f_ref, mask_ref, rotor_ref, bottom, top, arrived,
):
    lanes = iota(1)
    levels = [pltpu.make_async_copy(f_hbm.at[:, z], f_ref.at[:, z], arrived.at[z]) for z in range(LEVELS)]
    others = [
        pltpu.make_async_copy(source, target, arrived.at[LEVELS + n])
        for n, (source, target) in enumerate(
            ((mask_hbm, mask_ref), (rotor_hbm, rotor_ref), (bottom_hbm, bottom), (top_hbm, top))
        )
    ]
    for copy in [levels[0]] + others[:2] + levels[1:] + others[2:]:
        copy.start()
    others[0].wait()
    others[1].wait()
    waiting = list(levels)

    def f(z, j, a, b, c):
        if len(waiting) == LEVELS - z:
            waiting.pop(0).wait()
        return f_ref[9 * a + 3 * b + c, z, :, 128 * j : 128 * j + 128]

    def keep_speed(z, j, ux):
        here = (z, slice(None), slice(128 * j, 128 * j + 128))
        state[SPEED, j, 8 * z : 8 * z + 8, :] = ux
        labels[j, 8 * z : 8 * z + 8, :] = jnp.where(mask_ref[here] != 0, rotor_ref[here], EMPTY)

    collide(f, state, keep_speed)

    def edge(read):
        block = jnp.zeros((8, 128), jnp.float32)
        inner = block
        for z in range(LEVELS):
            moved = roll(jnp.where(lanes < 64, read(z, 0), read(z, 1)), 16 * z + 8, 1)
            block = jnp.where(lanes // 16 == z, moved, block)
            wanted = jnp.logical_or(((lanes - 16 * z + 2) & 127) < 2, ((lanes - 16 * z - 16) & 127) < 2)
            inner = jnp.where(wanted, moved, inner)
        return block, inner

    pairs = [edge(lambda z, j, n=n: state[n, j, 8 * z : 8 * z + 8, :]) for n in range(10)]
    pairs.append(edge(lambda z, j: labels[j, 8 * z : 8 * z + 8, :].astype(jnp.float32)))
    pairs.append(edge(lambda z, j: state[SPEED, j, 8 * z : 8 * z + 8, :]))
    blocks = [block for block, _ in pairs]
    inner_label, inner_speed = pairs[LABEL][1], pairs[LABEL + 1][1]
    for n, block in enumerate(blocks):
        edges[n] = block
    upward_first = lax.rem(lax.axis_index("gy"), 2) == 0
    low = (lanes & 8) == 0

    def send(n, upward, downward):
        to_even[n] = jnp.where(upward_first, upward, downward)
        to_odd[n] = jnp.where(upward_first, downward, upward)

    for n in range(6):
        one, other = blocks[2 * n], blocks[2 * n + 1]
        send(n, jnp.where(low, one, roll(other, 8, 1)), jnp.where(low, roll(other, -8, 1), one))
    column = lanes & 15
    send(
        6,
        jnp.where(column >= 14, inner_speed, jnp.where(column >= 12, roll(inner_label, -2, 1), float(EMPTY))),
        jnp.where(column < 2, inner_speed, jnp.where(column < 4, roll(inner_label, 2, 1), float(EMPTY))),
    )
    others[2].wait()
    others[3].wait()
    for place, source in ((7, bottom), (8, top)):
        upward = jnp.zeros((8, 128), jnp.float32)
        downward = upward
        for n in range(9):
            both = jnp.where(lanes < 64, source[n, :, 0:128], source[n, :, 128:256])
            moved = roll(both, 8 * n + 8, 1)
            upward = jnp.where(lanes // 8 == n, moved, upward)
            downward = jnp.where(lanes // 8 == n + 1, moved, downward)
        send(place, upward, downward)


def rows_of(blocks, row):
    rows = iota(0)
    out = jnp.broadcast_to(blocks[0][row : row + 1], (8, 128))
    for n in range(1, len(blocks)):
        out = jnp.where(rows == n, jnp.broadcast_to(blocks[n][row : row + 1], (8, 128)), out)
    return out


def edge_rows(state, target, row):
    slot = 0
    for index in X_FIELDS:
        for j in range(2):
            target[slot] = state[index, j, pl.ds(row, 8, stride=8), :]
            slot += 1
    return slot


def relay_kernel(state, labels, edges, own_sums, even, odd, domains, to_right, to_left, column_sums, beside):
    upward_first = lax.rem(lax.axis_index("gy"), 2) == 0
    below = [jnp.where(upward_first, odd[n], even[n]) for n in range(9)]
    above = [jnp.where(upward_first, even[n], odd[n]) for n in range(9)]
    for side, message in enumerate((below, above)):
        for n in range(2):
            beside[side, n] = message[7 + n]
    low = (iota(1) & 8) == 0
    for n in range(12):
        under, over = below[n // 2], above[n // 2]
        if n % 2:
            under, over = roll(under, -8, 1), roll(over, 8, 1)
        domains[0, n] = jnp.where(low, under, edges[n])
        domains[1, n] = jnp.where(low, edges[n], over)
    column = iota(1) & 15
    inner = jnp.where(
        column >= 14, roll(below[6], 2, 1), jnp.where(column < 2, roll(above[6], -2, 1), float(EMPTY))
    )
    sums = own_sums[...] + rotor_sums(
        [index_of(beside_tile(domains, LABEL)), index_of(inner)],
        [beside_tile(domains, LABEL + 1), jnp.where(column >= 8, below[6], above[6])],
    )
    column_sums[...] = sums
    for target, row in ((to_right, 7), (to_left, 0)):
        slot = edge_rows(state, target, row)
        for j in range(2):
            target[slot + j] = labels[j, pl.ds(row, 8, stride=8), :].astype(jnp.float32)
        for side in range(2):
            target[slot + 2 + side] = rows_of([domains[side, n] for n in X_FIELDS + (LABEL,)], row)
        target[slot + 4] = sums


look_up = take


def index_of(mark):
    return jnp.clip(mark, 0.0, float(EMPTY)).astype(jnp.int32)


def slot_value(d, parts, along_y, along_z, a, b, c):
    value = parts[a] * along_y[b] * along_z[c]
    ones = (a == 1) + (b == 1) + (c == 1)
    if ones == 3:
        return value - (d[DXX] + d[DYY] + d[DZZ])
    if ones == 2:
        return value + 0.5 * (d[DXX] if a != 1 else d[DYY] if b != 1 else d[DZZ])
    if ones == 1 and c == 1:
        return value + (0.25 * (a - 1) * (b - 1)) * d[DXY]
    if ones == 1 and b == 1:
        return value + (0.25 * (a - 1) * (c - 1)) * d[DXZ]
    if ones == 1:
        return value + (0.25 * (b - 1) * (c - 1)) * d[DYZ]
    return value


def entering(table, fields, mark, a):
    rho, vx, vy, vz, dxx, dxy, dxz = fields
    part = rho * shapes(vx - look_up(table, mark))[a]
    d = {DXX: dxx, DXY: dxy, DXZ: dxz}
    along_y, along_z = shapes(vy), shapes(vz)
    return {(b, c): slot_value(d, {a: part}, along_y, along_z, a, b, c) for b in range(3) for c in range(3)}


def shift_rows(value, a, before, after):
    if a == 2:
        return jnp.where(iota(0) == 0, before, roll(value, 1, 0))
    if a == 0:
        return jnp.where(iota(0) == 7, after, roll(value, -1, 0))
    return value


def row_blocks(block, count):
    return [jnp.broadcast_to(block[n : n + 1], (8, 128)) for n in range(count)]


def step_domain(table, side, domains, left, right, beside):
    lanes = iota(1)
    d = [domains[side, n] for n in range(10)]
    thrust = look_up(table, index_of(domains[side, LABEL]))
    parts = [d[RHO] * h for h in shapes(d[VX] - thrust)]
    along_y, along_z = shapes(d[VY]), shapes(d[VZ])
    n = 2 * len(X_FIELDS) + 2 + side
    outer = {}
    for a, message in ((2, left), (0, right)):
        fields = row_blocks(message[n], 8)
        outer[a] = entering(table, fields[:7], index_of(fields[7]), a)
    into, new = {}, {}
    for a in range(3):
        for b in range(3):
            for c in range(3):
                value = slot_value(d, parts, along_y, along_z, a, b, c)
                value = shift_rows(value, a, outer[2][b, c], outer[0][b, c])
                value = roll(value, b - 1, 1)
                if b == 2 - 2 * side:
                    into[a, c] = value
                slot = 3 * a + b
                if c == 2:
                    value = jnp.where(lanes < 16, roll(beside[side, 0], -8 * slot, 1), roll(value, 16, 1))
                elif c == 0:
                    value = jnp.where(lanes >= 112, roll(beside[side, 1], 112 - 8 * slot, 1), roll(value, -16, 1))
                new[a, b, c] = value
    return into, new


def last_columns(table, strip, left, right):
    even = (iota(1) & 1) == 0
    sign = jnp.where(even, 0.25, -0.25)

    def slots_of(fields, wanted):
        rho, vx, vy, vz, dyy, dxy, dyz, mark = fields
        along_x, along_y, along_z = shapes(vx - look_up(table, index_of(mark))), shapes(vy), shapes(vz)
        part = rho * jnp.where(even, along_y[2], along_y[0])
        slots = {}
        for a in wanted:
            piece = part * along_x[a]
            for c in range(3):
                value = piece * along_z[c]
                if a == 1 and c == 1:
                    value = value + 0.5 * dyy
                elif c == 1:
                    value = value + ((a - 1) * sign) * dxy
                elif a == 1:
                    value = value + ((c - 1) * sign) * dyz
                slots[a, c] = value
        return slots

    n = 2 * len(X_FIELDS)
    columns = slots_of([strip[k] for k in range(8)], (0, 1, 2))
    before = slots_of(row_blocks(left[n], 8), (2,))
    after = slots_of(row_blocks(right[n], 8), (0,))
    for c in range(3):
        columns[2, c] = shift_rows(columns[2, c], 2, before[2, c], None)
        columns[0, c] = shift_rows(columns[0, c], 0, None, after[0, c])
    return columns


def stream(table, state, labels, columns, left, right, left_marks, right_marks, bottom, top, out, ghost, whole=None):
    lanes = iota(1)
    for side, (source, marks) in enumerate(((left, left_marks), (right, right_marks))):
        a = 2 - 2 * side
        for j in range(2):
            fields = [source[2 * n + j] for n in range(len(X_FIELDS))]
            for (b, c), value in entering(table, fields, marks(j), a).items():
                ghost[side, 3 * b + c, j] = value

    for a in range(3):
        for b in range(3):
            out[9 * a + 3 * b + 2, 0] = bottom[3 * a + b]
            out[9 * a + 3 * b, LEVELS - 1] = top[3 * a + b]

    for z in range(LEVELS):
        tiles = []
        for j in range(2):
            fields = [state[index, j, 8 * z : 8 * z + 8, :] for index in range(10)]
            thrust = look_up(table, labels[j, 8 * z : 8 * z + 8, :])
            parts = [fields[RHO] * h for h in shapes(fields[VX] - thrust)]
            tiles.append((fields, parts, shapes(fields[VY]), shapes(fields[VZ])))
        for c in range(3):
            level = z + c - 1
            if level < 0 or level >= LEVELS:
                continue
            for a in range(3):
                inflow = roll(columns[a, c], -16 * z - 8, 1)
                for b in range(3):
                    first, second = (
                        shift_rows(
                            slot_value(*tile, a, b, c),
                            a,
                            ghost[0, 3 * b + c, j, z : z + 1, :],
                            ghost[1, 3 * b + c, j, z : z + 1, :],
                        )
                        for j, tile in enumerate(tiles)
                    )
                    if b == 2:
                        first, second = roll(first, 1, 1), roll(second, 1, 1)
                        second = jnp.where(lanes == 0, first, second)
                        first = jnp.where(lanes == 0, inflow, first)
                    elif b == 0:
                        first, second = roll(first, -1, 1), roll(second, -1, 1)
                        first = jnp.where(lanes == 127, second, first)
                        second = jnp.where(lanes == 127, inflow, second)
                    out[9 * a + 3 * b + c, level, :, 0:128] = first
                    out[9 * a + 3 * b + c, level, :, 128:256] = second
        if whole and z:
            whole(z - 1)
    if whole:
        whole(LEVELS - 1)


def disk_table(sums, counts):
    disk = sums / jnp.maximum(counts, 1.0)
    return jnp.where(iota(1) < ROTORS, THRUST_GAIN * disk * jnp.abs(disk), 0.0)


def marks_of(message):
    return lambda j: message[2 * len(X_FIELDS) + j].astype(jnp.int32)


def middle_kernel(
    state, labels, domains, column_sums, beside, starts, found, found_beside, left, right, bottom, top,
    new_state, to_right, to_left, strip, counts, sums_out, f_ref, ghost, speeds,
):
    lanes = iota(1)
    even = (lanes & 1) == 0
    last = 2 * len(X_FIELDS) + 4
    totals = column_sums[...] + left[last] + right[last]
    seen = roll(totals, 64, 1)
    counts[...] = seen
    table = disk_table(totals, seen)

    outside, kept, columns = [], [], [{}, {}]
    for side in range(2):
        columns[side], new = step_domain(table, side, domains, left, right, beside)
        ux, fields = relax(low_moments(lambda a, b, c: new[a, b, c]))
        outside.append(ux)
        kept.append([fields[n] for n in Y_FIELDS] + [domains[side, LABEL]])
    strips = [jnp.where(even, roll(one, 1, 1), roll(other, -1, 1)) for one, other in zip(*kept)]
    for n, block in enumerate(strips):
        strip[n] = block
    merged = {key: jnp.where(even, columns[0][key], columns[1][key]) for key in columns[0]}
    stream(table, state, labels, merged, left, right, marks_of(left), marks_of(right), bottom, top, f_ref, ghost)

    def f(z, j, a, b, c):
        return f_ref[9 * a + 3 * b + c, z, :, 128 * j : 128 * j + 128]

    def keep_speed(z, j, ux):
        speeds[j, z] = ux

    collide(f, new_state, keep_speed)
    sums = found_sums(
        lambda z, j: speeds[j, z],
        jnp.where((lanes & 8) == 0, outside[0], outside[1]),
        starts, found, found_beside,
    )
    sums_out[...] = sums
    for target, row in ((to_right, 7), (to_left, 0)):
        slot = edge_rows(new_state, target, row)
        target[slot] = rows_of(strips, row)
        target[slot + 1] = sums


def last_kernel(
    state, labels, strip, sums, counts, left, right, old_left, old_right, bottom, top, out_hbm, out, ghost, gone
):
    last = 2 * len(X_FIELDS) + 1
    totals = sums[...] + left[last] + right[last]
    table = disk_table(totals, counts[...])
    columns = last_columns(table, strip, left, right)
    copies = [pltpu.make_async_copy(out.at[:, z], out_hbm.at[:, z], gone.at[z]) for z in range(LEVELS)]
    stream(
        table, state, labels, columns, left, right, marks_of(old_left), marks_of(old_right), bottom, top, out, ghost,
        whole=lambda z: copies[z].start(),
    )
    for copy in copies:
        copy.wait()


def call(kernel, inputs, outputs, scratch=(), in_hbm=0, out_hbm=0, copies=0):
    inputs = [pltpu.with_memory_space_constraint(x, pltpu.HBM) if n < in_hbm else x for n, x in enumerate(inputs)]

    def specs(count, outside):
        return [pl.BlockSpec(memory_space=pltpu.HBM if n < outside else pltpu.VMEM) for n in range(count)]

    return pl.pallas_call(
        kernel,
        out_shape=[jax.ShapeDtypeStruct(shape, dtype) for shape, dtype in outputs],
        in_specs=specs(len(inputs), in_hbm),
        out_specs=specs(len(outputs), out_hbm),
        scratch_shapes=[pltpu.VMEM(shape, dtype) for shape, dtype in scratch]
        + ([pltpu.SemaphoreType.DMA((copies,))] if copies else []),
        compiler_params=pltpu.CompilerParams(vmem_limit_bytes=VMEM_LIMIT),
    )(*inputs)


def both_ways(upward, downward, axis):
    count = lax.axis_size(axis)
    return (
        lax.ppermute(upward, axis, [(i, (i + 1) % count) for i in range(count)]),
        lax.ppermute(downward, axis, [((i + 1) % count, i) for i in range(count)]),
    )


def swapped(even, odd, axis):
    count = lax.axis_size(axis)

    def pairs(start):
        there = [(i, (i + 1) % count) for i in range(start, count, 2)]
        return there + [(j, i) for i, j in there]

    return lax.ppermute(even, axis, pairs(0)), lax.ppermute(odd, axis, pairs(1))


def body(populations, bottom_in, top_in, turbine_mask, rotor_index):
    f32 = jnp.float32
    state_shape = ((10, 2, 64, 128), f32)
    one = ((8, 128), f32)
    ghost = ((2, 9, 2, 8, 128), f32)
    inflow = (bottom_in.shape, f32)
    cells = (turbine_mask.shape, jnp.int32)
    whole = (populations.shape, f32)
    n = 2 * len(X_FIELDS)

    def blocks(*count):
        return (count + (8, 128), f32)

    state, labels, edges, to_even, to_odd = call(
        first_kernel,
        (populations, turbine_mask, rotor_index, bottom_in, top_in),
        (((11, 2, 64, 128), f32), ((2, 64, 128), jnp.int32), blocks(12), blocks(9), blocks(9)),
        (whole, cells, cells, inflow, inflow),
        in_hbm=5,
        copies=LEVELS + 4,
    )
    even, odd = swapped(to_even, to_odd, "gy")
    (own_sums,) = call(sums_kernel, (state, labels), (one,))
    domains, to_right, to_left, column_sums, beside = call(
        relay_kernel,
        (state, labels, edges, own_sums, even, odd),
        (blocks(2, 12), blocks(n + 5), blocks(n + 5), one, blocks(2, 2)),
    )
    old_left, old_right = both_ways(to_right, to_left, "gx")
    starts, found, found_beside = call(
        places_kernel,
        (labels, domains),
        (((2, 8, 128), jnp.int32), blocks(SPAN, 2, LEVELS), blocks(SPAN, LEVELS)),
    )
    state, to_right, to_left, strip, counts, sums = call(
        middle_kernel,
        (
            state, labels, domains, column_sums, beside, starts, found, found_beside,
            old_left, old_right, bottom_in, top_in,
        ),
        (state_shape, blocks(n + 2), blocks(n + 2), blocks(8), one, one),
        (whole, ghost, blocks(2, LEVELS)),
    )
    left, right = both_ways(to_right, to_left, "gx")
    (out,) = call(
        last_kernel,
        (state, labels, strip, sums, counts, left, right, old_left, old_right, bottom_in, top_in),
        (whole,),
        (whole, ghost),
        out_hbm=1,
        copies=LEVELS,
    )
    return out


def solution(mesh):
    placed = (
        P(None, None, "gx", "gy"),
        P(None, "gx", "gy"),
        P(None, "gx", "gy"),
        P(None, "gx", "gy"),
        P(None, "gx", "gy"),
    )
    return jax.shard_map(
        body, mesh=mesh, in_specs=placed, out_specs=P(None, None, "gx", "gy"), check_vma=False
    )
```

```python
import functools

import jax
import jax.numpy as jnp
from jax import lax
from jax.experimental import pallas as pl
from jax.experimental.pallas import tpu as pltpu
from jax.sharding import PartitionSpec as P

ROTORS = 64
SOUND = 1.0 / 3.0
TAU_BASE = 0.52
SMAG_GAIN = 5.0
CORIOLIS = 0.05
GEO_U = 0.08
THRUST_GAIN = 4.0
EMPTY = 127
LEVELS = 8
VMEM_LIMIT = 24 * 1024 * 1024

RHO, VX, VY, VZ, DXX, DYY, DZZ, DXY, DXZ, DYZ = range(10)
SPEED = 10
LABEL = 10
SPAN = 5
X_FIELDS = (RHO, VX, VY, VZ, DXX, DXY, DXZ)
Y_FIELDS = (RHO, VX, VY, VZ, DYY, DXY, DYZ)


def iota(axis):
    return lax.broadcasted_iota(jnp.int32, (8, 128), axis)


def roll(block, shift, axis):
    size = block.shape[axis]
    return pltpu.roll(block, shift % size, axis) if shift % size else block


def low_moments(f):
    along_z = {}
    for a in range(3):
        for b in range(3):
            low, mid, high = f(a, b, 0), f(a, b, 1), f(a, b, 2)
            ends = low + high
            along_z[a, b] = (ends + mid, high - low, ends)
    slabs = []
    for a in range(3):
        (l0, l1, l2), (m0, m1, m2), (h0, h1, h2) = (along_z[a, b] for b in range(3))
        ends = l0 + h0
        slabs.append((ends + m0, h0 - l0, ends, l1 + m1 + h1, h1 - l1, l2 + m2 + h2))
    low, mid, high = slabs
    ends = low[0] + high[0]
    return {
        "0": ends + mid[0],
        "x": high[0] - low[0],
        "xx": ends,
        "y": low[1] + mid[1] + high[1],
        "xy": high[1] - low[1],
        "yy": low[2] + mid[2] + high[2],
        "z": low[3] + mid[3] + high[3],
        "xz": high[3] - low[3],
        "yz": low[4] + mid[4] + high[4],
        "zz": low[5] + mid[5] + high[5],
    }


def relax(m):
    rho = m["0"]
    inverse = 1.0 / rho
    ux, uy, uz = m["x"] * inverse, m["y"] * inverse, m["z"] * inverse
    third = rho * SOUND
    qxx = m["xx"] - (m["x"] * ux + third)
    qyy = m["yy"] - (m["y"] * uy + third)
    qzz = m["zz"] - (m["z"] * uz + third)
    qxy = m["xy"] - m["x"] * uy
    qxz = m["xz"] - m["x"] * uz
    qyz = m["yz"] - m["y"] * uz
    strain = qxx * qxx + qyy * qyy + qzz * qzz + 2.0 * (qxy * qxy + qxz * qxz + qyz * qyz)
    keep = 1.0 - 1.0 / (TAU_BASE + SMAG_GAIN * jnp.sqrt(strain))
    vx = ux + CORIOLIS * uy
    vy = uy - CORIOLIS * (ux - GEO_U)
    fields = [rho, vx, vy, uz] + [keep * q for q in (qxx, qyy, qzz, qxy, qxz, qyz)]
    return ux, fields


def shapes(speed):
    square = speed * speed + SOUND
    return (0.5 * (square - speed), 1.0 - square, 0.5 * (square + speed))


def over_rows(block, join=jnp.add):
    for shift in (4, 2, 1):
        block = join(block, roll(block, shift, 0))
    return block


def spread(leaf, join=jnp.add):
    lanes = iota(1)

    def node(stride, ways, rest, index):
        parts = [(node(*rest, index + d * stride) if rest else leaf(index + d * stride)) for d in range(ways)]
        digit = (lanes // stride) % ways
        moved = []
        for k in range(ways):
            picked = parts[k]
            for d in range(1, ways):
                picked = jnp.where(digit == d, parts[(d + k) % ways], picked)
            moved.append(roll(picked, k * stride, 1))
        return functools.reduce(join, moved)

    return over_rows(node(16, 8, (2, 8, (1, 2, ())), 0), join)


def rotor_sums(labels, speeds):
    def leaf(index):
        rotor, counting = index % ROTORS, index >= ROTORS
        total = jnp.zeros((8, 128), jnp.float32)
        for label, speed in zip(labels, speeds):
            total = total + jnp.where(label == rotor, 1.0 if counting else speed, 0.0)
        return total

    return spread(leaf)


def take(block, index):
    return jnp.take_along_axis(block, index, axis=1, mode="promise_in_bounds")


def sums_kernel(state, labels, own_sums):
    places = [(j, z) for j in range(2) for z in range(LEVELS)]
    own_sums[...] = rotor_sums(
        [labels[j, 8 * z : 8 * z + 8, :] for j, z in places],
        [state[SPEED, j, 8 * z : 8 * z + 8, :] for j, z in places],
    )


def beside_tile(domains, n):
    return jnp.where((iota(1) & 8) == 0, domains[0, n], domains[1, n])


def places_kernel(labels, domains, starts, found, found_beside):
    lanes = iota(1)
    far = 1024.0
    column = lanes & 15
    near = jnp.logical_and(column >= 3, column < 13)
    outside = jnp.where(near, index_of(beside_tile(domains, LABEL)), EMPTY)
    inside = {(j, z): labels[j, 8 * z : 8 * z + 8, :] for j in range(2) for z in range(LEVELS)}

    def leaf(index):
        rotor = index % ROTORS
        if index >= ROTORS:
            return jnp.where(outside == rotor, column.astype(jnp.float32), far)
        first = jnp.full((8, 128), far, jnp.float32)
        for j in range(2):
            hit = inside[j, 0] == rotor
            for z in range(1, LEVELS):
                hit = jnp.logical_or(hit, inside[j, z] == rotor)
            first = jnp.minimum(first, jnp.where(hit, (lanes + 128 * j).astype(jnp.float32), far))
        return first

    both = spread(leaf, jnp.minimum)
    begin = (jnp.where(both < far, both, 0.0)).astype(jnp.int32)
    begin_beside = roll(begin.astype(jnp.float32), 64, 1).astype(jnp.int32)
    starts[0] = begin
    starts[1] = begin_beside
    own = jnp.where(lanes < ROTORS, lanes, -1)
    for k in range(SPAN):
        index = (begin + k) & 127
        for z in range(LEVELS):
            for j in range(2):
                found[k, j, z] = jnp.where(take(inside[j, z], index) == own, 1.0, 0.0)
            index_beside = (begin_beside + (k + 16 * z)) & 127
            found_beside[k, z] = jnp.where(take(outside, index_beside) == own, 1.0, 0.0)


def found_sums(speed, speed_beside, starts, found, found_beside):
    total = jnp.zeros((8, 128), jnp.float32)
    for k in range(SPAN):
        index = (starts[0] + k) & 127
        for z in range(LEVELS):
            for j in range(2):
                total = total + jnp.where(found[k, j, z] > 0.0, take(speed(z, j), index), 0.0)
            index_beside = (starts[1] + (k + 16 * z)) & 127
            total = total + jnp.where(found_beside[k, z] > 0.0, take(speed_beside, index_beside), 0.0)
    return over_rows(total)


def collide(f, state, keep_speed):
    for z in range(LEVELS):
        for j in range(2):
            ux, fields = relax(low_moments(functools.partial(f, z, j)))
            for index, value in enumerate(fields):
                state[index, j, 8 * z : 8 * z + 8, :] = value
            keep_speed(z, j, ux)


def first_kernel(
    f_hbm, mask_hbm, rotor_hbm, bottom_hbm, top_hbm, state, labels, edges, to_even, to_odd,
    f_ref, mask_ref, rotor_ref, bottom, top, arrived,
):
    lanes = iota(1)
    levels = [pltpu.make_async_copy(f_hbm.at[:, z], f_ref.at[:, z], arrived.at[z]) for z in range(LEVELS)]
    others = [
        pltpu.make_async_copy(source, target, arrived.at[LEVELS + n])
        for n, (source, target) in enumerate(
            ((mask_hbm, mask_ref), (rotor_hbm, rotor_ref), (bottom_hbm, bottom), (top_hbm, top))
        )
    ]
    for copy in [levels[0]] + others[:2] + levels[1:] + others[2:]:
        copy.start()
    others[0].wait()
    others[1].wait()
    waiting = list(levels)

    def f(z, j, a, b, c):
        if len(waiting) == LEVELS - z:
            waiting.pop(0).wait()
        return f_ref[9 * a + 3 * b + c, z, :, 128 * j : 128 * j + 128]

    def keep_speed(z, j, ux):
        here = (z, slice(None), slice(128 * j, 128 * j + 128))
        state[SPEED, j, 8 * z : 8 * z + 8, :] = ux
        labels[j, 8 * z : 8 * z + 8, :] = jnp.where(mask_ref[here] != 0, rotor_ref[here], EMPTY)

    collide(f, state, keep_speed)

    def edge(read):
        block = jnp.zeros((8, 128), jnp.float32)
        inner = block
        for z in range(LEVELS):
            moved = roll(jnp.where(lanes < 64, read(z, 0), read(z, 1)), 16 * z + 8, 1)
            block = jnp.where(lanes // 16 == z, moved, block)
            wanted = jnp.logical_or(((lanes - 16 * z + 2) & 127) < 2, ((lanes - 16 * z - 16) & 127) < 2)
            inner = jnp.where(wanted, moved, inner)
        return block, inner

    pairs = [edge(lambda z, j, n=n: state[n, j, 8 * z : 8 * z + 8, :]) for n in range(10)]
    pairs.append(edge(lambda z, j: labels[j, 8 * z : 8 * z + 8, :].astype(jnp.float32)))
    pairs.append(edge(lambda z, j: state[SPEED, j, 8 * z : 8 * z + 8, :]))
    blocks = [block for block, _ in pairs]
    inner_label, inner_speed = pairs[LABEL][1], pairs[LABEL + 1][1]
    for n, block in enumerate(blocks):
        edges[n] = block
    upward_first = lax.rem(lax.axis_index("gy"), 2) == 0
    low = (lanes & 8) == 0

    def send(n, upward, downward):
        to_even[n] = jnp.where(upward_first, upward, downward)
        to_odd[n] = jnp.where(upward_first, downward, upward)

    for n in range(6):
        one, other = blocks[2 * n], blocks[2 * n + 1]
        send(n, jnp.where(low, one, roll(other, 8, 1)), jnp.where(low, roll(other, -8, 1), one))
    column = lanes & 15
    send(
        6,
        jnp.where(column >= 14, inner_speed, jnp.where(column >= 12, roll(inner_label, -2, 1), float(EMPTY))),
        jnp.where(column < 2, inner_speed, jnp.where(column < 4, roll(inner_label, 2, 1), float(EMPTY))),
    )
    others[2].wait()
    others[3].wait()
    for place, source in ((7, bottom), (8, top)):
        upward = jnp.zeros((8, 128), jnp.float32)
        downward = upward
        for n in range(9):
            both = jnp.where(lanes < 64, source[n, :, 0:128], source[n, :, 128:256])
            moved = roll(both, 8 * n + 8, 1)
            upward = jnp.where(lanes // 8 == n, moved, upward)
            downward = jnp.where(lanes // 8 == n + 1, moved, downward)
        send(place, upward, downward)


def rows_of(blocks, row):
    rows = iota(0)
    out = jnp.broadcast_to(blocks[0][row : row + 1], (8, 128))
    for n in range(1, len(blocks)):
        out = jnp.where(rows == n, jnp.broadcast_to(blocks[n][row : row + 1], (8, 128)), out)
    return out


def edge_rows(state, target, row):
    slot = 0
    for index in X_FIELDS:
        for j in range(2):
            target[slot] = state[index, j, pl.ds(row, 8, stride=8), :]
            slot += 1
    return slot


def relay_kernel(state, labels, edges, own_sums, even, odd, domains, to_right, to_left, column_sums, beside):
    upward_first = lax.rem(lax.axis_index("gy"), 2) == 0
    below = [jnp.where(upward_first, odd[n], even[n]) for n in range(9)]
    above = [jnp.where(upward_first, even[n], odd[n]) for n in range(9)]
    for side, message in enumerate((below, above)):
        for n in range(2):
            beside[side, n] = message[7 + n]
    low = (iota(1) & 8) == 0
    for n in range(12):
        under, over = below[n // 2], above[n // 2]
        if n % 2:
            under, over = roll(under, -8, 1), roll(over, 8, 1)
        domains[0, n] = jnp.where(low, under, edges[n])
        domains[1, n] = jnp.where(low, edges[n], over)
    column = iota(1) & 15
    inner = jnp.where(
        column >= 14, roll(below[6], 2, 1), jnp.where(column < 2, roll(above[6], -2, 1), float(EMPTY))
    )
    sums = own_sums[...] + rotor_sums(
        [index_of(beside_tile(domains, LABEL)), index_of(inner)],
        [beside_tile(domains, LABEL + 1), jnp.where(column >= 8, below[6], above[6])],
    )
    column_sums[...] = sums
    for target, row in ((to_right, 7), (to_left, 0)):
        slot = edge_rows(state, target, row)
        for j in range(2):
            target[slot + j] = labels[j, pl.ds(row, 8, stride=8), :].astype(jnp.float32)
        for side in range(2):
            target[slot + 2 + side] = rows_of([domains[side, n] for n in X_FIELDS + (LABEL,)], row)
        target[slot + 4] = sums


look_up = take


def index_of(mark):
    return jnp.clip(mark, 0.0, float(EMPTY)).astype(jnp.int32)


def slot_value(d, parts, along_y, along_z, a, b, c):
    value = parts[a] * along_y[b] * along_z[c]
    ones = (a == 1) + (b == 1) + (c == 1)
    if ones == 3:
        return value - (d[DXX] + d[DYY] + d[DZZ])
    if ones == 2:
        return value + 0.5 * (d[DXX] if a != 1 else d[DYY] if b != 1 else d[DZZ])
    if ones == 1 and c == 1:
        return value + (0.25 * (a - 1) * (b - 1)) * d[DXY]
    if ones == 1 and b == 1:
        return value + (0.25 * (a - 1) * (c - 1)) * d[DXZ]
    if ones == 1:
        return value + (0.25 * (b - 1) * (c - 1)) * d[DYZ]
    return value


def entering(table, fields, mark, a):
    rho, vx, vy, vz, dxx, dxy, dxz = fields
    part = rho * shapes(vx - look_up(table, mark))[a]
    d = {DXX: dxx, DXY: dxy, DXZ: dxz}
    along_y, along_z = shapes(vy), shapes(vz)
    return {(b, c): slot_value(d, {a: part}, along_y, along_z, a, b, c) for b in range(3) for c in range(3)}


def shift_rows(value, a, before, after):
    if a == 2:
        return jnp.where(iota(0) == 0, before, roll(value, 1, 0))
    if a == 0:
        return jnp.where(iota(0) == 7, after, roll(value, -1, 0))
    return value


def row_blocks(block, count):
    return [jnp.broadcast_to(block[n : n + 1], (8, 128)) for n in range(count)]


def step_domain(table, side, domains, left, right, beside):
    lanes = iota(1)
    d = [domains[side, n] for n in range(10)]
    thrust = look_up(table, index_of(domains[side, LABEL]))
    parts = [d[RHO] * h for h in shapes(d[VX] - thrust)]
    along_y, along_z = shapes(d[VY]), shapes(d[VZ])
    n = 2 * len(X_FIELDS) + 2 + side
    outer = {}
    for a, message in ((2, left), (0, right)):
        fields = row_blocks(message[n], 8)
        outer[a] = entering(table, fields[:7], index_of(fields[7]), a)
    new = {}
    for a in range(3):
        for b in range(3):
            for c in range(3):
                value = slot_value(d, parts, along_y, along_z, a, b, c)
                value = shift_rows(value, a, outer[2][b, c], outer[0][b, c])
                value = roll(value, b - 1, 1)
                slot = 3 * a + b
                if c == 2:
                    value = jnp.where(lanes < 16, roll(beside[side, 0], -8 * slot, 1), roll(value, 16, 1))
                elif c == 0:
                    value = jnp.where(lanes >= 112, roll(beside[side, 1], 112 - 8 * slot, 1), roll(value, -16, 1))
                new[a, b, c] = value
    return outer, new


def strip_corners(table, message, a):
    even = (iota(1) & 1) == 0
    rho, vx, vy, vz, _, dxy, _, mark = row_blocks(message[2 * len(X_FIELDS)], 8)
    along_y, along_z = shapes(vy), shapes(vz)
    part = rho * shapes(vx - look_up(table, index_of(mark)))[a] * jnp.where(even, along_y[2], along_y[0])
    slots = [part * along_z[c] for c in range(3)]
    slots[1] = slots[1] + ((a - 1) * jnp.where(even, 0.25, -0.25)) * dxy
    return slots


def merged_strip(left_end, right_end):
    return jnp.where((iota(1) & 1) == 0, roll(left_end, 1, 1), roll(right_end, -1, 1))


def shift_columns(first, second, b, inflow):
    lanes = iota(1)
    if b == 2:
        first, second = roll(first, 1, 1), roll(second, 1, 1)
        return jnp.where(lanes == 0, inflow, first), jnp.where(lanes == 0, first, second)
    if b == 0:
        first, second = roll(first, -1, 1), roll(second, -1, 1)
        return jnp.where(lanes == 127, second, first), jnp.where(lanes == 127, inflow, second)
    return first, second


def prepare(state, labels, strip, moved, moved_labels):
    even = (iota(1) & 1) == 0
    rho, vx, vy, vz, dyy, dxy, dyz, mark = strip
    sign = jnp.where(even, 0.25, -0.25)
    along_y, along_z = shapes(vy), shapes(vz)
    part = rho * jnp.where(even, along_y[2], along_y[0])
    outside = [vx] + [part * h for h in along_z] + [0.5 * dyy, sign * dyz, sign * dxy, mark]
    for z in range(LEVELS):
        inflow = [roll(block, -16 * z - 8, 1) for block in outside]
        tiles = []
        for j in range(2):
            d = [state[n, j, 8 * z : 8 * z + 8, :] for n in range(10)]
            mark = labels[j, 8 * z : 8 * z + 8, :].astype(jnp.float32)
            along_y, along_z = shapes(d[VY]), shapes(d[VZ])
            rows = [d[RHO] * h for h in along_y]
            tiles.append((d, mark, rows, along_z))
        for b in range(3):
            kept = []
            for d, mark, rows, along_z in tiles:
                if b == 1:
                    terms = [-(d[DXX] + d[DYY] + d[DZZ]), 0.5 * d[DZZ], 0.5 * d[DXX], mark, 0.25 * d[DXZ]]
                else:
                    terms = [0.5 * d[DYY], (0.25 * (b - 1)) * d[DYZ], (0.25 * (b - 1)) * d[DXY], mark]
                kept.append([d[VX]] + [rows[b] * h for h in along_z] + terms)
            if b != 1:
                pairs = [shift_columns(*pair) for pair in zip(*kept, [b] * 8, inflow)]
                kept = list(zip(*pairs))
            for j, fields in enumerate(kept):
                for a in range(3):
                    place = 3 * a + b
                    chosen = list(fields[:4])
                    if a == 1:
                        chosen += [fields[4], fields[5], fields[7]]
                    elif b == 1:
                        chosen += [fields[6], (a - 1) * fields[8], fields[7]]
                    else:
                        chosen += [(a - 1) * fields[6], None, fields[7]]
                    for n, value in enumerate(chosen):
                        if value is None:
                            continue
                        value = roll(value, a - 1, 0)
                        if n == 6:
                            moved_labels[place, j, z] = value.astype(jnp.int32)
                        else:
                            moved[place, n, j, z] = value


def first_prepare_kernel(state, labels, domains, moved, moved_labels):
    strip = [merged_strip(domains[0, n], domains[1, n]) for n in Y_FIELDS + (LABEL,)]
    prepare(state, labels, strip, moved, moved_labels)


def last_prepare_kernel(state, labels, strip, moved, moved_labels):
    prepare(state, labels, [strip[n] for n in range(8)], moved, moved_labels)


def stream(table, moved, moved_labels, left, right, left_marks, right_marks, corners, bottom, top, out, ghost, whole=None):
    rows = iota(0)
    for side, (source, marks) in enumerate(((left, left_marks), (right, right_marks))):
        a = 2 - 2 * side
        halves = [
            entering(table, [source[2 * n + j] for n in range(len(X_FIELDS))], marks(j), a) for j in range(2)
        ]
        for b in range(3):
            for c in range(3):
                inflow = None if b == 1 else take(corners[side][b, c], 16 * rows + (8 if b == 2 else 7))
                pair = shift_columns(halves[0][b, c], halves[1][b, c], b, inflow)
                for j in range(2):
                    ghost[side, 3 * b + c, j] = pair[j]
    for a in range(3):
        for b in range(3):
            out[9 * a + 3 * b + 2, 0] = bottom[3 * a + b]
            out[9 * a + 3 * b, LEVELS - 1] = top[3 * a + b]

    for z in range(LEVELS):
        for j in range(2):
            for a in range(3):
                for b in range(3):
                    place = 3 * a + b
                    speed = moved[place, 0, j, z] - look_up(table, moved_labels[place, j, z])
                    h = shapes(speed)[a]
                    for c in range(3):
                        level = z + c - 1
                        if level < 0 or level >= LEVELS:
                            continue
                        value = moved[place, 1 + c, j, z] * h
                        if c == 1:
                            value = value + moved[place, 4, j, z]
                        elif a == 1 and b == 1:
                            value = value + moved[place, 5, j, z]
                        elif a == 1 or b == 1:
                            value = value + (c - 1) * moved[place, 5, j, z]
                        if a == 2:
                            value = jnp.where(rows == 0, ghost[0, 3 * b + c, j, z : z + 1, :], value)
                        elif a == 0:
                            value = jnp.where(rows == 7, ghost[1, 3 * b + c, j, z : z + 1, :], value)
                        out[9 * a + 3 * b + c, level, :, 128 * j : 128 * j + 128] = value
        if whole and z:
            whole(z - 1)
    if whole:
        whole(LEVELS - 1)


def disk_table(sums, counts):
    disk = sums / jnp.maximum(counts, 1.0)
    return jnp.where(iota(1) < ROTORS, THRUST_GAIN * disk * jnp.abs(disk), 0.0)


def marks_of(message):
    return lambda j: message[2 * len(X_FIELDS) + j].astype(jnp.int32)


def middle_kernel(
    moved, moved_labels, domains, column_sums, beside, starts, found, found_beside, left, right, bottom, top,
    new_state, to_right, to_left, strip, counts, sums_out, f_ref, ghost, speeds,
):
    lanes = iota(1)
    last = 2 * len(X_FIELDS) + 4
    totals = column_sums[...] + left[last] + right[last]
    seen = roll(totals, 64, 1)
    counts[...] = seen
    table = disk_table(totals, seen)

    outside, kept, corners = [], [], [{}, {}]
    for side in range(2):
        outer, new = step_domain(table, side, domains, left, right, beside)
        ux, fields = relax(low_moments(lambda a, b, c: new[a, b, c]))
        outside.append(ux)
        kept.append([fields[n] for n in Y_FIELDS] + [domains[side, LABEL]])
        b = 2 - 2 * side
        for c in range(3):
            for row, a in ((0, 2), (1, 0)):
                corners[row][b, c] = roll(outer[a][b, c], b - 1, 1)
    strips = [merged_strip(one, other) for one, other in zip(*kept)]
    for n, block in enumerate(strips):
        strip[n] = block
    stream(
        table, moved, moved_labels, left, right, marks_of(left), marks_of(right), corners, bottom, top, f_ref, ghost
    )

    def f(z, j, a, b, c):
        return f_ref[9 * a + 3 * b + c, z, :, 128 * j : 128 * j + 128]

    def keep_speed(z, j, ux):
        speeds[j, z] = ux

    collide(f, new_state, keep_speed)
    sums = found_sums(
        lambda z, j: speeds[j, z],
        jnp.where((lanes & 8) == 0, outside[0], outside[1]),
        starts, found, found_beside,
    )
    sums_out[...] = sums
    for target, row in ((to_right, 7), (to_left, 0)):
        slot = edge_rows(new_state, target, row)
        target[slot] = rows_of(strips, row)
        target[slot + 1] = sums


def last_kernel(
    moved, moved_labels, sums, counts, left, right, old_left, old_right, bottom, top, out_hbm, out, ghost, gone
):
    last = 2 * len(X_FIELDS) + 1
    totals = sums[...] + left[last] + right[last]
    table = disk_table(totals, counts[...])
    corners = [
        {(b, c): value for c, value in enumerate(strip_corners(table, message, a)) for b in (0, 2)}
        for message, a in ((left, 2), (right, 0))
    ]
    copies = [pltpu.make_async_copy(out.at[:, z], out_hbm.at[:, z], gone.at[z]) for z in range(LEVELS)]
    stream(
        table, moved, moved_labels, left, right, marks_of(old_left), marks_of(old_right), corners, bottom, top, out, ghost,
        whole=lambda z: copies[z].start(),
    )
    for copy in copies:
        copy.wait()


def call(kernel, inputs, outputs, scratch=(), in_hbm=0, out_hbm=0, copies=0):
    inputs = [pltpu.with_memory_space_constraint(x, pltpu.HBM) if n < in_hbm else x for n, x in enumerate(inputs)]

    def specs(count, outside):
        return [pl.BlockSpec(memory_space=pltpu.HBM if n < outside else pltpu.VMEM) for n in range(count)]

    return pl.pallas_call(
        kernel,
        out_shape=[jax.ShapeDtypeStruct(shape, dtype) for shape, dtype in outputs],
        in_specs=specs(len(inputs), in_hbm),
        out_specs=specs(len(outputs), out_hbm),
        scratch_shapes=[pltpu.VMEM(shape, dtype) for shape, dtype in scratch]
        + ([pltpu.SemaphoreType.DMA((copies,))] if copies else []),
        compiler_params=pltpu.CompilerParams(vmem_limit_bytes=VMEM_LIMIT),
    )(*inputs)


def both_ways(upward, downward, axis):
    count = lax.axis_size(axis)
    return (
        lax.ppermute(upward, axis, [(i, (i + 1) % count) for i in range(count)]),
        lax.ppermute(downward, axis, [((i + 1) % count, i) for i in range(count)]),
    )


def swapped(even, odd, axis):
    count = lax.axis_size(axis)

    def pairs(start):
        there = [(i, (i + 1) % count) for i in range(start, count, 2)]
        return there + [(j, i) for i, j in there]

    return lax.ppermute(even, axis, pairs(0)), lax.ppermute(odd, axis, pairs(1))


def body(populations, bottom_in, top_in, turbine_mask, rotor_index):
    f32 = jnp.float32
    state_shape = ((10, 2, 64, 128), f32)
    one = ((8, 128), f32)
    ghost = ((2, 9, 2, 8, 128), f32)
    inflow = (bottom_in.shape, f32)
    cells = (turbine_mask.shape, jnp.int32)
    whole = (populations.shape, f32)
    n = 2 * len(X_FIELDS)

    def blocks(*count):
        return (count + (8, 128), f32)

    state, labels, edges, to_even, to_odd = call(
        first_kernel,
        (populations, turbine_mask, rotor_index, bottom_in, top_in),
        (((11, 2, 64, 128), f32), ((2, 64, 128), jnp.int32), blocks(12), blocks(9), blocks(9)),
        (whole, cells, cells, inflow, inflow),
        in_hbm=5,
        copies=LEVELS + 4,
    )
    even, odd = swapped(to_even, to_odd, "gy")
    (own_sums,) = call(sums_kernel, (state, labels), (one,))
    domains, to_right, to_left, column_sums, beside = call(
        relay_kernel,
        (state, labels, edges, own_sums, even, odd),
        (blocks(2, 12), blocks(n + 5), blocks(n + 5), one, blocks(2, 2)),
    )
    old_left, old_right = both_ways(to_right, to_left, "gx")
    starts, found, found_beside = call(
        places_kernel,
        (labels, domains),
        (((2, 8, 128), jnp.int32), blocks(SPAN, 2, LEVELS), blocks(SPAN, LEVELS)),
    )
    shifted = (blocks(9, 6, 2, LEVELS), ((9, 2, LEVELS, 8, 128), jnp.int32))
    moved, moved_labels = call(first_prepare_kernel, (state, labels, domains), shifted)
    state, to_right, to_left, strip, counts, sums = call(
        middle_kernel,
        (
            moved, moved_labels, domains, column_sums, beside, starts, found, found_beside,
            old_left, old_right, bottom_in, top_in,
        ),
        (state_shape, blocks(n + 2), blocks(n + 2), blocks(8), one, one),
        (whole, ghost, blocks(2, LEVELS)),
    )
    left, right = both_ways(to_right, to_left, "gx")
    moved, moved_labels = call(last_prepare_kernel, (state, labels, strip), shifted)
    (out,) = call(
        last_kernel,
        (moved, moved_labels, sums, counts, left, right, old_left, old_right, bottom_in, top_in),
        (whole,),
        (whole, ghost),
        out_hbm=1,
        copies=LEVELS,
    )
    return out


def solution(mesh):
    placed = (
        P(None, None, "gx", "gy"),
        P(None, "gx", "gy"),
        P(None, "gx", "gy"),
        P(None, "gx", "gy"),
        P(None, "gx", "gy"),
    )
    return jax.shard_map(
        body, mesh=mesh, in_specs=placed, out_specs=P(None, None, "gx", "gy"), check_vma=False
    )
```

```python
import functools

import jax
import jax.numpy as jnp
from jax import lax
from jax.experimental import pallas as pl
from jax.experimental.pallas import tpu as pltpu
from jax.sharding import PartitionSpec as P

ROTORS = 64
SOUND = 1.0 / 3.0
TAU_BASE = 0.52
SMAG_GAIN = 5.0
CORIOLIS = 0.05
GEO_U = 0.08
THRUST_GAIN = 4.0
EMPTY = 127
LEVELS = 8
VMEM_LIMIT = 24 * 1024 * 1024

RHO, VX, VY, VZ, DXX, DYY, DZZ, DXY, DXZ, DYZ = range(10)
SPEED = 10
LABEL = 10
SPAN = 5
X_FIELDS = (RHO, VX, VY, VZ, DXX, DXY, DXZ)
Y_FIELDS = (RHO, VX, VY, VZ, DYY, DXY, DYZ)


def iota(axis):
    return lax.broadcasted_iota(jnp.int32, (8, 128), axis)


def roll(block, shift, axis):
    size = block.shape[axis]
    return pltpu.roll(block, shift % size, axis) if shift % size else block


def low_moments(f):
    along_z = {}
    for a in range(3):
        for b in range(3):
            low, mid, high = f(a, b, 0), f(a, b, 1), f(a, b, 2)
            ends = low + high
            along_z[a, b] = (ends + mid, high - low, ends)
    slabs = []
    for a in range(3):
        (l0, l1, l2), (m0, m1, m2), (h0, h1, h2) = (along_z[a, b] for b in range(3))
        ends = l0 + h0
        slabs.append((ends + m0, h0 - l0, ends, l1 + m1 + h1, h1 - l1, l2 + m2 + h2))
    low, mid, high = slabs
    ends = low[0] + high[0]
    return {
        "0": ends + mid[0],
        "x": high[0] - low[0],
        "xx": ends,
        "y": low[1] + mid[1] + high[1],
        "xy": high[1] - low[1],
        "yy": low[2] + mid[2] + high[2],
        "z": low[3] + mid[3] + high[3],
        "xz": high[3] - low[3],
        "yz": low[4] + mid[4] + high[4],
        "zz": low[5] + mid[5] + high[5],
    }


def relax(m):
    rho = m["0"]
    inverse = 1.0 / rho
    ux, uy, uz = m["x"] * inverse, m["y"] * inverse, m["z"] * inverse
    third = rho * SOUND
    qxx = m["xx"] - (m["x"] * ux + third)
    qyy = m["yy"] - (m["y"] * uy + third)
    qzz = m["zz"] - (m["z"] * uz + third)
    qxy = m["xy"] - m["x"] * uy
    qxz = m["xz"] - m["x"] * uz
    qyz = m["yz"] - m["y"] * uz
    strain = qxx * qxx + qyy * qyy + qzz * qzz + 2.0 * (qxy * qxy + qxz * qxz + qyz * qyz)
    keep = 1.0 - 1.0 / (TAU_BASE + SMAG_GAIN * jnp.sqrt(strain))
    vx = ux + CORIOLIS * uy
    vy = uy - CORIOLIS * (ux - GEO_U)
    fields = [rho, vx, vy, uz] + [keep * q for q in (qxx, qyy, qzz, qxy, qxz, qyz)]
    return ux, fields


def shapes(speed):
    square = speed * speed + SOUND
    return (0.5 * (square - speed), 1.0 - square, 0.5 * (square + speed))


def over_rows(block, join=jnp.add):
    for shift in (4, 2, 1):
        block = join(block, roll(block, shift, 0))
    return block


def spread(leaf, join=jnp.add):
    lanes = iota(1)

    def node(stride, ways, rest, index):
        parts = [(node(*rest, index + d * stride) if rest else leaf(index + d * stride)) for d in range(ways)]
        digit = (lanes // stride) % ways
        moved = []
        for k in range(ways):
            picked = parts[k]
            for d in range(1, ways):
                picked = jnp.where(digit == d, parts[(d + k) % ways], picked)
            moved.append(roll(picked, k * stride, 1))
        return functools.reduce(join, moved)

    return over_rows(node(16, 8, (2, 8, (1, 2, ())), 0), join)


def rotor_sums(labels, speeds):
    def leaf(index):
        rotor, counting = index % ROTORS, index >= ROTORS
        total = jnp.zeros((8, 128), jnp.float32)
        for label, speed in zip(labels, speeds):
            total = total + jnp.where(label == rotor, 1.0 if counting else speed, 0.0)
        return total

    return spread(leaf)


def take(block, index):
    return jnp.take_along_axis(block, index, axis=1, mode="promise_in_bounds")


def sums_kernel(state, labels, own_sums):
    places = [(j, z) for j in range(2) for z in range(LEVELS)]
    own_sums[...] = rotor_sums(
        [labels[j, 8 * z : 8 * z + 8, :] for j, z in places],
        [state[SPEED, j, 8 * z : 8 * z + 8, :] for j, z in places],
    )


def beside_tile(domains, n):
    return jnp.where((iota(1) & 8) == 0, domains[0, n], domains[1, n])


def places_kernel(labels, domains, starts, found, found_beside):
    lanes = iota(1)
    far = 1024.0
    column = lanes & 15
    near = jnp.logical_and(column >= 3, column < 13)
    outside = jnp.where(near, index_of(beside_tile(domains, LABEL)), EMPTY)
    inside = {(j, z): labels[j, 8 * z : 8 * z + 8, :] for j in range(2) for z in range(LEVELS)}

    def leaf(index):
        rotor = index % ROTORS
        if index >= ROTORS:
            return jnp.where(outside == rotor, column.astype(jnp.float32), far)
        first = jnp.full((8, 128), far, jnp.float32)
        for j in range(2):
            hit = inside[j, 0] == rotor
            for z in range(1, LEVELS):
                hit = jnp.logical_or(hit, inside[j, z] == rotor)
            first = jnp.minimum(first, jnp.where(hit, (lanes + 128 * j).astype(jnp.float32), far))
        return first

    both = spread(leaf, jnp.minimum)
    begin = (jnp.where(both < far, both, 0.0)).astype(jnp.int32)
    begin_beside = roll(begin.astype(jnp.float32), 64, 1).astype(jnp.int32)
    starts[0] = begin
    starts[1] = begin_beside
    own = jnp.where(lanes < ROTORS, lanes, -1)
    for k in range(SPAN):
        index = (begin + k) & 127
        for z in range(LEVELS):
            for j in range(2):
                found[k, j, z] = jnp.where(take(inside[j, z], index) == own, 1.0, 0.0)
            index_beside = (begin_beside + (k + 16 * z)) & 127
            found_beside[k, z] = jnp.where(take(outside, index_beside) == own, 1.0, 0.0)


def found_sums(speed, speed_beside, starts, found, found_beside):
    total = jnp.zeros((8, 128), jnp.float32)
    for k in range(SPAN):
        index = (starts[0] + k) & 127
        for z in range(LEVELS):
            for j in range(2):
                total = total + jnp.where(found[k, j, z] > 0.0, take(speed(z, j), index), 0.0)
            index_beside = (starts[1] + (k + 16 * z)) & 127
            total = total + jnp.where(found_beside[k, z] > 0.0, take(speed_beside, index_beside), 0.0)
    return over_rows(total)


def collide(f, state, keep_speed):
    for z in range(LEVELS):
        for j in range(2):
            ux, fields = relax(low_moments(functools.partial(f, z, j)))
            for index, value in enumerate(fields):
                state[index, j, 8 * z : 8 * z + 8, :] = value
            keep_speed(z, j, ux)


def first_kernel(
    f_hbm, mask_hbm, rotor_hbm, bottom_hbm, top_hbm, state, labels, edges, to_even, to_odd,
    f_ref, mask_ref, rotor_ref, bottom, top, arrived,
):
    lanes = iota(1)
    levels = [pltpu.make_async_copy(f_hbm.at[:, z], f_ref.at[:, z], arrived.at[z]) for z in range(LEVELS)]
    others = [
        pltpu.make_async_copy(source, target, arrived.at[LEVELS + n])
        for n, (source, target) in enumerate(
            ((mask_hbm, mask_ref), (rotor_hbm, rotor_ref), (bottom_hbm, bottom), (top_hbm, top))
        )
    ]
    for copy in [levels[0]] + others[:2] + levels[1:] + others[2:]:
        copy.start()
    others[0].wait()
    others[1].wait()
    waiting = list(levels)

    def f(z, j, a, b, c):
        if len(waiting) == LEVELS - z:
            waiting.pop(0).wait()
        return f_ref[9 * a + 3 * b + c, z, :, 128 * j : 128 * j + 128]

    def keep_speed(z, j, ux):
        here = (z, slice(None), slice(128 * j, 128 * j + 128))
        state[SPEED, j, 8 * z : 8 * z + 8, :] = ux
        labels[j, 8 * z : 8 * z + 8, :] = jnp.where(mask_ref[here] != 0, rotor_ref[here], EMPTY)

    collide(f, state, keep_speed)

    def edge(read):
        block = jnp.zeros((8, 128), jnp.float32)
        inner = block
        for z in range(LEVELS):
            moved = roll(jnp.where(lanes < 64, read(z, 0), read(z, 1)), 16 * z + 8, 1)
            block = jnp.where(lanes // 16 == z, moved, block)
            wanted = jnp.logical_or(((lanes - 16 * z + 2) & 127) < 2, ((lanes - 16 * z - 16) & 127) < 2)
            inner = jnp.where(wanted, moved, inner)
        return block, inner

    pairs = [edge(lambda z, j, n=n: state[n, j, 8 * z : 8 * z + 8, :]) for n in range(10)]
    pairs.append(edge(lambda z, j: labels[j, 8 * z : 8 * z + 8, :].astype(jnp.float32)))
    pairs.append(edge(lambda z, j: state[SPEED, j, 8 * z : 8 * z + 8, :]))
    blocks = [block for block, _ in pairs]
    inner_label, inner_speed = pairs[LABEL][1], pairs[LABEL + 1][1]
    for n, block in enumerate(blocks):
        edges[n] = block
    low = (lanes & 8) == 0
    send = Paired("gy", to_even, to_odd).put

    for n in range(6):
        one, other = blocks[2 * n], blocks[2 * n + 1]
        send(n, jnp.where(low, one, roll(other, 8, 1)), jnp.where(low, roll(other, -8, 1), one))
    column = lanes & 15
    send(
        6,
        jnp.where(column >= 14, inner_speed, jnp.where(column >= 12, roll(inner_label, -2, 1), float(EMPTY))),
        jnp.where(column < 2, inner_speed, jnp.where(column < 4, roll(inner_label, 2, 1), float(EMPTY))),
    )
    others[2].wait()
    others[3].wait()
    for place, source in ((7, bottom), (8, top)):
        upward = jnp.zeros((8, 128), jnp.float32)
        downward = upward
        for n in range(9):
            both = jnp.where(lanes < 64, source[n, :, 0:128], source[n, :, 128:256])
            moved = roll(both, 8 * n + 8, 1)
            upward = jnp.where(lanes // 8 == n, moved, upward)
            downward = jnp.where(lanes // 8 == n + 1, moved, downward)
        send(place, upward, downward)


class Paired:
    def __init__(self, axis, even, odd):
        self.next_first = lax.rem(lax.axis_index(axis), 2) == 0
        self.refs = (even, odd)

    def put(self, n, to_next, to_previous):
        even, odd = self.refs
        even[n] = jnp.where(self.next_first, to_next, to_previous)
        odd[n] = jnp.where(self.next_first, to_previous, to_next)

    def received(self):
        even, odd = self.refs
        return Chosen(self.next_first, odd, even), Chosen(self.next_first, even, odd)


class Chosen:
    def __init__(self, flag, one, other):
        self.flag, self.one, self.other = flag, one, other

    def __getitem__(self, n):
        return jnp.where(self.flag, self.one[n], self.other[n])


def rows_of(blocks, row):
    rows = iota(0)
    out = jnp.broadcast_to(blocks[0][row : row + 1], (8, 128))
    for n in range(1, len(blocks)):
        out = jnp.where(rows == n, jnp.broadcast_to(blocks[n][row : row + 1], (8, 128)), out)
    return out


def edge_rows(state, sent):
    slot = 0
    for index in X_FIELDS:
        for j in range(2):
            sent.put(slot, *(state[index, j, pl.ds(row, 8, stride=8), :] for row in (7, 0)))
            slot += 1
    return slot


def relay_kernel(state, labels, edges, own_sums, even, odd, domains, to_even, to_odd, column_sums, beside):
    below, above = ([chosen[n] for n in range(9)] for chosen in Paired("gy", even, odd).received())
    for side, message in enumerate((below, above)):
        for n in range(2):
            beside[side, n] = message[7 + n]
    low = (iota(1) & 8) == 0
    for n in range(12):
        under, over = below[n // 2], above[n // 2]
        if n % 2:
            under, over = roll(under, -8, 1), roll(over, 8, 1)
        domains[0, n] = jnp.where(low, under, edges[n])
        domains[1, n] = jnp.where(low, edges[n], over)
    column = iota(1) & 15
    inner = jnp.where(
        column >= 14, roll(below[6], 2, 1), jnp.where(column < 2, roll(above[6], -2, 1), float(EMPTY))
    )
    sums = own_sums[...] + rotor_sums(
        [index_of(beside_tile(domains, LABEL)), index_of(inner)],
        [beside_tile(domains, LABEL + 1), jnp.where(column >= 8, below[6], above[6])],
    )
    column_sums[...] = sums
    sent = Paired("gx", to_even, to_odd)
    slot = edge_rows(state, sent)
    for j in range(2):
        sent.put(slot + j, *(labels[j, pl.ds(row, 8, stride=8), :].astype(jnp.float32) for row in (7, 0)))
    for side in range(2):
        blocks = [domains[side, n] for n in X_FIELDS + (LABEL,)]
        sent.put(slot + 2 + side, rows_of(blocks, 7), rows_of(blocks, 0))
    sent.put(slot + 4, sums, sums)


look_up = take


def index_of(mark):
    return jnp.clip(mark, 0.0, float(EMPTY)).astype(jnp.int32)


def slot_value(d, parts, along_y, along_z, a, b, c):
    value = parts[a] * along_y[b] * along_z[c]
    ones = (a == 1) + (b == 1) + (c == 1)
    if ones == 3:
        return value - (d[DXX] + d[DYY] + d[DZZ])
    if ones == 2:
        return value + 0.5 * (d[DXX] if a != 1 else d[DYY] if b != 1 else d[DZZ])
    if ones == 1 and c == 1:
        return value + (0.25 * (a - 1) * (b - 1)) * d[DXY]
    if ones == 1 and b == 1:
        return value + (0.25 * (a - 1) * (c - 1)) * d[DXZ]
    if ones == 1:
        return value + (0.25 * (b - 1) * (c - 1)) * d[DYZ]
    return value


def entering(table, fields, mark, a):
    rho, vx, vy, vz, dxx, dxy, dxz = fields
    part = rho * shapes(vx - look_up(table, mark))[a]
    d = {DXX: dxx, DXY: dxy, DXZ: dxz}
    along_y, along_z = shapes(vy), shapes(vz)
    return {(b, c): slot_value(d, {a: part}, along_y, along_z, a, b, c) for b in range(3) for c in range(3)}


def shift_rows(value, a, before, after):
    if a == 2:
        return jnp.where(iota(0) == 0, before, roll(value, 1, 0))
    if a == 0:
        return jnp.where(iota(0) == 7, after, roll(value, -1, 0))
    return value


def row_blocks(block, count):
    return [jnp.broadcast_to(block[n : n + 1], (8, 128)) for n in range(count)]


def step_domain(table, side, domains, left, right, beside):
    lanes = iota(1)
    d = [domains[side, n] for n in range(10)]
    thrust = look_up(table, index_of(domains[side, LABEL]))
    parts = [d[RHO] * h for h in shapes(d[VX] - thrust)]
    along_y, along_z = shapes(d[VY]), shapes(d[VZ])
    n = 2 * len(X_FIELDS) + 2 + side
    outer = {}
    for a, message in ((2, left), (0, right)):
        fields = row_blocks(message[n], 8)
        outer[a] = entering(table, fields[:7], index_of(fields[7]), a)
    new = {}
    for a in range(3):
        for b in range(3):
            for c in range(3):
                value = slot_value(d, parts, along_y, along_z, a, b, c)
                value = shift_rows(value, a, outer[2][b, c], outer[0][b, c])
                value = roll(value, b - 1, 1)
                slot = 3 * a + b
                if c == 2:
                    value = jnp.where(lanes < 16, roll(beside[side, 0], -8 * slot, 1), roll(value, 16, 1))
                elif c == 0:
                    value = jnp.where(lanes >= 112, roll(beside[side, 1], 112 - 8 * slot, 1), roll(value, -16, 1))
                new[a, b, c] = value
    return outer, new


def strip_corners(table, message, a):
    even = (iota(1) & 1) == 0
    rho, vx, vy, vz, _, dxy, _, mark = row_blocks(message[2 * len(X_FIELDS)], 8)
    along_y, along_z = shapes(vy), shapes(vz)
    part = rho * shapes(vx - look_up(table, index_of(mark)))[a] * jnp.where(even, along_y[2], along_y[0])
    slots = [part * along_z[c] for c in range(3)]
    slots[1] = slots[1] + ((a - 1) * jnp.where(even, 0.25, -0.25)) * dxy
    return slots


def merged_strip(left_end, right_end):
    return jnp.where((iota(1) & 1) == 0, roll(left_end, 1, 1), roll(right_end, -1, 1))


def shift_columns(first, second, b, inflow):
    lanes = iota(1)
    if b == 2:
        first, second = roll(first, 1, 1), roll(second, 1, 1)
        return jnp.where(lanes == 0, inflow, first), jnp.where(lanes == 0, first, second)
    if b == 0:
        first, second = roll(first, -1, 1), roll(second, -1, 1)
        return jnp.where(lanes == 127, second, first), jnp.where(lanes == 127, inflow, second)
    return first, second


def prepare(state, labels, strip, moved, moved_labels):
    even = (iota(1) & 1) == 0
    rho, vx, vy, vz, dyy, dxy, dyz, mark = strip
    sign = jnp.where(even, 0.25, -0.25)
    along_y, along_z = shapes(vy), shapes(vz)
    part = rho * jnp.where(even, along_y[2], along_y[0])
    outside = [vx] + [part * h for h in along_z] + [0.5 * dyy, sign * dyz, sign * dxy, mark]
    for z in range(LEVELS):
        inflow = [roll(block, -16 * z - 8, 1) for block in outside]
        tiles = []
        for j in range(2):
            d = [state[n, j, 8 * z : 8 * z + 8, :] for n in range(10)]
            mark = labels[j, 8 * z : 8 * z + 8, :].astype(jnp.float32)
            along_y, along_z = shapes(d[VY]), shapes(d[VZ])
            rows = [d[RHO] * h for h in along_y]
            tiles.append((d, mark, rows, along_z))
        for b in range(3):
            kept = []
            for d, mark, rows, along_z in tiles:
                if b == 1:
                    terms = [-(d[DXX] + d[DYY] + d[DZZ]), 0.5 * d[DZZ], 0.5 * d[DXX], mark, 0.25 * d[DXZ]]
                else:
                    terms = [0.5 * d[DYY], (0.25 * (b - 1)) * d[DYZ], (0.25 * (b - 1)) * d[DXY], mark]
                kept.append([d[VX]] + [rows[b] * h for h in along_z] + terms)
            if b != 1:
                pairs = [shift_columns(*pair) for pair in zip(*kept, [b] * 8, inflow)]
                kept = list(zip(*pairs))
            for j, fields in enumerate(kept):
                for a in range(3):
                    place = 3 * a + b
                    chosen = list(fields[:4])
                    if a == 1:
                        chosen += [fields[4], fields[5], fields[7]]
                    elif b == 1:
                        chosen += [fields[6], (a - 1) * fields[8], fields[7]]
                    else:
                        chosen += [(a - 1) * fields[6], None, fields[7]]
                    for n, value in enumerate(chosen):
                        if value is None:
                            continue
                        value = roll(value, a - 1, 0)
                        if n == 6:
                            moved_labels[place, j, z] = value.astype(jnp.int32)
                        else:
                            moved[place, n, j, z] = value


def first_prepare_kernel(state, labels, domains, moved, moved_labels):
    strip = [merged_strip(domains[0, n], domains[1, n]) for n in Y_FIELDS + (LABEL,)]
    prepare(state, labels, strip, moved, moved_labels)


def last_prepare_kernel(state, labels, strip, moved, moved_labels):
    prepare(state, labels, [strip[n] for n in range(8)], moved, moved_labels)


def stream(table, moved, moved_labels, left, right, left_marks, right_marks, corners, bottom, top, out, ghost, whole=None):
    rows = iota(0)
    for side, (source, marks) in enumerate(((left, left_marks), (right, right_marks))):
        a = 2 - 2 * side
        halves = [
            entering(table, [source[2 * n + j] for n in range(len(X_FIELDS))], marks(j), a) for j in range(2)
        ]
        for b in range(3):
            for c in range(3):
                inflow = None if b == 1 else take(corners[side][b, c], 16 * rows + (8 if b == 2 else 7))
                pair = shift_columns(halves[0][b, c], halves[1][b, c], b, inflow)
                for j in range(2):
                    ghost[side, 3 * b + c, j] = pair[j]
    for a in range(3):
        for b in range(3):
            out[9 * a + 3 * b + 2, 0] = bottom[3 * a + b]
            out[9 * a + 3 * b, LEVELS - 1] = top[3 * a + b]

    for z in range(LEVELS):
        for j in range(2):
            for a in range(3):
                for b in range(3):
                    place = 3 * a + b
                    speed = moved[place, 0, j, z] - look_up(table, moved_labels[place, j, z])
                    h = shapes(speed)[a]
                    for c in range(3):
                        level = z + c - 1
                        if level < 0 or level >= LEVELS:
                            continue
                        value = moved[place, 1 + c, j, z] * h
                        if c == 1:
                            value = value + moved[place, 4, j, z]
                        elif a == 1 and b == 1:
                            value = value + moved[place, 5, j, z]
                        elif a == 1 or b == 1:
                            value = value + (c - 1) * moved[place, 5, j, z]
                        if a == 2:
                            value = jnp.where(rows == 0, ghost[0, 3 * b + c, j, z : z + 1, :], value)
                        elif a == 0:
                            value = jnp.where(rows == 7, ghost[1, 3 * b + c, j, z : z + 1, :], value)
                        out[9 * a + 3 * b + c, level, :, 128 * j : 128 * j + 128] = value
        if whole and z:
            whole(z - 1)
    if whole:
        whole(LEVELS - 1)


def disk_table(sums, counts):
    disk = sums / jnp.maximum(counts, 1.0)
    return jnp.where(iota(1) < ROTORS, THRUST_GAIN * disk * jnp.abs(disk), 0.0)


def marks_of(message):
    return lambda j: message[2 * len(X_FIELDS) + j].astype(jnp.int32)


def middle_kernel(
    moved, moved_labels, domains, column_sums, beside, starts, found, found_beside, even, odd, bottom, top,
    new_state, to_even, to_odd, strip, counts, sums_out, f_ref, ghost, speeds,
):
    lanes = iota(1)
    left, right = Paired("gx", even, odd).received()
    last = 2 * len(X_FIELDS) + 4
    totals = column_sums[...] + left[last] + right[last]
    seen = roll(totals, 64, 1)
    counts[...] = seen
    table = disk_table(totals, seen)

    outside, kept, corners = [], [], [{}, {}]
    for side in range(2):
        outer, new = step_domain(table, side, domains, left, right, beside)
        ux, fields = relax(low_moments(lambda a, b, c: new[a, b, c]))
        outside.append(ux)
        kept.append([fields[n] for n in Y_FIELDS] + [domains[side, LABEL]])
        b = 2 - 2 * side
        for c in range(3):
            for row, a in ((0, 2), (1, 0)):
                corners[row][b, c] = roll(outer[a][b, c], b - 1, 1)
    strips = [merged_strip(one, other) for one, other in zip(*kept)]
    for n, block in enumerate(strips):
        strip[n] = block
    stream(
        table, moved, moved_labels, left, right, marks_of(left), marks_of(right), corners, bottom, top, f_ref, ghost
    )

    def f(z, j, a, b, c):
        return f_ref[9 * a + 3 * b + c, z, :, 128 * j : 128 * j + 128]

    def keep_speed(z, j, ux):
        speeds[j, z] = ux

    collide(f, new_state, keep_speed)
    sums = found_sums(
        lambda z, j: speeds[j, z],
        jnp.where((lanes & 8) == 0, outside[0], outside[1]),
        starts, found, found_beside,
    )
    sums_out[...] = sums
    sent = Paired("gx", to_even, to_odd)
    slot = edge_rows(new_state, sent)
    sent.put(slot, rows_of(strips, 7), rows_of(strips, 0))
    sent.put(slot + 1, sums, sums)


def last_kernel(
    moved, moved_labels, sums, counts, even, odd, old_even, old_odd, bottom, top, out_hbm, out, ghost, gone
):
    left, right = Paired("gx", even, odd).received()
    old_left, old_right = Paired("gx", old_even, old_odd).received()
    last = 2 * len(X_FIELDS) + 1
    totals = sums[...] + left[last] + right[last]
    table = disk_table(totals, counts[...])
    corners = [
        {(b, c): value for c, value in enumerate(strip_corners(table, message, a)) for b in (0, 2)}
        for message, a in ((left, 2), (right, 0))
    ]
    copies = [pltpu.make_async_copy(out.at[:, z], out_hbm.at[:, z], gone.at[z]) for z in range(LEVELS)]
    stream(
        table, moved, moved_labels, left, right, marks_of(old_left), marks_of(old_right), corners, bottom, top, out, ghost,
        whole=lambda z: copies[z].start(),
    )
    for copy in copies:
        copy.wait()


def call(kernel, inputs, outputs, scratch=(), in_hbm=0, out_hbm=0, copies=0):
    inputs = [pltpu.with_memory_space_constraint(x, pltpu.HBM) if n < in_hbm else x for n, x in enumerate(inputs)]

    def specs(count, outside):
        return [pl.BlockSpec(memory_space=pltpu.HBM if n < outside else pltpu.VMEM) for n in range(count)]

    return pl.pallas_call(
        kernel,
        out_shape=[jax.ShapeDtypeStruct(shape, dtype) for shape, dtype in outputs],
        in_specs=specs(len(inputs), in_hbm),
        out_specs=specs(len(outputs), out_hbm),
        scratch_shapes=[pltpu.VMEM(shape, dtype) for shape, dtype in scratch]
        + ([pltpu.SemaphoreType.DMA((copies,))] if copies else []),
        compiler_params=pltpu.CompilerParams(vmem_limit_bytes=VMEM_LIMIT),
    )(*inputs)


def swapped(even, odd, axis):
    count = lax.axis_size(axis)

    def pairs(start):
        there = [(i, (i + 1) % count) for i in range(start, count, 2)]
        return there + [(j, i) for i, j in there]

    return lax.ppermute(even, axis, pairs(0)), lax.ppermute(odd, axis, pairs(1))


def body(populations, bottom_in, top_in, turbine_mask, rotor_index):
    f32 = jnp.float32
    state_shape = ((10, 2, 64, 128), f32)
    one = ((8, 128), f32)
    ghost = ((2, 9, 2, 8, 128), f32)
    inflow = (bottom_in.shape, f32)
    cells = (turbine_mask.shape, jnp.int32)
    whole = (populations.shape, f32)
    n = 2 * len(X_FIELDS)

    def blocks(*count):
        return (count + (8, 128), f32)

    state, labels, edges, to_even, to_odd = call(
        first_kernel,
        (populations, turbine_mask, rotor_index, bottom_in, top_in),
        (((11, 2, 64, 128), f32), ((2, 64, 128), jnp.int32), blocks(12), blocks(9), blocks(9)),
        (whole, cells, cells, inflow, inflow),
        in_hbm=5,
        copies=LEVELS + 4,
    )
    even, odd = swapped(to_even, to_odd, "gy")
    (own_sums,) = call(sums_kernel, (state, labels), (one,))
    domains, to_even, to_odd, column_sums, beside = call(
        relay_kernel,
        (state, labels, edges, own_sums, even, odd),
        (blocks(2, 12), blocks(n + 5), blocks(n + 5), one, blocks(2, 2)),
    )
    old_even, old_odd = swapped(to_even, to_odd, "gx")
    starts, found, found_beside = call(
        places_kernel,
        (labels, domains),
        (((2, 8, 128), jnp.int32), blocks(SPAN, 2, LEVELS), blocks(SPAN, LEVELS)),
    )
    shifted = (blocks(9, 6, 2, LEVELS), ((9, 2, LEVELS, 8, 128), jnp.int32))
    moved, moved_labels = call(first_prepare_kernel, (state, labels, domains), shifted)
    state, to_even, to_odd, strip, counts, sums = call(
        middle_kernel,
        (
            moved, moved_labels, domains, column_sums, beside, starts, found, found_beside,
            old_even, old_odd, bottom_in, top_in,
        ),
        (state_shape, blocks(n + 2), blocks(n + 2), blocks(8), one, one),
        (whole, ghost, blocks(2, LEVELS)),
    )
    even, odd = swapped(to_even, to_odd, "gx")
    moved, moved_labels = call(last_prepare_kernel, (state, labels, strip), shifted)
    (out,) = call(
        last_kernel,
        (moved, moved_labels, sums, counts, even, odd, old_even, old_odd, bottom_in, top_in),
        (whole,),
        (whole, ghost),
        out_hbm=1,
        copies=LEVELS,
    )
    return out


def solution(mesh):
    placed = (
        P(None, None, "gx", "gy"),
        P(None, "gx", "gy"),
        P(None, "gx", "gy"),
        P(None, "gx", "gy"),
        P(None, "gx", "gy"),
    )
    return jax.shard_map(
        body, mesh=mesh, in_specs=placed, out_specs=P(None, None, "gx", "gy"), check_vma=False
    )
```

```python
import functools

import jax
import jax.numpy as jnp
from jax import lax
from jax.experimental import pallas as pl
from jax.experimental.pallas import tpu as pltpu
from jax.sharding import PartitionSpec as P

ROTORS = 64
SOUND = 1.0 / 3.0
TAU_BASE = 0.52
SMAG_GAIN = 5.0
CORIOLIS = 0.05
GEO_U = 0.08
THRUST_GAIN = 4.0
EMPTY = 127
LEVELS = 8
VMEM_LIMIT = 24 * 1024 * 1024

RHO, VX, VY, VZ, DXX, DYY, DZZ, DXY, DXZ, DYZ = range(10)
SPEED = 10
LABEL = 10
SPAN = 5
X_FIELDS = (RHO, VX, VY, VZ, DXX, DXY, DXZ)
Y_FIELDS = (RHO, VX, VY, VZ, DYY, DXY, DYZ)


def iota(axis):
    return lax.broadcasted_iota(jnp.int32, (8, 128), axis)


def roll(block, shift, axis):
    size = block.shape[axis]
    return pltpu.roll(block, shift % size, axis) if shift % size else block


def low_moments(f):
    along_z = {}
    for a in range(3):
        for b in range(3):
            low, mid, high = f(a, b, 0), f(a, b, 1), f(a, b, 2)
            ends = low + high
            along_z[a, b] = (ends + mid, high - low, ends)
    slabs = []
    for a in range(3):
        (l0, l1, l2), (m0, m1, m2), (h0, h1, h2) = (along_z[a, b] for b in range(3))
        ends = l0 + h0
        slabs.append((ends + m0, h0 - l0, ends, l1 + m1 + h1, h1 - l1, l2 + m2 + h2))
    low, mid, high = slabs
    ends = low[0] + high[0]
    return {
        "0": ends + mid[0],
        "x": high[0] - low[0],
        "xx": ends,
        "y": low[1] + mid[1] + high[1],
        "xy": high[1] - low[1],
        "yy": low[2] + mid[2] + high[2],
        "z": low[3] + mid[3] + high[3],
        "xz": high[3] - low[3],
        "yz": low[4] + mid[4] + high[4],
        "zz": low[5] + mid[5] + high[5],
    }


def relax(m):
    rho = m["0"]
    inverse = 1.0 / rho
    ux, uy, uz = m["x"] * inverse, m["y"] * inverse, m["z"] * inverse
    third = rho * SOUND
    qxx = m["xx"] - (m["x"] * ux + third)
    qyy = m["yy"] - (m["y"] * uy + third)
    qzz = m["zz"] - (m["z"] * uz + third)
    qxy = m["xy"] - m["x"] * uy
    qxz = m["xz"] - m["x"] * uz
    qyz = m["yz"] - m["y"] * uz
    strain = qxx * qxx + qyy * qyy + qzz * qzz + 2.0 * (qxy * qxy + qxz * qxz + qyz * qyz)
    keep = 1.0 - 1.0 / (TAU_BASE + SMAG_GAIN * jnp.sqrt(strain))
    vx = ux + CORIOLIS * uy
    vy = uy - CORIOLIS * (ux - GEO_U)
    fields = [rho, vx, vy, uz] + [keep * q for q in (qxx, qyy, qzz, qxy, qxz, qyz)]
    return ux, fields


def shapes(speed):
    square = speed * speed + SOUND
    return (0.5 * (square - speed), 1.0 - square, 0.5 * (square + speed))


def over_rows(block, join=jnp.add):
    for shift in (4, 2, 1):
        block = join(block, roll(block, shift, 0))
    return block


def spread(leaf, join=jnp.add):
    lanes = iota(1)

    def node(stride, ways, rest, index):
        parts = [(node(*rest, index + d * stride) if rest else leaf(index + d * stride)) for d in range(ways)]
        digit = (lanes // stride) % ways
        moved = []
        for k in range(ways):
            picked = parts[k]
            for d in range(1, ways):
                picked = jnp.where(digit == d, parts[(d + k) % ways], picked)
            moved.append(roll(picked, k * stride, 1))
        return functools.reduce(join, moved)

    return over_rows(node(16, 8, (2, 8, (1, 2, ())), 0), join)


def rotor_sums(labels, speeds):
    def leaf(index):
        rotor, counting = index % ROTORS, index >= ROTORS
        total = jnp.zeros((8, 128), jnp.float32)
        for label, speed in zip(labels, speeds):
            total = total + jnp.where(label == rotor, 1.0 if counting else speed, 0.0)
        return total

    return spread(leaf)


def take(block, index):
    return jnp.take_along_axis(block, index, axis=1, mode="promise_in_bounds")


def sums_kernel(state, labels, own_sums):
    places = [(j, z) for j in range(2) for z in range(LEVELS)]
    own_sums[...] = rotor_sums(
        [labels[j, 8 * z : 8 * z + 8, :] for j, z in places],
        [state[SPEED, j, 8 * z : 8 * z + 8, :] for j, z in places],
    )


def beside_tile(domains, n):
    return jnp.where((iota(1) & 8) == 0, domains[0, n], domains[1, n])


def places_kernel(labels, domains, starts, found, found_beside):
    lanes = iota(1)
    far = 1024.0
    column = lanes & 15
    near = jnp.logical_and(column >= 3, column < 13)
    outside = jnp.where(near, index_of(beside_tile(domains, LABEL)), EMPTY)
    inside = {(j, z): labels[j, 8 * z : 8 * z + 8, :] for j in range(2) for z in range(LEVELS)}

    def leaf(index):
        rotor = index % ROTORS
        if index >= ROTORS:
            return jnp.where(outside == rotor, column.astype(jnp.float32), far)
        first = jnp.full((8, 128), far, jnp.float32)
        for j in range(2):
            hit = inside[j, 0] == rotor
            for z in range(1, LEVELS):
                hit = jnp.logical_or(hit, inside[j, z] == rotor)
            first = jnp.minimum(first, jnp.where(hit, (lanes + 128 * j).astype(jnp.float32), far))
        return first

    both = spread(leaf, jnp.minimum)
    begin = (jnp.where(both < far, both, 0.0)).astype(jnp.int32)
    begin_beside = roll(begin.astype(jnp.float32), 64, 1).astype(jnp.int32)
    starts[0] = begin
    starts[1] = begin_beside
    own = jnp.where(lanes < ROTORS, lanes, -1)
    for k in range(SPAN):
        index = (begin + k) & 127
        for z in range(LEVELS):
            for j in range(2):
                found[k, j, z] = jnp.where(take(inside[j, z], index) == own, 1.0, 0.0)
            index_beside = (begin_beside + (k + 16 * z)) & 127
            found_beside[k, z] = jnp.where(take(outside, index_beside) == own, 1.0, 0.0)


def found_sums(speed, speed_beside, starts, found, found_beside):
    total = jnp.zeros((8, 128), jnp.float32)
    for k in range(SPAN):
        index = (starts[0] + k) & 127
        for z in range(LEVELS):
            for j in range(2):
                total = total + jnp.where(found[k, j, z] > 0.0, take(speed(z, j), index), 0.0)
            index_beside = (starts[1] + (k + 16 * z)) & 127
            total = total + jnp.where(found_beside[k, z] > 0.0, take(speed_beside, index_beside), 0.0)
    return over_rows(total)


def collide(f, state, keep_speed):
    for z in range(LEVELS):
        for j in range(2):
            ux, fields = relax(low_moments(functools.partial(f, z, j)))
            for index, value in enumerate(fields):
                state[index, j, 8 * z : 8 * z + 8, :] = value
            keep_speed(z, j, ux)


def first_kernel(
    f_hbm, mask_hbm, rotor_hbm, bottom_hbm, top_hbm, state, labels, edges, to_even, to_odd,
    f_ref, mask_ref, rotor_ref, bottom, top, arrived,
):
    lanes = iota(1)
    levels = [pltpu.make_async_copy(f_hbm.at[:, z], f_ref.at[:, z], arrived.at[z]) for z in range(LEVELS)]
    others = [
        pltpu.make_async_copy(source, target, arrived.at[LEVELS + n])
        for n, (source, target) in enumerate(
            ((mask_hbm, mask_ref), (rotor_hbm, rotor_ref), (bottom_hbm, bottom), (top_hbm, top))
        )
    ]
    for copy in [levels[0]] + others[:2] + levels[1:] + others[2:]:
        copy.start()
    others[0].wait()
    others[1].wait()
    waiting = list(levels)

    def f(z, j, a, b, c):
        if len(waiting) == LEVELS - z:
            waiting.pop(0).wait()
        return f_ref[9 * a + 3 * b + c, z, :, 128 * j : 128 * j + 128]

    def keep_speed(z, j, ux):
        here = (z, slice(None), slice(128 * j, 128 * j + 128))
        state[SPEED, j, 8 * z : 8 * z + 8, :] = ux
        labels[j, 8 * z : 8 * z + 8, :] = jnp.where(mask_ref[here] != 0, rotor_ref[here], EMPTY)

    collide(f, state, keep_speed)

    def edge(read):
        block = jnp.zeros((8, 128), jnp.float32)
        inner = block
        for z in range(LEVELS):
            moved = roll(jnp.where(lanes < 64, read(z, 0), read(z, 1)), 16 * z + 8, 1)
            block = jnp.where(lanes // 16 == z, moved, block)
            wanted = jnp.logical_or(((lanes - 16 * z + 2) & 127) < 2, ((lanes - 16 * z - 16) & 127) < 2)
            inner = jnp.where(wanted, moved, inner)
        return block, inner

    pairs = [edge(lambda z, j, n=n: state[n, j, 8 * z : 8 * z + 8, :]) for n in range(10)]
    pairs.append(edge(lambda z, j: labels[j, 8 * z : 8 * z + 8, :].astype(jnp.float32)))
    pairs.append(edge(lambda z, j: state[SPEED, j, 8 * z : 8 * z + 8, :]))
    blocks = [block for block, _ in pairs]
    inner_label, inner_speed = pairs[LABEL][1], pairs[LABEL + 1][1]
    for n, block in enumerate(blocks):
        edges[n] = block
    low = (lanes & 8) == 0
    send = Paired("gy", to_even, to_odd).put

    for n in range(6):
        one, other = blocks[2 * n], blocks[2 * n + 1]
        send(n, jnp.where(low, one, roll(other, 8, 1)), jnp.where(low, roll(other, -8, 1), one))
    column = lanes & 15
    send(
        6,
        jnp.where(column >= 14, inner_speed, jnp.where(column >= 12, roll(inner_label, -2, 1), float(EMPTY))),
        jnp.where(column < 2, inner_speed, jnp.where(column < 4, roll(inner_label, 2, 1), float(EMPTY))),
    )
    others[2].wait()
    others[3].wait()
    for place, source in ((7, bottom), (8, top)):
        upward = jnp.zeros((8, 128), jnp.float32)
        downward = upward
        for n in range(9):
            both = jnp.where(lanes < 64, source[n, :, 0:128], source[n, :, 128:256])
            moved = roll(both, 8 * n + 8, 1)
            upward = jnp.where(lanes // 8 == n, moved, upward)
            downward = jnp.where(lanes // 8 == n + 1, moved, downward)
        send(place, upward, downward)


class Paired:
    def __init__(self, axis, even, odd):
        self.next_first = lax.rem(lax.axis_index(axis), 2) == 0
        self.refs = (even, odd)

    def put(self, n, to_next, to_previous):
        even, odd = self.refs
        even[n] = jnp.where(self.next_first, to_next, to_previous)
        odd[n] = jnp.where(self.next_first, to_previous, to_next)

    def received(self):
        even, odd = self.refs
        return Chosen(self.next_first, odd, even), Chosen(self.next_first, even, odd)


class Chosen:
    def __init__(self, flag, one, other):
        self.flag, self.one, self.other = flag, one, other

    def __getitem__(self, n):
        return jnp.where(self.flag, self.one[n], self.other[n])


def rows_of(blocks, row):
    rows = iota(0)
    out = jnp.broadcast_to(blocks[0][row : row + 1], (8, 128))
    for n in range(1, len(blocks)):
        out = jnp.where(rows == n, jnp.broadcast_to(blocks[n][row : row + 1], (8, 128)), out)
    return out


def edge_rows(state, sent):
    slot = 0
    for index in X_FIELDS:
        for j in range(2):
            sent.put(slot, *(state[index, j, pl.ds(row, 8, stride=8), :] for row in (7, 0)))
            slot += 1
    return slot


def relay_kernel(state, labels, edges, own_sums, even, odd, domains, to_even, to_odd, column_sums, beside):
    below, above = ([chosen[n] for n in range(9)] for chosen in Paired("gy", even, odd).received())
    for side, message in enumerate((below, above)):
        for n in range(2):
            beside[side, n] = message[7 + n]
    low = (iota(1) & 8) == 0
    for n in range(12):
        under, over = below[n // 2], above[n // 2]
        if n % 2:
            under, over = roll(under, -8, 1), roll(over, 8, 1)
        domains[0, n] = jnp.where(low, under, edges[n])
        domains[1, n] = jnp.where(low, edges[n], over)
    column = iota(1) & 15
    inner = jnp.where(
        column >= 14, roll(below[6], 2, 1), jnp.where(column < 2, roll(above[6], -2, 1), float(EMPTY))
    )
    sums = own_sums[...] + rotor_sums(
        [index_of(beside_tile(domains, LABEL)), index_of(inner)],
        [beside_tile(domains, LABEL + 1), jnp.where(column >= 8, below[6], above[6])],
    )
    column_sums[...] = sums
    sent = Paired("gx", to_even, to_odd)
    slot = edge_rows(state, sent)
    for j in range(2):
        sent.put(slot + j, *(labels[j, pl.ds(row, 8, stride=8), :].astype(jnp.float32) for row in (7, 0)))
    ends = [
        jnp.where(column < 9, domains[0, n], roll(domains[1, n], 2, 1)) for n in X_FIELDS + (LABEL,)
    ]
    sent.put(slot + 2, rows_of(ends, 7), rows_of(ends, 0))
    sent.put(slot + 3, sums, sums)


look_up = take


def index_of(mark):
    return jnp.clip(mark, 0.0, float(EMPTY)).astype(jnp.int32)


def slot_value(d, parts, along_y, along_z, a, b, c):
    value = parts[a] * along_y[b] * along_z[c]
    ones = (a == 1) + (b == 1) + (c == 1)
    if ones == 3:
        return value - (d[DXX] + d[DYY] + d[DZZ])
    if ones == 2:
        return value + 0.5 * (d[DXX] if a != 1 else d[DYY] if b != 1 else d[DZZ])
    if ones == 1 and c == 1:
        return value + (0.25 * (a - 1) * (b - 1)) * d[DXY]
    if ones == 1 and b == 1:
        return value + (0.25 * (a - 1) * (c - 1)) * d[DXZ]
    if ones == 1:
        return value + (0.25 * (b - 1) * (c - 1)) * d[DYZ]
    return value


def entering(table, fields, mark, a):
    rho, vx, vy, vz, dxx, dxy, dxz = fields
    part = rho * shapes(vx - look_up(table, mark))[a]
    d = {DXX: dxx, DXY: dxy, DXZ: dxz}
    along_y, along_z = shapes(vy), shapes(vz)
    return {(b, c): slot_value(d, {a: part}, along_y, along_z, a, b, c) for b in range(3) for c in range(3)}


def shift_rows(value, a, before, after):
    if a == 2:
        return jnp.where(iota(0) == 0, before, roll(value, 1, 0))
    if a == 0:
        return jnp.where(iota(0) == 7, after, roll(value, -1, 0))
    return value


def row_blocks(block, count):
    return [jnp.broadcast_to(block[n : n + 1], (8, 128)) for n in range(count)]


def step_domain(table, side, domains, left, right, beside):
    lanes = iota(1)
    d = [domains[side, n] for n in range(10)]
    thrust = look_up(table, index_of(domains[side, LABEL]))
    parts = [d[RHO] * h for h in shapes(d[VX] - thrust)]
    along_y, along_z = shapes(d[VY]), shapes(d[VZ])
    n = 2 * len(X_FIELDS) + 2
    outer = {}
    for a, message in ((2, left), (0, right)):
        fields = row_blocks(roll(message[n], -2 * side, 1), 8)
        outer[a] = entering(table, fields[:7], index_of(fields[7]), a)
    new = {}
    for a in range(3):
        for b in range(3):
            for c in range(3):
                value = slot_value(d, parts, along_y, along_z, a, b, c)
                value = shift_rows(value, a, outer[2][b, c], outer[0][b, c])
                value = roll(value, b - 1, 1)
                slot = 3 * a + b
                if c == 2:
                    value = jnp.where(lanes < 16, roll(beside[side, 0], -8 * slot, 1), roll(value, 16, 1))
                elif c == 0:
                    value = jnp.where(lanes >= 112, roll(beside[side, 1], 112 - 8 * slot, 1), roll(value, -16, 1))
                new[a, b, c] = value
    return outer, new


def strip_corners(table, message, a):
    even = (iota(1) & 1) == 0
    rho, vx, vy, vz, _, dxy, _, mark = row_blocks(message[2 * len(X_FIELDS)], 8)
    along_y, along_z = shapes(vy), shapes(vz)
    part = rho * shapes(vx - look_up(table, index_of(mark)))[a] * jnp.where(even, along_y[2], along_y[0])
    slots = [part * along_z[c] for c in range(3)]
    slots[1] = slots[1] + ((a - 1) * jnp.where(even, 0.25, -0.25)) * dxy
    return slots


def merged_strip(left_end, right_end):
    return jnp.where((iota(1) & 1) == 0, roll(left_end, 1, 1), roll(right_end, -1, 1))


def shift_columns(first, second, b, inflow):
    lanes = iota(1)
    if b == 2:
        first, second = roll(first, 1, 1), roll(second, 1, 1)
        return jnp.where(lanes == 0, inflow, first), jnp.where(lanes == 0, first, second)
    if b == 0:
        first, second = roll(first, -1, 1), roll(second, -1, 1)
        return jnp.where(lanes == 127, second, first), jnp.where(lanes == 127, inflow, second)
    return first, second


def prepare(state, labels, strip, moved, moved_labels):
    even = (iota(1) & 1) == 0
    rho, vx, vy, vz, dyy, dxy, dyz, mark = strip
    sign = jnp.where(even, 0.25, -0.25)
    along_y, along_z = shapes(vy), shapes(vz)
    part = rho * jnp.where(even, along_y[2], along_y[0])
    outside = [vx] + [part * h for h in along_z] + [0.5 * dyy, sign * dyz, sign * dxy, mark]
    for z in range(LEVELS):
        inflow = [roll(block, -16 * z - 8, 1) for block in outside]
        tiles = []
        for j in range(2):
            d = [state[n, j, 8 * z : 8 * z + 8, :] for n in range(10)]
            mark = labels[j, 8 * z : 8 * z + 8, :].astype(jnp.float32)
            along_y, along_z = shapes(d[VY]), shapes(d[VZ])
            rows = [d[RHO] * h for h in along_y]
            tiles.append((d, mark, rows, along_z))
        for b in range(3):
            kept = []
            for d, mark, rows, along_z in tiles:
                if b == 1:
                    terms = [-(d[DXX] + d[DYY] + d[DZZ]), 0.5 * d[DZZ], 0.5 * d[DXX], mark, 0.25 * d[DXZ]]
                else:
                    terms = [0.5 * d[DYY], (0.25 * (b - 1)) * d[DYZ], (0.25 * (b - 1)) * d[DXY], mark]
                kept.append([d[VX]] + [rows[b] * h for h in along_z] + terms)
            if b != 1:
                pairs = [shift_columns(*pair) for pair in zip(*kept, [b] * 8, inflow)]
                kept = list(zip(*pairs))
            for j, fields in enumerate(kept):
                for a in range(3):
                    place = 3 * a + b
                    chosen = list(fields[:4])
                    if a == 1:
                        chosen += [fields[4], fields[5], fields[7]]
                    elif b == 1:
                        chosen += [fields[6], (a - 1) * fields[8], fields[7]]
                    else:
                        chosen += [(a - 1) * fields[6], None, fields[7]]
                    for n, value in enumerate(chosen):
                        if value is None:
                            continue
                        value = roll(value, a - 1, 0)
                        if n == 6:
                            moved_labels[place, j, z] = value.astype(jnp.int32)
                        else:
                            moved[place, n, j, z] = value


def first_prepare_kernel(state, labels, domains, moved, moved_labels):
    strip = [merged_strip(domains[0, n], domains[1, n]) for n in Y_FIELDS + (LABEL,)]
    prepare(state, labels, strip, moved, moved_labels)


def last_prepare_kernel(state, labels, strip, moved, moved_labels):
    prepare(state, labels, [strip[n] for n in range(8)], moved, moved_labels)


def streamed(table, moved, moved_labels, left, right, left_marks, right_marks, corners, bottom, top, ghost):
    rows = iota(0)
    for side, (source, marks) in enumerate(((left, left_marks), (right, right_marks))):
        a = 2 - 2 * side
        halves = [
            entering(table, [source[2 * n + j] for n in range(len(X_FIELDS))], marks(j), a) for j in range(2)
        ]
        for b in range(3):
            for c in range(3):
                inflow = None if b == 1 else take(corners[side][b, c], 16 * rows + (8 if b == 2 else 7))
                pair = shift_columns(halves[0][b, c], halves[1][b, c], b, inflow)
                for j in range(2):
                    ghost[side, 3 * b + c, j] = pair[j]

    @functools.cache
    def along_x(place, j, z):
        return shapes(moved[place, 0, j, z] - look_up(table, moved_labels[place, j, z]))[place // 3]

    def slot(level, j, a, b, c):
        z, place = level + 1 - c, 3 * a + b
        if z < 0 or z >= LEVELS:
            return (bottom if z < 0 else top)[place, :, 128 * j : 128 * j + 128]
        value = moved[place, 1 + c, j, z] * along_x(place, j, z)
        if c == 1:
            value = value + moved[place, 4, j, z]
        elif a == 1 and b == 1:
            value = value + moved[place, 5, j, z]
        elif a == 1 or b == 1:
            value = value + (c - 1) * moved[place, 5, j, z]
        if a == 2:
            return jnp.where(rows == 0, ghost[0, 3 * b + c, j, z : z + 1, :], value)
        if a == 0:
            return jnp.where(rows == 7, ghost[1, 3 * b + c, j, z : z + 1, :], value)
        return value

    return slot


def disk_table(sums, counts):
    disk = sums / jnp.maximum(counts, 1.0)
    return jnp.where(iota(1) < ROTORS, THRUST_GAIN * disk * jnp.abs(disk), 0.0)


def marks_of(message):
    return lambda j: message[2 * len(X_FIELDS) + j].astype(jnp.int32)


def middle_kernel(
    moved, moved_labels, domains, column_sums, beside, starts, found, found_beside, even, odd, bottom, top,
    new_state, to_even, to_odd, strip, counts, sums_out, ghost, speeds,
):
    lanes = iota(1)
    left, right = Paired("gx", even, odd).received()
    last = 2 * len(X_FIELDS) + 3
    totals = column_sums[...] + left[last] + right[last]
    seen = roll(totals, 64, 1)
    counts[...] = seen
    table = disk_table(totals, seen)

    outside, kept, corners = [], [], [{}, {}]
    for side in range(2):
        outer, new = step_domain(table, side, domains, left, right, beside)
        ux, fields = relax(low_moments(lambda a, b, c: new[a, b, c]))
        outside.append(ux)
        kept.append([fields[n] for n in Y_FIELDS] + [domains[side, LABEL]])
        b = 2 - 2 * side
        for c in range(3):
            for row, a in ((0, 2), (1, 0)):
                corners[row][b, c] = roll(outer[a][b, c], b - 1, 1)
    strips = [merged_strip(one, other) for one, other in zip(*kept)]
    for n, block in enumerate(strips):
        strip[n] = block
    f = streamed(
        table, moved, moved_labels, left, right, marks_of(left), marks_of(right), corners, bottom, top, ghost
    )

    def keep_speed(z, j, ux):
        speeds[j, z] = ux

    collide(f, new_state, keep_speed)
    sums = found_sums(
        lambda z, j: speeds[j, z],
        jnp.where((lanes & 8) == 0, outside[0], outside[1]),
        starts, found, found_beside,
    )
    sums_out[...] = sums
    sent = Paired("gx", to_even, to_odd)
    slot = edge_rows(new_state, sent)
    sent.put(slot, rows_of(strips, 7), rows_of(strips, 0))
    sent.put(slot + 1, sums, sums)


def last_kernel(
    moved, moved_labels, sums, counts, even, odd, old_even, old_odd, bottom, top, out_hbm, out, ghost, gone
):
    left, right = Paired("gx", even, odd).received()
    old_left, old_right = Paired("gx", old_even, old_odd).received()
    last = 2 * len(X_FIELDS) + 1
    totals = sums[...] + left[last] + right[last]
    table = disk_table(totals, counts[...])
    corners = [
        {(b, c): value for c, value in enumerate(strip_corners(table, message, a)) for b in (0, 2)}
        for message, a in ((left, 2), (right, 0))
    ]
    copies = [pltpu.make_async_copy(out.at[:, z], out_hbm.at[:, z], gone.at[z]) for z in range(LEVELS)]
    f = streamed(
        table, moved, moved_labels, left, right, marks_of(old_left), marks_of(old_right), corners, bottom, top, ghost
    )
    for z in range(LEVELS):
        for j in range(2):
            for slot in range(27):
                out[slot, z, :, 128 * j : 128 * j + 128] = f(z, j, slot // 9, slot // 3 % 3, slot % 3)
        copies[z].start()
    for copy in copies:
        copy.wait()


def call(kernel, inputs, outputs, scratch=(), in_hbm=0, out_hbm=0, copies=0):
    inputs = [pltpu.with_memory_space_constraint(x, pltpu.HBM) if n < in_hbm else x for n, x in enumerate(inputs)]

    def specs(count, outside):
        return [pl.BlockSpec(memory_space=pltpu.HBM if n < outside else pltpu.VMEM) for n in range(count)]

    return pl.pallas_call(
        kernel,
        out_shape=[jax.ShapeDtypeStruct(shape, dtype) for shape, dtype in outputs],
        in_specs=specs(len(inputs), in_hbm),
        out_specs=specs(len(outputs), out_hbm),
        scratch_shapes=[pltpu.VMEM(shape, dtype) for shape, dtype in scratch]
        + ([pltpu.SemaphoreType.DMA((copies,))] if copies else []),
        compiler_params=pltpu.CompilerParams(vmem_limit_bytes=VMEM_LIMIT),
    )(*inputs)


def swapped(even, odd, axis):
    count = lax.axis_size(axis)

    def pairs(start):
        there = [(i, (i + 1) % count) for i in range(start, count, 2)]
        return there + [(j, i) for i, j in there]

    return lax.ppermute(even, axis, pairs(0)), lax.ppermute(odd, axis, pairs(1))


def body(populations, bottom_in, top_in, turbine_mask, rotor_index):
    f32 = jnp.float32
    state_shape = ((10, 2, 64, 128), f32)
    one = ((8, 128), f32)
    ghost = ((2, 9, 2, 8, 128), f32)
    inflow = (bottom_in.shape, f32)
    cells = (turbine_mask.shape, jnp.int32)
    whole = (populations.shape, f32)
    n = 2 * len(X_FIELDS)

    def blocks(*count):
        return (count + (8, 128), f32)

    state, labels, edges, to_even, to_odd = call(
        first_kernel,
        (populations, turbine_mask, rotor_index, bottom_in, top_in),
        (((11, 2, 64, 128), f32), ((2, 64, 128), jnp.int32), blocks(12), blocks(9), blocks(9)),
        (whole, cells, cells, inflow, inflow),
        in_hbm=5,
        copies=LEVELS + 4,
    )
    even, odd = swapped(to_even, to_odd, "gy")
    (own_sums,) = call(sums_kernel, (state, labels), (one,))
    domains, to_even, to_odd, column_sums, beside = call(
        relay_kernel,
        (state, labels, edges, own_sums, even, odd),
        (blocks(2, 12), blocks(n + 4), blocks(n + 4), one, blocks(2, 2)),
    )
    old_even, old_odd = swapped(to_even, to_odd, "gx")
    starts, found, found_beside = call(
        places_kernel,
        (labels, domains),
        (((2, 8, 128), jnp.int32), blocks(SPAN, 2, LEVELS), blocks(SPAN, LEVELS)),
    )
    shifted = (blocks(9, 6, 2, LEVELS), ((9, 2, LEVELS, 8, 128), jnp.int32))
    moved, moved_labels = call(first_prepare_kernel, (state, labels, domains), shifted)
    state, to_even, to_odd, strip, counts, sums = call(
        middle_kernel,
        (
            moved, moved_labels, domains, column_sums, beside, starts, found, found_beside,
            old_even, old_odd, bottom_in, top_in,
        ),
        (state_shape, blocks(n + 2), blocks(n + 2), blocks(8), one, one),
        (ghost, blocks(2, LEVELS)),
    )
    even, odd = swapped(to_even, to_odd, "gx")
    moved, moved_labels = call(last_prepare_kernel, (state, labels, strip), shifted)
    (out,) = call(
        last_kernel,
        (moved, moved_labels, sums, counts, even, odd, old_even, old_odd, bottom_in, top_in),
        (whole,),
        (whole, ghost),
        out_hbm=1,
        copies=LEVELS,
    )
    return out


def solution(mesh):
    placed = (
        P(None, None, "gx", "gy"),
        P(None, "gx", "gy"),
        P(None, "gx", "gy"),
        P(None, "gx", "gy"),
        P(None, "gx", "gy"),
    )
    return jax.shard_map(
        body, mesh=mesh, in_specs=placed, out_specs=P(None, None, "gx", "gy"), check_vma=False
    )
```

```python
import functools

import jax
import jax.numpy as jnp
from jax import lax
from jax.experimental import pallas as pl
from jax.experimental.pallas import tpu as pltpu
from jax.sharding import PartitionSpec as P

ROTORS = 64
SOUND = 1.0 / 3.0
TAU_BASE = 0.52
SMAG_GAIN = 5.0
CORIOLIS = 0.05
GEO_U = 0.08
THRUST_GAIN = 4.0
EMPTY = 127
LEVELS = 8
VMEM_LIMIT = 24 * 1024 * 1024

RHO, VX, VY, VZ, DXX, DYY, DZZ, DXY, DXZ, DYZ = range(10)
SPEED = 10
LABEL = 10
SPAN = 5
X_FIELDS = (RHO, VX, VY, VZ, DXX, DXY, DXZ)
Y_FIELDS = (RHO, VX, VY, VZ, DYY, DXY, DYZ)


def iota(axis):
    return lax.broadcasted_iota(jnp.int32, (8, 128), axis)


def roll(block, shift, axis):
    size = block.shape[axis]
    return pltpu.roll(block, shift % size, axis) if shift % size else block


def low_moments(f):
    along_z = {}
    for a in range(3):
        for b in range(3):
            low, mid, high = f(a, b, 0), f(a, b, 1), f(a, b, 2)
            ends = low + high
            along_z[a, b] = (ends + mid, high - low, ends)
    slabs = []
    for a in range(3):
        (l0, l1, l2), (m0, m1, m2), (h0, h1, h2) = (along_z[a, b] for b in range(3))
        ends = l0 + h0
        slabs.append((ends + m0, h0 - l0, ends, l1 + m1 + h1, h1 - l1, l2 + m2 + h2))
    low, mid, high = slabs
    ends = low[0] + high[0]
    return {
        "0": ends + mid[0],
        "x": high[0] - low[0],
        "xx": ends,
        "y": low[1] + mid[1] + high[1],
        "xy": high[1] - low[1],
        "yy": low[2] + mid[2] + high[2],
        "z": low[3] + mid[3] + high[3],
        "xz": high[3] - low[3],
        "yz": low[4] + mid[4] + high[4],
        "zz": low[5] + mid[5] + high[5],
    }


def relax(m):
    rho = m["0"]
    inverse = 1.0 / rho
    ux, uy, uz = m["x"] * inverse, m["y"] * inverse, m["z"] * inverse
    third = rho * SOUND
    qxx = m["xx"] - (m["x"] * ux + third)
    qyy = m["yy"] - (m["y"] * uy + third)
    qzz = m["zz"] - (m["z"] * uz + third)
    qxy = m["xy"] - m["x"] * uy
    qxz = m["xz"] - m["x"] * uz
    qyz = m["yz"] - m["y"] * uz
    strain = qxx * qxx + qyy * qyy + qzz * qzz + 2.0 * (qxy * qxy + qxz * qxz + qyz * qyz)
    keep = 1.0 - 1.0 / (TAU_BASE + SMAG_GAIN * jnp.sqrt(strain))
    vx = ux + CORIOLIS * uy
    vy = uy - CORIOLIS * (ux - GEO_U)
    fields = [rho, vx, vy, uz] + [keep * q for q in (qxx, qyy, qzz, qxy, qxz, qyz)]
    return ux, fields


def shapes(speed):
    square = speed * speed + SOUND
    return (0.5 * (square - speed), 1.0 - square, 0.5 * (square + speed))


def over_rows(block, join=jnp.add):
    for shift in (4, 2, 1):
        block = join(block, roll(block, shift, 0))
    return block


def spread(leaf, join=jnp.add):
    lanes = iota(1)

    def node(stride, ways, rest, index):
        parts = [(node(*rest, index + d * stride) if rest else leaf(index + d * stride)) for d in range(ways)]
        digit = (lanes // stride) % ways
        moved = []
        for k in range(ways):
            picked = parts[k]
            for d in range(1, ways):
                picked = jnp.where(digit == d, parts[(d + k) % ways], picked)
            moved.append(roll(picked, k * stride, 1))
        return functools.reduce(join, moved)

    return over_rows(node(16, 8, (2, 8, (1, 2, ())), 0), join)


def rotor_sums(labels, speeds):
    def leaf(index):
        rotor, counting = index % ROTORS, index >= ROTORS
        total = jnp.zeros((8, 128), jnp.float32)
        for label, speed in zip(labels, speeds):
            total = total + jnp.where(label == rotor, 1.0 if counting else speed, 0.0)
        return total

    return spread(leaf)


def take(block, index):
    return jnp.take_along_axis(block, index, axis=1, mode="promise_in_bounds")


def sums_kernel(state, labels, own_sums):
    places = [(j, z) for j in range(2) for z in range(LEVELS)]
    own_sums[...] = rotor_sums(
        [labels[j, 8 * z : 8 * z + 8, :] for j, z in places],
        [state[SPEED, j, 8 * z : 8 * z + 8, :] for j, z in places],
    )


def beside_tile(domains, n):
    return jnp.where((iota(1) & 8) == 0, domains[0, n], domains[1, n])


def places_kernel(labels, domains, starts, found, found_beside):
    lanes = iota(1)
    far = 1024.0
    column = lanes & 15
    near = jnp.logical_and(column >= 3, column < 13)
    outside = jnp.where(near, index_of(beside_tile(domains, LABEL)), EMPTY)
    inside = {(j, z): labels[j, 8 * z : 8 * z + 8, :] for j in range(2) for z in range(LEVELS)}

    def leaf(index):
        rotor = index % ROTORS
        if index >= ROTORS:
            return jnp.where(outside == rotor, column.astype(jnp.float32), far)
        first = jnp.full((8, 128), far, jnp.float32)
        for j in range(2):
            hit = inside[j, 0] == rotor
            for z in range(1, LEVELS):
                hit = jnp.logical_or(hit, inside[j, z] == rotor)
            first = jnp.minimum(first, jnp.where(hit, (lanes + 128 * j).astype(jnp.float32), far))
        return first

    both = spread(leaf, jnp.minimum)
    begin = (jnp.where(both < far, both, 0.0)).astype(jnp.int32)
    begin_beside = roll(begin.astype(jnp.float32), 64, 1).astype(jnp.int32)
    starts[0] = begin
    starts[1] = begin_beside
    own = jnp.where(lanes < ROTORS, lanes, -1)
    for k in range(SPAN):
        index = (begin + k) & 127
        for z in range(LEVELS):
            for j in range(2):
                found[k, j, z] = jnp.where(take(inside[j, z], index) == own, 1.0, 0.0)
            index_beside = (begin_beside + (k + 16 * z)) & 127
            found_beside[k, z] = jnp.where(take(outside, index_beside) == own, 1.0, 0.0)


def found_sums(speed, speed_beside, starts, found, found_beside):
    total = jnp.zeros((8, 128), jnp.float32)
    for k in range(SPAN):
        index = (starts[0] + k) & 127
        for z in range(LEVELS):
            for j in range(2):
                total = total + jnp.where(found[k, j, z] > 0.0, take(speed(z, j), index), 0.0)
            index_beside = (starts[1] + (k + 16 * z)) & 127
            total = total + jnp.where(found_beside[k, z] > 0.0, take(speed_beside, index_beside), 0.0)
    return over_rows(total)


def collide(f, state, keep_speed):
    for z in range(LEVELS):
        for j in range(2):
            ux, fields = relax(low_moments(functools.partial(f, z, j)))
            for index, value in enumerate(fields):
                state[index, j, 8 * z : 8 * z + 8, :] = value
            keep_speed(z, j, ux)


def first_kernel(
    f_hbm, mask_hbm, rotor_hbm, bottom_hbm, top_hbm, state, labels, edges, to_even, to_odd,
    f_ref, mask_ref, rotor_ref, bottom, top, arrived,
):
    lanes = iota(1)
    levels = [pltpu.make_async_copy(f_hbm.at[:, z], f_ref.at[:, z], arrived.at[z]) for z in range(LEVELS)]
    others = [
        pltpu.make_async_copy(source, target, arrived.at[LEVELS + n])
        for n, (source, target) in enumerate(
            ((mask_hbm, mask_ref), (rotor_hbm, rotor_ref), (bottom_hbm, bottom), (top_hbm, top))
        )
    ]
    for copy in others + levels:
        copy.start()
    for copy in others:
        copy.wait()
    send = Paired("gy", to_even, to_odd).put
    for place, source in ((7, bottom), (8, top)):
        upward = jnp.zeros((8, 128), jnp.float32)
        downward = upward
        for n in range(9):
            both = jnp.where(lanes < 64, source[n, :, 0:128], source[n, :, 128:256])
            moved = roll(both, 8 * n + 8, 1)
            upward = jnp.where(lanes // 8 == n, moved, upward)
            downward = jnp.where(lanes // 8 == n + 1, moved, downward)
        send(place, upward, downward)
    waiting = list(levels)

    def f(z, j, a, b, c):
        if len(waiting) == LEVELS - z:
            waiting.pop(0).wait()
        return f_ref[9 * a + 3 * b + c, z, :, 128 * j : 128 * j + 128]

    def keep_speed(z, j, ux):
        here = (z, slice(None), slice(128 * j, 128 * j + 128))
        state[SPEED, j, 8 * z : 8 * z + 8, :] = ux
        labels[j, 8 * z : 8 * z + 8, :] = jnp.where(mask_ref[here] != 0, rotor_ref[here], EMPTY)

    collide(f, state, keep_speed)

    def edge(read):
        block = jnp.zeros((8, 128), jnp.float32)
        inner = block
        for z in range(LEVELS):
            moved = roll(jnp.where(lanes < 64, read(z, 0), read(z, 1)), 16 * z + 8, 1)
            block = jnp.where(lanes // 16 == z, moved, block)
            wanted = jnp.logical_or(((lanes - 16 * z + 2) & 127) < 2, ((lanes - 16 * z - 16) & 127) < 2)
            inner = jnp.where(wanted, moved, inner)
        return block, inner

    pairs = [edge(lambda z, j, n=n: state[n, j, 8 * z : 8 * z + 8, :]) for n in range(10)]
    pairs.append(edge(lambda z, j: labels[j, 8 * z : 8 * z + 8, :].astype(jnp.float32)))
    pairs.append(edge(lambda z, j: state[SPEED, j, 8 * z : 8 * z + 8, :]))
    blocks = [block for block, _ in pairs]
    inner_label, inner_speed = pairs[LABEL][1], pairs[LABEL + 1][1]
    for n, block in enumerate(blocks):
        edges[n] = block
    low = (lanes & 8) == 0

    for n in range(6):
        one, other = blocks[2 * n], blocks[2 * n + 1]
        send(n, jnp.where(low, one, roll(other, 8, 1)), jnp.where(low, roll(other, -8, 1), one))
    column = lanes & 15
    send(
        6,
        jnp.where(column >= 14, inner_speed, jnp.where(column >= 12, roll(inner_label, -2, 1), float(EMPTY))),
        jnp.where(column < 2, inner_speed, jnp.where(column < 4, roll(inner_label, 2, 1), float(EMPTY))),
    )


class Paired:
    def __init__(self, axis, even, odd):
        self.next_first = lax.rem(lax.axis_index(axis), 2) == 0
        self.refs = (even, odd)

    def put(self, n, to_next, to_previous):
        even, odd = self.refs
        even[n] = jnp.where(self.next_first, to_next, to_previous)
        odd[n] = jnp.where(self.next_first, to_previous, to_next)

    def received(self):
        even, odd = self.refs
        return Chosen(self.next_first, odd, even), Chosen(self.next_first, even, odd)


class Chosen:
    def __init__(self, flag, one, other):
        self.flag, self.one, self.other = flag, one, other

    def __getitem__(self, n):
        return jnp.where(self.flag, self.one[n], self.other[n])


def rows_of(blocks, row):
    rows = iota(0)
    out = jnp.broadcast_to(blocks[0][row : row + 1], (8, 128))
    for n in range(1, len(blocks)):
        out = jnp.where(rows == n, jnp.broadcast_to(blocks[n][row : row + 1], (8, 128)), out)
    return out


def edge_rows(state, sent):
    slot = 0
    for index in X_FIELDS:
        for j in range(2):
            sent.put(slot, *(state[index, j, pl.ds(row, 8, stride=8), :] for row in (7, 0)))
            slot += 1
    return slot


def relay_kernel(state, labels, edges, own_sums, even, odd, domains, to_even, to_odd, column_sums, beside):
    below, above = ([chosen[n] for n in range(9)] for chosen in Paired("gy", even, odd).received())
    for side, message in enumerate((below, above)):
        for n in range(2):
            beside[side, n] = message[7 + n]
    low = (iota(1) & 8) == 0
    for n in range(12):
        under, over = below[n // 2], above[n // 2]
        if n % 2:
            under, over = roll(under, -8, 1), roll(over, 8, 1)
        domains[0, n] = jnp.where(low, under, edges[n])
        domains[1, n] = jnp.where(low, edges[n], over)
    column = iota(1) & 15
    inner = jnp.where(
        column >= 14, roll(below[6], 2, 1), jnp.where(column < 2, roll(above[6], -2, 1), float(EMPTY))
    )
    sums = own_sums[...] + rotor_sums(
        [index_of(beside_tile(domains, LABEL)), index_of(inner)],
        [beside_tile(domains, LABEL + 1), jnp.where(column >= 8, below[6], above[6])],
    )
    column_sums[...] = sums
    sent = Paired("gx", to_even, to_odd)
    slot = edge_rows(state, sent)
    for j in range(2):
        sent.put(slot + j, *(labels[j, pl.ds(row, 8, stride=8), :].astype(jnp.float32) for row in (7, 0)))
    ends = [
        jnp.where(column < 9, domains[0, n], roll(domains[1, n], 2, 1)) for n in X_FIELDS + (LABEL,)
    ]
    sent.put(slot + 2, rows_of(ends, 7), rows_of(ends, 0))
    sent.put(slot + 3, sums, sums)


look_up = take


def index_of(mark):
    return jnp.clip(mark, 0.0, float(EMPTY)).astype(jnp.int32)


def slot_value(d, parts, along_y, along_z, a, b, c):
    value = parts[a] * along_y[b] * along_z[c]
    ones = (a == 1) + (b == 1) + (c == 1)
    if ones == 3:
        return value - (d[DXX] + d[DYY] + d[DZZ])
    if ones == 2:
        return value + 0.5 * (d[DXX] if a != 1 else d[DYY] if b != 1 else d[DZZ])
    if ones == 1 and c == 1:
        return value + (0.25 * (a - 1) * (b - 1)) * d[DXY]
    if ones == 1 and b == 1:
        return value + (0.25 * (a - 1) * (c - 1)) * d[DXZ]
    if ones == 1:
        return value + (0.25 * (b - 1) * (c - 1)) * d[DYZ]
    return value


def entering(table, fields, mark, a):
    rho, vx, vy, vz, dxx, dxy, dxz = fields
    part = rho * shapes(vx - look_up(table, mark))[a]
    d = {DXX: dxx, DXY: dxy, DXZ: dxz}
    along_y, along_z = shapes(vy), shapes(vz)
    return {(b, c): slot_value(d, {a: part}, along_y, along_z, a, b, c) for b in range(3) for c in range(3)}


def shift_rows(value, a, before, after):
    if a == 2:
        return jnp.where(iota(0) == 0, before, roll(value, 1, 0))
    if a == 0:
        return jnp.where(iota(0) == 7, after, roll(value, -1, 0))
    return value


def row_blocks(block, count):
    return [jnp.broadcast_to(block[n : n + 1], (8, 128)) for n in range(count)]


def step_domain(table, side, domains, left, right, beside):
    lanes = iota(1)
    d = [domains[side, n] for n in range(10)]
    thrust = look_up(table, index_of(domains[side, LABEL]))
    parts = [d[RHO] * h for h in shapes(d[VX] - thrust)]
    along_y, along_z = shapes(d[VY]), shapes(d[VZ])
    n = 2 * len(X_FIELDS) + 2
    outer = {}
    for a, message in ((2, left), (0, right)):
        fields = row_blocks(roll(message[n], -2 * side, 1), 8)
        outer[a] = entering(table, fields[:7], index_of(fields[7]), a)
    new = {}
    for a in range(3):
        for b in range(3):
            for c in range(3):
                value = slot_value(d, parts, along_y, along_z, a, b, c)
                value = shift_rows(value, a, outer[2][b, c], outer[0][b, c])
                value = roll(value, b - 1, 1)
                slot = 3 * a + b
                if c == 2:
                    value = jnp.where(lanes < 16, roll(beside[side, 0], -8 * slot, 1), roll(value, 16, 1))
                elif c == 0:
                    value = jnp.where(lanes >= 112, roll(beside[side, 1], 112 - 8 * slot, 1), roll(value, -16, 1))
                new[a, b, c] = value
    return outer, new


def strip_corners(table, message, a):
    even = (iota(1) & 1) == 0
    rho, vx, vy, vz, _, dxy, _, mark = row_blocks(message[2 * len(X_FIELDS)], 8)
    along_y, along_z = shapes(vy), shapes(vz)
    part = rho * shapes(vx - look_up(table, index_of(mark)))[a] * jnp.where(even, along_y[2], along_y[0])
    slots = [part * along_z[c] for c in range(3)]
    slots[1] = slots[1] + ((a - 1) * jnp.where(even, 0.25, -0.25)) * dxy
    return slots


def merged_strip(left_end, right_end):
    return jnp.where((iota(1) & 1) == 0, roll(left_end, 1, 1), roll(right_end, -1, 1))


def shift_columns(first, second, b, inflow):
    lanes = iota(1)
    if b == 2:
        first, second = roll(first, 1, 1), roll(second, 1, 1)
        return jnp.where(lanes == 0, inflow, first), jnp.where(lanes == 0, first, second)
    if b == 0:
        first, second = roll(first, -1, 1), roll(second, -1, 1)
        return jnp.where(lanes == 127, second, first), jnp.where(lanes == 127, inflow, second)
    return first, second


def prepare(state, labels, strip, moved, moved_labels):
    even = (iota(1) & 1) == 0
    rho, vx, vy, vz, dyy, dxy, dyz, mark = strip
    sign = jnp.where(even, 0.25, -0.25)
    along_y, along_z = shapes(vy), shapes(vz)
    part = rho * jnp.where(even, along_y[2], along_y[0])
    outside = [vx] + [part * h for h in along_z] + [0.5 * dyy, sign * dyz, sign * dxy, mark]
    for z in range(LEVELS):
        inflow = [roll(block, -16 * z - 8, 1) for block in outside]
        tiles = []
        for j in range(2):
            d = [state[n, j, 8 * z : 8 * z + 8, :] for n in range(10)]
            mark = labels[j, 8 * z : 8 * z + 8, :].astype(jnp.float32)
            along_y, along_z = shapes(d[VY]), shapes(d[VZ])
            rows = [d[RHO] * h for h in along_y]
            tiles.append((d, mark, rows, along_z))
        for b in range(3):
            kept = []
            for d, mark, rows, along_z in tiles:
                if b == 1:
                    terms = [-(d[DXX] + d[DYY] + d[DZZ]), 0.5 * d[DZZ], 0.5 * d[DXX], mark, 0.25 * d[DXZ]]
                else:
                    terms = [0.5 * d[DYY], (0.25 * (b - 1)) * d[DYZ], (0.25 * (b - 1)) * d[DXY], mark]
                kept.append([d[VX]] + [rows[b] * h for h in along_z] + terms)
            if b != 1:
                pairs = [shift_columns(*pair) for pair in zip(*kept, [b] * 8, inflow)]
                kept = list(zip(*pairs))
            for j, fields in enumerate(kept):
                for a in range(3):
                    place = 3 * a + b
                    chosen = list(fields[:4])
                    if a == 1:
                        chosen += [fields[4], fields[5], fields[7]]
                    elif b == 1:
                        chosen += [fields[6], (a - 1) * fields[8], fields[7]]
                    else:
                        chosen += [(a - 1) * fields[6], None, fields[7]]
                    for n, value in enumerate(chosen):
                        if value is None:
                            continue
                        value = roll(value, a - 1, 0)
                        if n == 6:
                            moved_labels[place, j, z] = value.astype(jnp.int32)
                        else:
                            moved[place, n, j, z] = value


def first_prepare_kernel(state, labels, domains, moved, moved_labels):
    strip = [merged_strip(domains[0, n], domains[1, n]) for n in Y_FIELDS + (LABEL,)]
    prepare(state, labels, strip, moved, moved_labels)


def last_prepare_kernel(state, labels, strip, moved, moved_labels):
    prepare(state, labels, [strip[n] for n in range(8)], moved, moved_labels)


def streamed(table, moved, moved_labels, left, right, left_marks, right_marks, corners, bottom, top, ghost):
    rows = iota(0)
    for side, (source, marks) in enumerate(((left, left_marks), (right, right_marks))):
        a = 2 - 2 * side
        halves = [
            entering(table, [source[2 * n + j] for n in range(len(X_FIELDS))], marks(j), a) for j in range(2)
        ]
        for b in range(3):
            for c in range(3):
                inflow = None if b == 1 else take(corners[side][b, c], 16 * rows + (8 if b == 2 else 7))
                pair = shift_columns(halves[0][b, c], halves[1][b, c], b, inflow)
                for j in range(2):
                    ghost[side, 3 * b + c, j] = pair[j]

    @functools.cache
    def along_x(place, j, z):
        return shapes(moved[place, 0, j, z] - look_up(table, moved_labels[place, j, z]))[place // 3]

    def slot(level, j, a, b, c):
        z, place = level + 1 - c, 3 * a + b
        if z < 0 or z >= LEVELS:
            return (bottom if z < 0 else top)[place, :, 128 * j : 128 * j + 128]
        value = moved[place, 1 + c, j, z] * along_x(place, j, z)
        if c == 1:
            value = value + moved[place, 4, j, z]
        elif a == 1 and b == 1:
            value = value + moved[place, 5, j, z]
        elif a == 1 or b == 1:
            value = value + (c - 1) * moved[place, 5, j, z]
        if a == 2:
            return jnp.where(rows == 0, ghost[0, 3 * b + c, j, z : z + 1, :], value)
        if a == 0:
            return jnp.where(rows == 7, ghost[1, 3 * b + c, j, z : z + 1, :], value)
        return value

    return slot


def disk_table(sums, counts):
    disk = sums / jnp.maximum(counts, 1.0)
    return jnp.where(iota(1) < ROTORS, THRUST_GAIN * disk * jnp.abs(disk), 0.0)


def marks_of(message):
    return lambda j: message[2 * len(X_FIELDS) + j].astype(jnp.int32)


def middle_kernel(
    moved, moved_labels, domains, column_sums, beside, starts, found, found_beside, even, odd, bottom, top,
    new_state, to_even, to_odd, strip, counts, sums_out, ghost, speeds,
):
    lanes = iota(1)
    left, right = Paired("gx", even, odd).received()
    last = 2 * len(X_FIELDS) + 3
    totals = column_sums[...] + left[last] + right[last]
    seen = roll(totals, 64, 1)
    counts[...] = seen
    table = disk_table(totals, seen)

    outside, kept, corners = [], [], [{}, {}]
    for side in range(2):
        outer, new = step_domain(table, side, domains, left, right, beside)
        ux, fields = relax(low_moments(lambda a, b, c: new[a, b, c]))
        outside.append(ux)
        kept.append([fields[n] for n in Y_FIELDS] + [domains[side, LABEL]])
        b = 2 - 2 * side
        for c in range(3):
            for row, a in ((0, 2), (1, 0)):
                corners[row][b, c] = roll(outer[a][b, c], b - 1, 1)
    strips = [merged_strip(one, other) for one, other in zip(*kept)]
    for n, block in enumerate(strips):
        strip[n] = block
    f = streamed(
        table, moved, moved_labels, left, right, marks_of(left), marks_of(right), corners, bottom, top, ghost
    )

    def keep_speed(z, j, ux):
        speeds[j, z] = ux

    collide(f, new_state, keep_speed)
    sums = found_sums(
        lambda z, j: speeds[j, z],
        jnp.where((lanes & 8) == 0, outside[0], outside[1]),
        starts, found, found_beside,
    )
    sums_out[...] = sums
    sent = Paired("gx", to_even, to_odd)
    slot = edge_rows(new_state, sent)
    sent.put(slot, rows_of(strips, 7), rows_of(strips, 0))
    sent.put(slot + 1, sums, sums)


def last_kernel(
    moved, moved_labels, sums, counts, even, odd, old_even, old_odd, bottom, top, out_hbm, out, ghost, gone
):
    left, right = Paired("gx", even, odd).received()
    old_left, old_right = Paired("gx", old_even, old_odd).received()
    last = 2 * len(X_FIELDS) + 1
    totals = sums[...] + left[last] + right[last]
    table = disk_table(totals, counts[...])
    corners = [
        {(b, c): value for c, value in enumerate(strip_corners(table, message, a)) for b in (0, 2)}
        for message, a in ((left, 2), (right, 0))
    ]
    copies = [pltpu.make_async_copy(out.at[:, z], out_hbm.at[:, z], gone.at[z]) for z in range(LEVELS)]
    f = streamed(
        table, moved, moved_labels, left, right, marks_of(old_left), marks_of(old_right), corners, bottom, top, ghost
    )
    for z in range(LEVELS):
        for j in range(2):
            for slot in range(27):
                out[slot, z, :, 128 * j : 128 * j + 128] = f(z, j, slot // 9, slot // 3 % 3, slot % 3)
        copies[z].start()
    for copy in copies:
        copy.wait()


def call(kernel, inputs, outputs, scratch=(), in_hbm=0, out_hbm=0, copies=0):
    inputs = [pltpu.with_memory_space_constraint(x, pltpu.HBM) if n < in_hbm else x for n, x in enumerate(inputs)]

    def specs(count, outside):
        return [pl.BlockSpec(memory_space=pltpu.HBM if n < outside else pltpu.VMEM) for n in range(count)]

    return pl.pallas_call(
        kernel,
        out_shape=[jax.ShapeDtypeStruct(shape, dtype) for shape, dtype in outputs],
        in_specs=specs(len(inputs), in_hbm),
        out_specs=specs(len(outputs), out_hbm),
        scratch_shapes=[pltpu.VMEM(shape, dtype) for shape, dtype in scratch]
        + ([pltpu.SemaphoreType.DMA((copies,))] if copies else []),
        compiler_params=pltpu.CompilerParams(vmem_limit_bytes=VMEM_LIMIT),
    )(*inputs)


def swapped(even, odd, axis):
    count = lax.axis_size(axis)

    def pairs(start):
        there = [(i, (i + 1) % count) for i in range(start, count, 2)]
        return there + [(j, i) for i, j in there]

    return lax.ppermute(even, axis, pairs(0)), lax.ppermute(odd, axis, pairs(1))


def body(populations, bottom_in, top_in, turbine_mask, rotor_index):
    f32 = jnp.float32
    state_shape = ((10, 2, 64, 128), f32)
    one = ((8, 128), f32)
    ghost = ((2, 9, 2, 8, 128), f32)
    inflow = (bottom_in.shape, f32)
    cells = (turbine_mask.shape, jnp.int32)
    whole = (populations.shape, f32)
    n = 2 * len(X_FIELDS)

    def blocks(*count):
        return (count + (8, 128), f32)

    state, labels, edges, to_even, to_odd = call(
        first_kernel,
        (populations, turbine_mask, rotor_index, bottom_in, top_in),
        (((11, 2, 64, 128), f32), ((2, 64, 128), jnp.int32), blocks(12), blocks(9), blocks(9)),
        (whole, cells, cells, inflow, inflow),
        in_hbm=5,
        copies=LEVELS + 4,
    )
    even, odd = swapped(to_even, to_odd, "gy")
    (own_sums,) = call(sums_kernel, (state, labels), (one,))
    domains, to_even, to_odd, column_sums, beside = call(
        relay_kernel,
        (state, labels, edges, own_sums, even, odd),
        (blocks(2, 12), blocks(n + 4), blocks(n + 4), one, blocks(2, 2)),
    )
    old_even, old_odd = swapped(to_even, to_odd, "gx")
    starts, found, found_beside = call(
        places_kernel,
        (labels, domains),
        (((2, 8, 128), jnp.int32), blocks(SPAN, 2, LEVELS), blocks(SPAN, LEVELS)),
    )
    shifted = (blocks(9, 6, 2, LEVELS), ((9, 2, LEVELS, 8, 128), jnp.int32))
    moved, moved_labels = call(first_prepare_kernel, (state, labels, domains), shifted)
    state, to_even, to_odd, strip, counts, sums = call(
        middle_kernel,
        (
            moved, moved_labels, domains, column_sums, beside, starts, found, found_beside,
            old_even, old_odd, bottom_in, top_in,
        ),
        (state_shape, blocks(n + 2), blocks(n + 2), blocks(8), one, one),
        (ghost, blocks(2, LEVELS)),
    )
    even, odd = swapped(to_even, to_odd, "gx")
    moved, moved_labels = call(last_prepare_kernel, (state, labels, strip), shifted)
    (out,) = call(
        last_kernel,
        (moved, moved_labels, sums, counts, even, odd, old_even, old_odd, bottom_in, top_in),
        (whole,),
        (whole, ghost),
        out_hbm=1,
        copies=LEVELS,
    )
    return out


def solution(mesh):
    placed = (
        P(None, None, "gx", "gy"),
        P(None, "gx", "gy"),
        P(None, "gx", "gy"),
        P(None, "gx", "gy"),
        P(None, "gx", "gy"),
    )
    return jax.shard_map(
        body, mesh=mesh, in_specs=placed, out_specs=P(None, None, "gx", "gy"), check_vma=False
    )
```

```python
import functools

import jax
import jax.numpy as jnp
from jax import lax
from jax.experimental import pallas as pl
from jax.experimental.pallas import tpu as pltpu
from jax.sharding import PartitionSpec as P

ROTORS = 64
SOUND = 1.0 / 3.0
TAU_BASE = 0.52
SMAG_GAIN = 5.0
CORIOLIS = 0.05
GEO_U = 0.08
THRUST_GAIN = 4.0
EMPTY = 127
LEVELS = 8
VMEM_LIMIT = 24 * 1024 * 1024

RHO, VX, VY, VZ, DXX, DYY, DZZ, DXY, DXZ, DYZ = range(10)
SPEED = 10
LABEL = 10
SPAN = 5
X_FIELDS = (RHO, VX, VY, VZ, DXX, DXY, DXZ)
Y_FIELDS = (RHO, VX, VY, VZ, DYY, DXY, DYZ)


def iota(axis):
    return lax.broadcasted_iota(jnp.int32, (8, 128), axis)


def roll(block, shift, axis):
    size = block.shape[axis]
    return pltpu.roll(block, shift % size, axis) if shift % size else block


def low_moments(f):
    along_z = {}
    for a in range(3):
        for b in range(3):
            low, mid, high = f(a, b, 0), f(a, b, 1), f(a, b, 2)
            ends = low + high
            along_z[a, b] = (ends + mid, high - low, ends)
    slabs = []
    for a in range(3):
        (l0, l1, l2), (m0, m1, m2), (h0, h1, h2) = (along_z[a, b] for b in range(3))
        ends = l0 + h0
        slabs.append((ends + m0, h0 - l0, ends, l1 + m1 + h1, h1 - l1, l2 + m2 + h2))
    low, mid, high = slabs
    ends = low[0] + high[0]
    return {
        "0": ends + mid[0],
        "x": high[0] - low[0],
        "xx": ends,
        "y": low[1] + mid[1] + high[1],
        "xy": high[1] - low[1],
        "yy": low[2] + mid[2] + high[2],
        "z": low[3] + mid[3] + high[3],
        "xz": high[3] - low[3],
        "yz": low[4] + mid[4] + high[4],
        "zz": low[5] + mid[5] + high[5],
    }


def relax(m):
    rho = m["0"]
    inverse = 1.0 / rho
    ux, uy, uz = m["x"] * inverse, m["y"] * inverse, m["z"] * inverse
    third = rho * SOUND
    qxx = m["xx"] - (m["x"] * ux + third)
    qyy = m["yy"] - (m["y"] * uy + third)
    qzz = m["zz"] - (m["z"] * uz + third)
    qxy = m["xy"] - m["x"] * uy
    qxz = m["xz"] - m["x"] * uz
    qyz = m["yz"] - m["y"] * uz
    strain = qxx * qxx + qyy * qyy + qzz * qzz + 2.0 * (qxy * qxy + qxz * qxz + qyz * qyz)
    keep = 1.0 - 1.0 / (TAU_BASE + SMAG_GAIN * jnp.sqrt(strain))
    vx = ux + CORIOLIS * uy
    vy = uy - CORIOLIS * (ux - GEO_U)
    fields = [rho, vx, vy, uz] + [keep * q for q in (qxx, qyy, qzz, qxy, qxz, qyz)]
    return ux, fields


def shapes(speed):
    square = speed * speed + SOUND
    return (0.5 * (square - speed), 1.0 - square, 0.5 * (square + speed))


def over_rows(block, join=jnp.add):
    for shift in (4, 2, 1):
        block = join(block, roll(block, shift, 0))
    return block


def spread(leaf, join=jnp.add, tree=(16, 8, (2, 8, (1, 2, ())))):
    lanes = iota(1)

    def node(stride, ways, rest, index):
        parts = [(node(*rest, index + d * stride) if rest else leaf(index + d * stride)) for d in range(ways)]
        digit = (lanes // stride) % ways
        moved = []
        for k in range(ways):
            picked = parts[k]
            for d in range(1, ways):
                picked = jnp.where(digit == d, parts[(d + k) % ways], picked)
            moved.append(roll(picked, k * stride, 1))
        return functools.reduce(join, moved)

    return over_rows(node(*tree, 0), join)


def rotor_sums(labels, speeds):
    def leaf(index):
        rotor, counting = index % ROTORS, index >= ROTORS
        total = jnp.zeros((8, 128), jnp.float32)
        for label, speed in zip(labels, speeds):
            total = total + jnp.where(label == rotor, 1.0 if counting else speed, 0.0)
        return total

    return spread(leaf)


def take(block, index):
    return jnp.take_along_axis(block, index, axis=1, mode="promise_in_bounds")


def sums_kernel(state, labels, own_sums):
    places = [(j, z) for j in range(2) for z in range(LEVELS)]
    own_sums[...] = rotor_sums(
        [labels[j, 8 * z : 8 * z + 8, :] for j, z in places],
        [state[SPEED, j, 8 * z : 8 * z + 8, :] for j, z in places],
    )


def beside_tile(domains, n):
    return jnp.where((iota(1) & 8) == 0, domains[0, n], domains[1, n])


def places_kernel(labels, domains, starts, found, found_beside):
    lanes = iota(1)
    far = 1024.0
    column = lanes & 15
    near = jnp.logical_and(column >= 3, column < 13)
    outside = jnp.where(near, index_of(beside_tile(domains, LABEL)), EMPTY)
    inside = {(j, z): labels[j, 8 * z : 8 * z + 8, :] for j in range(2) for z in range(LEVELS)}

    def leaf(index):
        rotor = index % ROTORS
        if index >= ROTORS:
            return jnp.where(outside == rotor, column.astype(jnp.float32), far)
        first = jnp.full((8, 128), far, jnp.float32)
        for j in range(2):
            hit = inside[j, 0] == rotor
            for z in range(1, LEVELS):
                hit = jnp.logical_or(hit, inside[j, z] == rotor)
            first = jnp.minimum(first, jnp.where(hit, (lanes + 128 * j).astype(jnp.float32), far))
        return first

    both = spread(leaf, jnp.minimum, (8, 16, (1, 8, ())))
    begin = (jnp.where(both < far, both, 0.0)).astype(jnp.int32)
    begin_beside = roll(begin.astype(jnp.float32), 64, 1).astype(jnp.int32)
    starts[0] = begin
    starts[1] = begin_beside
    own = jnp.where(lanes < ROTORS, lanes, -1)
    for k in range(SPAN):
        index = (begin + k) & 127
        for z in range(LEVELS):
            for j in range(2):
                found[k, j, z] = jnp.where(take(inside[j, z], index) == own, 1.0, 0.0)
            index_beside = (begin_beside + (k + 16 * z)) & 127
            found_beside[k, z] = jnp.where(take(outside, index_beside) == own, 1.0, 0.0)


def found_sums(speed, speed_beside, starts, found, found_beside):
    total = jnp.zeros((8, 128), jnp.float32)
    for k in range(SPAN):
        index = (starts[0] + k) & 127
        for z in range(LEVELS):
            for j in range(2):
                total = total + jnp.where(found[k, j, z] > 0.0, take(speed(z, j), index), 0.0)
            index_beside = (starts[1] + (k + 16 * z)) & 127
            total = total + jnp.where(found_beside[k, z] > 0.0, take(speed_beside, index_beside), 0.0)
    return over_rows(total)


def collide(f, state, keep_speed):
    for z in range(LEVELS):
        for j in range(2):
            ux, fields = relax(low_moments(functools.partial(f, z, j)))
            for index, value in enumerate(fields):
                state[index, j, 8 * z : 8 * z + 8, :] = value
            keep_speed(z, j, ux)


def first_kernel(
    f_hbm, mask_hbm, rotor_hbm, bottom_hbm, top_hbm, state, labels, edges, to_even, to_odd,
    f_ref, mask_ref, rotor_ref, bottom, top, arrived,
):
    lanes = iota(1)
    levels = [pltpu.make_async_copy(f_hbm.at[:, z], f_ref.at[:, z], arrived.at[z]) for z in range(LEVELS)]
    others = [
        pltpu.make_async_copy(source, target, arrived.at[LEVELS + n])
        for n, (source, target) in enumerate(
            ((mask_hbm, mask_ref), (rotor_hbm, rotor_ref), (bottom_hbm, bottom), (top_hbm, top))
        )
    ]
    for copy in others + levels:
        copy.start()
    for copy in others:
        copy.wait()
    send = Paired("gy", to_even, to_odd).put
    for place, source in ((7, bottom), (8, top)):
        upward = jnp.zeros((8, 128), jnp.float32)
        downward = upward
        for n in range(9):
            both = jnp.where(lanes < 64, source[n, :, 0:128], source[n, :, 128:256])
            moved = roll(both, 8 * n + 8, 1)
            upward = jnp.where(lanes // 8 == n, moved, upward)
            downward = jnp.where(lanes // 8 == n + 1, moved, downward)
        send(place, upward, downward)
    waiting = list(levels)

    def f(z, j, a, b, c):
        if len(waiting) == LEVELS - z:
            waiting.pop(0).wait()
        return f_ref[9 * a + 3 * b + c, z, :, 128 * j : 128 * j + 128]

    def keep_speed(z, j, ux):
        here = (z, slice(None), slice(128 * j, 128 * j + 128))
        state[SPEED, j, 8 * z : 8 * z + 8, :] = ux
        labels[j, 8 * z : 8 * z + 8, :] = jnp.where(mask_ref[here] != 0, rotor_ref[here], EMPTY)

    collide(f, state, keep_speed)

    def edge(read):
        block = jnp.zeros((8, 128), jnp.float32)
        inner = block
        for z in range(LEVELS):
            moved = roll(jnp.where(lanes < 64, read(z, 0), read(z, 1)), 16 * z + 8, 1)
            block = jnp.where(lanes // 16 == z, moved, block)
            wanted = jnp.logical_or(((lanes - 16 * z + 2) & 127) < 2, ((lanes - 16 * z - 16) & 127) < 2)
            inner = jnp.where(wanted, moved, inner)
        return block, inner

    pairs = [edge(lambda z, j, n=n: state[n, j, 8 * z : 8 * z + 8, :]) for n in range(10)]
    pairs.append(edge(lambda z, j: labels[j, 8 * z : 8 * z + 8, :].astype(jnp.float32)))
    pairs.append(edge(lambda z, j: state[SPEED, j, 8 * z : 8 * z + 8, :]))
    blocks = [block for block, _ in pairs]
    inner_label, inner_speed = pairs[LABEL][1], pairs[LABEL + 1][1]
    for n, block in enumerate(blocks):
        edges[n] = block
    low = (lanes & 8) == 0

    for n in range(6):
        one, other = blocks[2 * n], blocks[2 * n + 1]
        send(n, jnp.where(low, one, roll(other, 8, 1)), jnp.where(low, roll(other, -8, 1), one))
    column = lanes & 15
    send(
        6,
        jnp.where(column >= 14, inner_speed, jnp.where(column >= 12, roll(inner_label, -2, 1), float(EMPTY))),
        jnp.where(column < 2, inner_speed, jnp.where(column < 4, roll(inner_label, 2, 1), float(EMPTY))),
    )


class Paired:
    def __init__(self, axis, even, odd):
        self.next_first = lax.rem(lax.axis_index(axis), 2) == 0
        self.refs = (even, odd)

    def put(self, n, to_next, to_previous):
        even, odd = self.refs
        even[n] = jnp.where(self.next_first, to_next, to_previous)
        odd[n] = jnp.where(self.next_first, to_previous, to_next)

    def received(self):
        even, odd = self.refs
        return Chosen(self.next_first, odd, even), Chosen(self.next_first, even, odd)


class Chosen:
    def __init__(self, flag, one, other):
        self.flag, self.one, self.other = flag, one, other

    def __getitem__(self, n):
        return jnp.where(self.flag, self.one[n], self.other[n])


def rows_of(blocks, row):
    rows = iota(0)
    out = jnp.broadcast_to(blocks[0][row : row + 1], (8, 128))
    for n in range(1, len(blocks)):
        out = jnp.where(rows == n, jnp.broadcast_to(blocks[n][row : row + 1], (8, 128)), out)
    return out


def edge_rows(state, sent):
    slot = 0
    for index in X_FIELDS:
        for j in range(2):
            sent.put(slot, *(state[index, j, pl.ds(row, 8, stride=8), :] for row in (7, 0)))
            slot += 1
    return slot


def relay_kernel(state, labels, edges, own_sums, even, odd, domains, to_even, to_odd, column_sums, beside):
    below, above = ([chosen[n] for n in range(9)] for chosen in Paired("gy", even, odd).received())
    for side, message in enumerate((below, above)):
        for n in range(2):
            beside[side, n] = message[7 + n]
    low = (iota(1) & 8) == 0
    for n in range(12):
        under, over = below[n // 2], above[n // 2]
        if n % 2:
            under, over = roll(under, -8, 1), roll(over, 8, 1)
        domains[0, n] = jnp.where(low, under, edges[n])
        domains[1, n] = jnp.where(low, edges[n], over)
    column = iota(1) & 15
    inner = jnp.where(
        column >= 14, roll(below[6], 2, 1), jnp.where(column < 2, roll(above[6], -2, 1), float(EMPTY))
    )
    sums = own_sums[...] + rotor_sums(
        [index_of(beside_tile(domains, LABEL)), index_of(inner)],
        [beside_tile(domains, LABEL + 1), jnp.where(column >= 8, below[6], above[6])],
    )
    column_sums[...] = sums
    sent = Paired("gx", to_even, to_odd)
    slot = edge_rows(state, sent)
    for j in range(2):
        sent.put(slot + j, *(labels[j, pl.ds(row, 8, stride=8), :].astype(jnp.float32) for row in (7, 0)))
    ends = [
        jnp.where(column < 9, domains[0, n], roll(domains[1, n], 2, 1)) for n in X_FIELDS + (LABEL,)
    ]
    sent.put(slot + 2, rows_of(ends, 7), rows_of(ends, 0))
    sent.put(slot + 3, sums, sums)


look_up = take


def index_of(mark):
    return jnp.clip(mark, 0.0, float(EMPTY)).astype(jnp.int32)


def slot_value(d, parts, along_y, along_z, a, b, c):
    value = parts[a] * along_y[b] * along_z[c]
    ones = (a == 1) + (b == 1) + (c == 1)
    if ones == 3:
        return value - (d[DXX] + d[DYY] + d[DZZ])
    if ones == 2:
        return value + 0.5 * (d[DXX] if a != 1 else d[DYY] if b != 1 else d[DZZ])
    if ones == 1 and c == 1:
        return value + (0.25 * (a - 1) * (b - 1)) * d[DXY]
    if ones == 1 and b == 1:
        return value + (0.25 * (a - 1) * (c - 1)) * d[DXZ]
    if ones == 1:
        return value + (0.25 * (b - 1) * (c - 1)) * d[DYZ]
    return value


def entering(table, fields, mark, a):
    rho, vx, vy, vz, dxx, dxy, dxz = fields
    part = rho * shapes(vx - look_up(table, mark))[a]
    d = {DXX: dxx, DXY: dxy, DXZ: dxz}
    along_y, along_z = shapes(vy), shapes(vz)
    return {(b, c): slot_value(d, {a: part}, along_y, along_z, a, b, c) for b in range(3) for c in range(3)}


def shift_rows(value, a, before, after):
    if a == 2:
        return jnp.where(iota(0) == 0, before, roll(value, 1, 0))
    if a == 0:
        return jnp.where(iota(0) == 7, after, roll(value, -1, 0))
    return value


def row_blocks(block, count):
    return [jnp.broadcast_to(block[n : n + 1], (8, 128)) for n in range(count)]


def step_domain(table, side, domains, left, right, beside):
    lanes = iota(1)
    d = [domains[side, n] for n in range(10)]
    thrust = look_up(table, index_of(domains[side, LABEL]))
    parts = [d[RHO] * h for h in shapes(d[VX] - thrust)]
    along_y, along_z = shapes(d[VY]), shapes(d[VZ])
    n = 2 * len(X_FIELDS) + 2
    outer = {}
    for a, message in ((2, left), (0, right)):
        fields = row_blocks(roll(message[n], -2 * side, 1), 8)
        outer[a] = entering(table, fields[:7], index_of(fields[7]), a)
    new = {}
    for a in range(3):
        for b in range(3):
            for c in range(3):
                value = slot_value(d, parts, along_y, along_z, a, b, c)
                value = shift_rows(value, a, outer[2][b, c], outer[0][b, c])
                value = roll(value, b - 1, 1)
                slot = 3 * a + b
                if c == 2:
                    value = jnp.where(lanes < 16, roll(beside[side, 0], -8 * slot, 1), roll(value, 16, 1))
                elif c == 0:
                    value = jnp.where(lanes >= 112, roll(beside[side, 1], 112 - 8 * slot, 1), roll(value, -16, 1))
                new[a, b, c] = value
    return outer, new


def strip_corners(table, message, a):
    even = (iota(1) & 1) == 0
    rho, vx, vy, vz, _, dxy, _, mark = row_blocks(message[2 * len(X_FIELDS)], 8)
    along_y, along_z = shapes(vy), shapes(vz)
    part = rho * shapes(vx - look_up(table, index_of(mark)))[a] * jnp.where(even, along_y[2], along_y[0])
    slots = [part * along_z[c] for c in range(3)]
    slots[1] = slots[1] + ((a - 1) * jnp.where(even, 0.25, -0.25)) * dxy
    return slots


def merged_strip(left_end, right_end):
    return jnp.where((iota(1) & 1) == 0, roll(left_end, 1, 1), roll(right_end, -1, 1))


def shift_columns(first, second, b, inflow):
    lanes = iota(1)
    if b == 2:
        first, second = roll(first, 1, 1), roll(second, 1, 1)
        return jnp.where(lanes == 0, inflow, first), jnp.where(lanes == 0, first, second)
    if b == 0:
        first, second = roll(first, -1, 1), roll(second, -1, 1)
        return jnp.where(lanes == 127, second, first), jnp.where(lanes == 127, inflow, second)
    return first, second


def prepare(state, labels, strip, moved, moved_labels):
    even = (iota(1) & 1) == 0
    rho, vx, vy, vz, dyy, dxy, dyz, mark = strip
    sign = jnp.where(even, 0.25, -0.25)
    along_y, along_z = shapes(vy), shapes(vz)
    part = rho * jnp.where(even, along_y[2], along_y[0])
    outside = [vx] + [part * h for h in along_z] + [0.5 * dyy, sign * dyz, sign * dxy, mark]
    for z in range(LEVELS):
        inflow = [roll(block, -16 * z - 8, 1) for block in outside]
        tiles = []
        for j in range(2):
            d = [state[n, j, 8 * z : 8 * z + 8, :] for n in range(10)]
            mark = labels[j, 8 * z : 8 * z + 8, :].astype(jnp.float32)
            along_y, along_z = shapes(d[VY]), shapes(d[VZ])
            rows = [d[RHO] * h for h in along_y]
            tiles.append((d, mark, rows, along_z))
        for b in range(3):
            kept = []
            for d, mark, rows, along_z in tiles:
                if b == 1:
                    terms = [-(d[DXX] + d[DYY] + d[DZZ]), 0.5 * d[DZZ], 0.5 * d[DXX], mark, 0.25 * d[DXZ]]
                else:
                    terms = [0.5 * d[DYY], (0.25 * (b - 1)) * d[DYZ], (0.25 * (b - 1)) * d[DXY], mark]
                kept.append([d[VX]] + [rows[b] * h for h in along_z] + terms)
            if b != 1:
                pairs = [shift_columns(*pair) for pair in zip(*kept, [b] * 8, inflow)]
                kept = list(zip(*pairs))
            for j, fields in enumerate(kept):
                for a in range(3):
                    place = 3 * a + b
                    chosen = list(fields[:4])
                    if a == 1:
                        chosen += [fields[4], fields[5], fields[7]]
                    elif b == 1:
                        chosen += [fields[6], (a - 1) * fields[8], fields[7]]
                    else:
                        chosen += [(a - 1) * fields[6], None, fields[7]]
                    for n, value in enumerate(chosen):
                        if value is None:
                            continue
                        value = roll(value, a - 1, 0)
                        if n == 6:
                            moved_labels[place, j, z] = value.astype(jnp.int32)
                        else:
                            moved[place, n, j, z] = value


def first_prepare_kernel(state, labels, domains, moved, moved_labels):
    strip = [merged_strip(domains[0, n], domains[1, n]) for n in Y_FIELDS + (LABEL,)]
    prepare(state, labels, strip, moved, moved_labels)


def last_prepare_kernel(state, labels, strip, moved, moved_labels):
    prepare(state, labels, [strip[n] for n in range(8)], moved, moved_labels)


def streamed(table, moved, moved_labels, left, right, left_marks, right_marks, corners, bottom, top, ghost):
    rows = iota(0)
    for side, (source, marks) in enumerate(((left, left_marks), (right, right_marks))):
        a = 2 - 2 * side
        halves = [
            entering(table, [source[2 * n + j] for n in range(len(X_FIELDS))], marks(j), a) for j in range(2)
        ]
        for b in range(3):
            for c in range(3):
                inflow = None if b == 1 else take(corners[side][b, c], 16 * rows + (8 if b == 2 else 7))
                pair = shift_columns(halves[0][b, c], halves[1][b, c], b, inflow)
                for j in range(2):
                    ghost[side, 3 * b + c, j] = pair[j]

    @functools.cache
    def along_x(place, j, z):
        return shapes(moved[place, 0, j, z] - look_up(table, moved_labels[place, j, z]))[place // 3]

    def slot(level, j, a, b, c):
        z, place = level + 1 - c, 3 * a + b
        if z < 0 or z >= LEVELS:
            return (bottom if z < 0 else top)[place, :, 128 * j : 128 * j + 128]
        value = moved[place, 1 + c, j, z] * along_x(place, j, z)
        if c == 1:
            value = value + moved[place, 4, j, z]
        elif a == 1 and b == 1:
            value = value + moved[place, 5, j, z]
        elif a == 1 or b == 1:
            value = value + (c - 1) * moved[place, 5, j, z]
        if a == 2:
            return jnp.where(rows == 0, ghost[0, 3 * b + c, j, z : z + 1, :], value)
        if a == 0:
            return jnp.where(rows == 7, ghost[1, 3 * b + c, j, z : z + 1, :], value)
        return value

    return slot


def disk_table(sums, counts):
    disk = sums / jnp.maximum(counts, 1.0)
    return jnp.where(iota(1) < ROTORS, THRUST_GAIN * disk * jnp.abs(disk), 0.0)


def marks_of(message):
    return lambda j: message[2 * len(X_FIELDS) + j].astype(jnp.int32)


def middle_kernel(
    moved, moved_labels, domains, column_sums, beside, starts, found, found_beside, even, odd, bottom, top,
    new_state, to_even, to_odd, strip, counts, sums_out, ghost, speeds,
):
    lanes = iota(1)
    left, right = Paired("gx", even, odd).received()
    last = 2 * len(X_FIELDS) + 3
    totals = column_sums[...] + left[last] + right[last]
    seen = roll(totals, 64, 1)
    counts[...] = seen
    table = disk_table(totals, seen)

    outside, kept, corners = [], [], [{}, {}]
    for side in range(2):
        outer, new = step_domain(table, side, domains, left, right, beside)
        ux, fields = relax(low_moments(lambda a, b, c: new[a, b, c]))
        outside.append(ux)
        kept.append([fields[n] for n in Y_FIELDS] + [domains[side, LABEL]])
        b = 2 - 2 * side
        for c in range(3):
            for row, a in ((0, 2), (1, 0)):
                corners[row][b, c] = roll(outer[a][b, c], b - 1, 1)
    strips = [merged_strip(one, other) for one, other in zip(*kept)]
    for n, block in enumerate(strips):
        strip[n] = block
    f = streamed(
        table, moved, moved_labels, left, right, marks_of(left), marks_of(right), corners, bottom, top, ghost
    )

    def keep_speed(z, j, ux):
        speeds[j, z] = ux

    collide(f, new_state, keep_speed)
    sums = found_sums(
        lambda z, j: speeds[j, z],
        jnp.where((lanes & 8) == 0, outside[0], outside[1]),
        starts, found, found_beside,
    )
    sums_out[...] = sums
    sent = Paired("gx", to_even, to_odd)
    slot = edge_rows(new_state, sent)
    sent.put(slot, rows_of(strips, 7), rows_of(strips, 0))
    sent.put(slot + 1, sums, sums)


def last_kernel(
    moved, moved_labels, sums, counts, even, odd, old_even, old_odd, bottom, top, out_hbm, out, ghost, gone
):
    left, right = Paired("gx", even, odd).received()
    old_left, old_right = Paired("gx", old_even, old_odd).received()
    last = 2 * len(X_FIELDS) + 1
    totals = sums[...] + left[last] + right[last]
    table = disk_table(totals, counts[...])
    corners = [
        {(b, c): value for c, value in enumerate(strip_corners(table, message, a)) for b in (0, 2)}
        for message, a in ((left, 2), (right, 0))
    ]
    copies = [pltpu.make_async_copy(out.at[:, z], out_hbm.at[:, z], gone.at[z]) for z in range(LEVELS)]
    f = streamed(
        table, moved, moved_labels, left, right, marks_of(old_left), marks_of(old_right), corners, bottom, top, ghost
    )
    for z in range(LEVELS):
        for j in range(2):
            for slot in range(27):
                out[slot, z, :, 128 * j : 128 * j + 128] = f(z, j, slot // 9, slot // 3 % 3, slot % 3)
        copies[z].start()
    for copy in copies:
        copy.wait()


def call(kernel, inputs, outputs, scratch=(), in_hbm=0, out_hbm=0, copies=0):
    inputs = [pltpu.with_memory_space_constraint(x, pltpu.HBM) if n < in_hbm else x for n, x in enumerate(inputs)]

    def specs(count, outside):
        return [pl.BlockSpec(memory_space=pltpu.HBM if n < outside else pltpu.VMEM) for n in range(count)]

    return pl.pallas_call(
        kernel,
        out_shape=[jax.ShapeDtypeStruct(shape, dtype) for shape, dtype in outputs],
        in_specs=specs(len(inputs), in_hbm),
        out_specs=specs(len(outputs), out_hbm),
        scratch_shapes=[pltpu.VMEM(shape, dtype) for shape, dtype in scratch]
        + ([pltpu.SemaphoreType.DMA((copies,))] if copies else []),
        compiler_params=pltpu.CompilerParams(vmem_limit_bytes=VMEM_LIMIT),
    )(*inputs)


def swapped(even, odd, axis):
    count = lax.axis_size(axis)

    def pairs(start):
        there = [(i, (i + 1) % count) for i in range(start, count, 2)]
        return there + [(j, i) for i, j in there]

    return lax.ppermute(even, axis, pairs(0)), lax.ppermute(odd, axis, pairs(1))


def body(populations, bottom_in, top_in, turbine_mask, rotor_index):
    f32 = jnp.float32
    state_shape = ((10, 2, 64, 128), f32)
    one = ((8, 128), f32)
    ghost = ((2, 9, 2, 8, 128), f32)
    inflow = (bottom_in.shape, f32)
    cells = (turbine_mask.shape, jnp.int32)
    whole = (populations.shape, f32)
    n = 2 * len(X_FIELDS)

    def blocks(*count):
        return (count + (8, 128), f32)

    state, labels, edges, to_even, to_odd = call(
        first_kernel,
        (populations, turbine_mask, rotor_index, bottom_in, top_in),
        (((11, 2, 64, 128), f32), ((2, 64, 128), jnp.int32), blocks(12), blocks(9), blocks(9)),
        (whole, cells, cells, inflow, inflow),
        in_hbm=5,
        copies=LEVELS + 4,
    )
    even, odd = swapped(to_even, to_odd, "gy")
    (own_sums,) = call(sums_kernel, (state, labels), (one,))
    domains, to_even, to_odd, column_sums, beside = call(
        relay_kernel,
        (state, labels, edges, own_sums, even, odd),
        (blocks(2, 12), blocks(n + 4), blocks(n + 4), one, blocks(2, 2)),
    )
    old_even, old_odd = swapped(to_even, to_odd, "gx")
    starts, found, found_beside = call(
        places_kernel,
        (labels, domains),
        (((2, 8, 128), jnp.int32), blocks(SPAN, 2, LEVELS), blocks(SPAN, LEVELS)),
    )
    shifted = (blocks(9, 6, 2, LEVELS), ((9, 2, LEVELS, 8, 128), jnp.int32))
    moved, moved_labels = call(first_prepare_kernel, (state, labels, domains), shifted)
    state, to_even, to_odd, strip, counts, sums = call(
        middle_kernel,
        (
            moved, moved_labels, domains, column_sums, beside, starts, found, found_beside,
            old_even, old_odd, bottom_in, top_in,
        ),
        (state_shape, blocks(n + 2), blocks(n + 2), blocks(8), one, one),
        (ghost, blocks(2, LEVELS)),
    )
    even, odd = swapped(to_even, to_odd, "gx")
    moved, moved_labels = call(last_prepare_kernel, (state, labels, strip), shifted)
    (out,) = call(
        last_kernel,
        (moved, moved_labels, sums, counts, even, odd, old_even, old_odd, bottom_in, top_in),
        (whole,),
        (whole, ghost),
        out_hbm=1,
        copies=LEVELS,
    )
    return out


def solution(mesh):
    placed = (
        P(None, None, "gx", "gy"),
        P(None, "gx", "gy"),
        P(None, "gx", "gy"),
        P(None, "gx", "gy"),
        P(None, "gx", "gy"),
    )
    return jax.shard_map(
        body, mesh=mesh, in_specs=placed, out_specs=P(None, None, "gx", "gy"), check_vma=False
    )
```
